512 devices in a mesh: stream: 32 (over z, x_hi), span: 16 (over y, x_lo, core).
Axes of the slice: x: 4 (x_hi: 2, x_lo: 2; x = x_hi * 2 + x_lo), y: 4, z: 16, core: 2. Of those that a mesh axis runs over, the one named last changes fastest.
Arguments:
- checkpoint: float32 [19, 128, 128, 128], P(None, 'stream', 'span'), may hold values from 0.5 to 1.5
- porosity: float32 [128, 128, 128], P('stream', 'span'), may hold values from 0 to 1
- deposit_weight: float32 [128, 128, 128], P('stream', 'span'), may hold values from -24 to 24
- solid_mask: int32 [128, 128, 128], P('stream', 'span'), may hold values 0 or 1
- surface_mask: int32 [128, 128, 128], P('stream', 'span'), may hold values 0 or 1
Outputs:
- adjoint_state: float32 [19, 128, 128, 128], P(None, 'stream', 'span')
- shape_sensitivity: float32 [128, 128, 128], P('stream', 'span')
The draws below stay inside these ranges and needn't reach their ends.
All inputs are finite; a program needn't handle non-finite values. No bound on the sum of `solid_mask` or of `surface_mask` on one device may be relied on, other than what follows from the above.
Results may differ from the reference program's by a relative error of at most 0.0003.
Values sent between devices are 32-bit elements; how exact they have to be, the bound alone decides.
No kernel may reach another device: no remote copies, remote signals or barrier semaphores. Data moves between devices by JAX's collectives and lax.ppermute only.
A program may use at most 64 MiB of HBM per device.

```python
import math
import jax
import jax.numpy as jnp
import numpy as np
from jax import lax

NZ = 128
ITERS = 2
NX = 128
NY = 128


def touch_ends(result, stream_key, low, high):
    index_at = [jax.random.randint(jax.random.fold_in(stream_key, axis), (), 0, length) for axis, length in enumerate(result.shape)]
    widest = result.shape.index(max(result.shape))
    beside = index_at[:widest] + [(index_at[widest] + 1) % result.shape[widest]] + index_at[widest + 1:]
    return result.at[tuple(index_at)].set(low).at[tuple(beside)].set(high)


def block_levels(key, dims, cuts, low, largest):
    loudness = 1.0
    for axis_at, shards_of in cuts:
        draws = jax.random.uniform(jax.random.fold_in(jax.random.fold_in(key, 6), axis_at), (shards_of,), jnp.float32, low / len(cuts), largest / len(cuts))
        loudness = loudness * jnp.repeat(jnp.exp(draws), dims[axis_at] // shards_of).reshape((-1,) + (1,) * (len(dims) - 1 - axis_at))
    return loudness


def bell_draw(own_key, shape, scale, most, cuts=(), held_as=jnp.bfloat16):
    loudness = block_levels(own_key, shape, cuts, -0.22, 0.18) if cuts else 1.0
    drawn = jax.random.normal(own_key, shape, jnp.float32) * scale * loudness
    return jnp.minimum(jnp.maximum(drawn, -most), most).astype(held_as)


def setup_inputs(seed: int = 0) -> dict:
    seeds = jax.random.split(jax.random.key(seed), 6)
    return {
        "checkpoint": jnp.clip(jnp.exp(math.log(1.5) - 1.0986123 * jax.random.uniform(seeds[0], (19, NX, NY, NZ), jnp.float32) ** block_levels(seeds[0], (19, NX, NY, NZ), ((1, 32), (2, 16)), -0.2, 0.2)), 0.5, 1.5),
        "porosity": jnp.clip(1.0 * jax.random.uniform(seeds[1], (NX, NY, NZ), jnp.float32) ** block_levels(seeds[1], (NX, NY, NZ), ((0, 32), (1, 16)), -0.2, 0.2), 0.0, 1.0),
        "deposit_weight": bell_draw(seeds[2], (NX, NY, NZ), 4.0, 24.0, ((0, 32), (1, 16)), jnp.float32),
        "solid_mask": touch_ends((jax.random.randint(seeds[3], (NX, NY, NZ), 0, 8) < 1).astype(jnp.int32), jax.random.fold_in(seeds[3], 1), 0, 1),
        "surface_mask": touch_ends((jax.random.randint(seeds[4], (NX, NY, NZ), 0, 4) < 1).astype(jnp.int32), jax.random.fold_in(seeds[4], 1), 0, 1),
    }


VELOCITY = np.array([[0, 0, 0], [1, 0, 0], [-1, 0, 0], [0, 1, 0], [0, -1, 0], [0, 0, 1], [0, 0, -1], [1, 1, 0], [-1, -1, 0], [1, -1, 0], [-1, 1, 0], [1, 0, 1], [-1, 0, -1], [1, 0, -1], [-1, 0, 1], [0, 1, 1], [0, -1, -1], [0, 1, -1], [0, -1, 1]])
WEIGHTS = np.array([1.0 / 3.0] + [1.0 / 18.0] * 6 + [1.0 / 36.0] * 12)
RELAX_RATE = 0.9
GHOST_DENSITY = 18.0
INFLOW_SPEED = 0.08
GHOST_STATE = WEIGHTS * GHOST_DENSITY * (1.0 + 3.0 * VELOCITY[:, 0] * INFLOW_SPEED + 4.5 * (VELOCITY[:, 0] * INFLOW_SPEED) ** 2 - 1.5 * INFLOW_SPEED ** 2)

def moments(field):
    velocity = jnp.asarray(VELOCITY, field.dtype)
    density = lax.optimization_barrier(jnp.sum(field, axis=0))
    momentum = jnp.tensordot(velocity.T, field, axes=1, precision=lax.Precision.HIGHEST)
    return (density, momentum)

def collide(field, blend):
    velocity = jnp.asarray(VELOCITY, field.dtype)
    density, momentum = moments(field)
    speed = momentum / density
    along = jnp.tensordot(velocity, speed, axes=1, precision=lax.Precision.HIGHEST)
    square = lax.optimization_barrier(jnp.sum(speed * speed, axis=0))
    weights = jnp.asarray(WEIGHTS, field.dtype).reshape(19, 1, 1, 1)
    equil = weights * density * (1.0 + 3.0 * along + 4.5 * along * along - 1.5 * square)
    relaxed = field - RELAX_RATE * (field - equil)
    tail = field[1:].reshape((9, 2) + field.shape[1:])[:, ::-1].reshape((18,) + field.shape[1:])
    bounced = jnp.concatenate([field[:1], tail], axis=0)
    return relaxed + blend * (bounced - relaxed)

def pull(extended, sign, outside):
    count, width, height, depth = extended.shape
    zplane = jnp.broadcast_to(outside.reshape(count, 1, 1, 1), (count, width, height, 1))
    padded = jnp.concatenate([zplane, extended, zplane], axis=3)
    sizex, sizey, sizez = (width - 2, height - 2, depth)
    pieces = []
    for popul in range(19):
        offx = 1 - sign * int(VELOCITY[popul, 0])
        offy = 1 - sign * int(VELOCITY[popul, 1])
        offz = 1 - sign * int(VELOCITY[popul, 2])
        pieces.append(padded[popul, offx:offx + sizex, offy:offy + sizey, offz:offz + sizez])
    return jnp.stack(pieces, axis=0)

def pad_grid(field, outside):
    count, width, height, depth = field.shape
    xplane = jnp.broadcast_to(outside.reshape(count, 1, 1, 1), (count, 1, height, depth))
    padded = jnp.concatenate([xplane, field, xplane], axis=1)
    return jnp.concatenate([padded[:, :, -1:], padded, padded[:, :, :1]], axis=2)

def one_step(field, blend):
    outside = jnp.asarray(GHOST_STATE, field.dtype)
    return pull(pad_grid(collide(field, blend), outside), 1, outside)

def measure_of(field, deposit_weight):
    density, momentum = moments(field)
    return jnp.sum(deposit_weight * lax.optimization_barrier(jnp.sum(momentum * momentum, axis=0)) / (2.0 * density))

def reference(checkpoint, porosity, deposit_weight, solid_mask, surface_mask):
    stepper = jax.checkpoint(one_step)

    def total(start, share):
        blend = jnp.where(solid_mask == 1, jnp.ones_like(share), jnp.where(surface_mask == 1, share, jnp.zeros_like(share)))
        field = start
        for repeat in range(ITERS):
            field = stepper(field, blend)
        return measure_of(field, deposit_weight)
    value, backward = jax.vjp(total, checkpoint, porosity)
    adjoint_state, shape_sensitivity = backward(jnp.ones_like(value))
    return (adjoint_state, shape_sensitivity)
```

```python
import functools

import jax
import jax.numpy as jnp
import numpy as np
from jax import lax
from jax.experimental import pallas as pl
from jax.experimental.pallas import tpu as pltpu
from jax.sharding import PartitionSpec as P

VELOCITY = np.array(
    [
        [0, 0, 0],
        [1, 0, 0],
        [-1, 0, 0],
        [0, 1, 0],
        [0, -1, 0],
        [0, 0, 1],
        [0, 0, -1],
        [1, 1, 0],
        [-1, -1, 0],
        [1, -1, 0],
        [-1, 1, 0],
        [1, 0, 1],
        [-1, 0, -1],
        [1, 0, -1],
        [-1, 0, 1],
        [0, 1, 1],
        [0, -1, -1],
        [0, 1, -1],
        [0, -1, 1],
    ]
)
WEIGHTS = np.array([1.0 / 3.0] + [1.0 / 18.0] * 6 + [1.0 / 36.0] * 12)
GHOST_DENSITY = 18.0
INFLOW_SPEED = 0.08
GHOST_STATE = (
    WEIGHTS
    * GHOST_DENSITY
    * (
        1.0
        + 3.0 * VELOCITY[:, 0] * INFLOW_SPEED
        + 4.5 * (VELOCITY[:, 0] * INFLOW_SPEED) ** 2
        - 1.5 * INFLOW_SPEED**2
    )
)
GHOST = [float(value) for value in GHOST_STATE]
VEL = [tuple(int(part) for part in row) for row in VELOCITY]
CX = [row[0] for row in VEL]
UP = [p for p in range(19) if CX[p] == 1]
DOWN = [p for p in range(19) if CX[p] == -1]
FLAT = [p for p in range(19) if CX[p] == 0]
BLEND, WEIGHT = 19, 20
NEAR, NEAR_FLAT, NEAR_BLEND, NEAR_WEIGHT = 0, 5, 14, 15
FAR, FAR_NEXT, FAR_PART, FAR_WEIGHT, LAYERS = 16, 21, 26, 30, 31


def sublane(tile):
    return lax.broadcasted_iota(jnp.int32, tile.shape, len(tile.shape) - 2)


def lane(tile):
    return lax.broadcasted_iota(jnp.int32, tile.shape, len(tile.shape) - 1)


def shift_z(tile, step, fill):
    if step == 0:
        return tile
    rolled = pltpu.roll(tile, step % 128, 1)
    return jnp.where(lane(tile) == (0 if step == 1 else 127), fill, rolled)


def shift_y(pair, step):
    if step == 0:
        return pair
    own, side = (pltpu.roll(tile, step % 8, 0) for tile in pair)
    edge = sublane(own) == (0 if step == 1 else 7)
    return (jnp.where(edge, side, own), jnp.where(edge, own, side))


def shift_pair(pair, stepy, stepz, fill):
    return tuple(shift_z(tile, stepz, fill) for tile in shift_y(pair, stepy))


def pairs_of(f):
    sums = [f[2 * i + 1] + f[2 * i + 2] for i in range(9)]
    diffs = [f[2 * i + 1] - f[2 * i + 2] for i in range(9)]
    return sums, diffs


def along_axes(v):
    return (
        v[0] + v[3] + v[4] + v[5] + v[6],
        v[1] + v[3] - v[4] + v[7] + v[8],
        v[2] + v[5] - v[6] + v[7] - v[8],
    )


def dots(u):
    x, y, z = u
    return [x, y, z, x + y, x - y, x + z, x - z, y + z, y - z]


def flow(f0, sums, diffs):
    density = f0 + sum(sums[1:], sums[0])
    inverse = 1.0 / density
    u = [m * inverse for m in along_axes(diffs)]
    square = u[0] * u[0] + u[1] * u[1] + u[2] * u[2]
    return density, u, square


def collide(f, b):
    sums, diffs = pairs_of(f)
    density, u, square = flow(f[0], sums, diffs)
    keep = 1.0 - b
    j = 0.1 * keep
    alpha, beta = 0.5 * (j + b), 0.5 * (j - b)
    scaled = (0.9 * keep) * density
    rest = scaled * (1.0 - 1.5 * square)
    flux = dots([scaled * part for part in u])
    out = [(j + b) * f[0] + (1.0 / 3.0) * rest]
    rest_axis, rest_diag = rest * (1.0 / 18.0), rest * (1.0 / 36.0)
    for i, along in enumerate(dots(u)):
        w = 1.0 / 18.0 if i < 3 else 1.0 / 36.0
        even = alpha * sums[i] + (rest_axis if i < 3 else rest_diag) + flux[i] * along * (4.5 * w)
        odd = beta * diffs[i] + flux[i] * (3.0 * w)
        out += [even + odd, even - odd]
    return out


def adjoint_collide(f, b, h, wanted, blend_part):
    fsums, fdiffs = pairs_of(f)
    density, u, square = flow(f[0], fsums, fdiffs)
    s, d = pairs_of(h)
    axis = (s[0] + s[1] + s[2]) * (1.0 / 18.0)
    h0 = h[0] * (1.0 / 3.0) + axis + sum(s[4:], s[3]) * (1.0 / 36.0)
    w = [1.0 / 18.0] * 3 + [1.0 / 36.0] * 6
    h1 = along_axes([d[i] * w[i] for i in range(9)])
    t = [s[i] * w[i] for i in range(9)]
    xx = t[0] + t[3] + t[4] + t[5] + t[6]
    yy = t[1] + t[3] + t[4] + t[7] + t[8]
    zz = t[2] + t[5] + t[6] + t[7] + t[8]
    xy, xz, yz = t[3] - t[4], t[5] - t[6], t[7] - t[8]
    v = (
        xx * u[0] + xy * u[1] + xz * u[2],
        xy * u[0] + yy * u[1] + yz * u[2],
        xz * u[0] + yz * u[1] + zz * u[2],
    )
    quad = u[0] * v[0] + u[1] * v[1] + u[2] * v[2]
    keep = 1.0 - b
    j, k = 0.1 * keep, 0.9 * keep
    alpha, beta = 0.5 * (j + b), 0.5 * (j - b)
    base = k * (h0 * (1.0 + 1.5 * square) - 4.5 * quad)
    push = dots([k * (3.0 * h1[i] + 9.0 * v[i] - 3.0 * u[i] * h0) for i in range(3)])
    out = {}
    if 0 in wanted:
        out[0] = (j + b) * h[0] + base
    for i in range(9):
        first, second = 2 * i + 1, 2 * i + 2
        if first in wanted or second in wanted:
            even = alpha * s[i] + base
            odd = beta * d[i] + push[i]
            if first in wanted:
                out[first] = even + odd
            if second in wanted:
                out[second] = even - odd
    part = None
    if blend_part:
        equil = h0 * (1.0 - 1.5 * square) + 4.5 * quad
        equil = equil + 3.0 * (u[0] * h1[0] + u[1] * h1[1] + u[2] * h1[2])
        evens = sum((s[i] * fsums[i] for i in range(1, 9)), s[0] * fsums[0])
        odds = sum((d[i] * fdiffs[i] for i in range(1, 9)), d[0] * fdiffs[0])
        part = 0.9 * h[0] * f[0] + 0.45 * evens - 0.55 * odds - 0.9 * density * equil
    return out, part


def moment_sums(values):
    density = functools.reduce(lambda a, b: a + b, values.values())
    momentum = []
    for k in range(3):
        total = None
        for p, value in values.items():
            if VEL[p][k] == 1:
                total = value if total is None else total + value
        for p, value in values.items():
            if VEL[p][k] == -1:
                total = -value if total is None else total - value
        momentum.append(total)
    return [density] + momentum


def start_kernel(f_ref, porosity_ref, weight_ref, solid_ref, surface_ref, own_ref, half_ref):
    core = lax.rem(lax.axis_index("span"), 2)
    for x in range(4):
        porosity = porosity_ref[x]
        blend = jnp.where(
            solid_ref[x] == 1, 1.0, jnp.where(surface_ref[x] == 1, porosity, 0.0)
        )
        out = collide([f_ref[p, x] for p in range(19)], blend)
        for p in range(19):
            own_ref[p, x] = out[p]
        own_ref[BLEND, x] = blend
        own_ref[WEIGHT, x] = weight_ref[x]
    for layer in range(21):
        for pair in range(2):
            first, second = own_ref[layer, 2 * pair], own_ref[layer, 2 * pair + 1]
            low = (sublane(first) < 4) == (core == 0)
            half_ref[layer, pair] = jnp.where(low, first, pltpu.roll(second, 4, 0))


def inner_kernel(own_ref, both_ref, half_ref, side_ref, state_ref, next_ref, up_ref, down_ref):
    core = lax.rem(lax.axis_index("span"), 2)
    for layer in range(21):
        for pair in range(2):
            came = half_ref[layer, pair]
            low = (sublane(came) < 4) == (core == 0)
            for x, tile in ((2 * pair, came), (2 * pair + 1, pltpu.roll(came, 4, 0))):
                side_ref[layer, x] = jnp.where(low, both_ref[1 - core, layer, x], tile)

    for x in (1, 2):
        f = []
        for p in range(19):
            cx, cy, cz = VEL[p]
            f.append(shift_pair((own_ref[p, x - cx], side_ref[p, x - cx]), cy, cz, GHOST[p]))
        for t in range(2):
            blend = (own_ref, side_ref)[t][BLEND, x]
            tiles = [f[p][t] for p in range(19)]
            out = collide(tiles, blend)
            for p in range(19):
                state_ref[p, x - 1, t] = tiles[p]
                next_ref[p, x - 1, t] = out[p]

    for ref, near, far, inward in ((up_ref, 3, 2, UP), (down_ref, 0, 1, DOWN)):
        for t, block in ((0, own_ref), (1, side_ref)):
            for i, p in enumerate(inward):
                ref[NEAR + i, t] = block[p, near]
                ref[FAR + i, t] = block[p, far]
                ref[FAR_NEXT + i, t] = next_ref[p, far - 1, t]
            for i, p in enumerate(FLAT):
                ref[NEAR_FLAT + i, t] = block[p, near]
            ref[NEAR_BLEND, t] = block[BLEND, near]
            ref[NEAR_WEIGHT, t] = block[WEIGHT, near]
            ref[FAR_WEIGHT, t] = block[WEIGHT, far]
        came = {}
        for p in inward + FLAT:
            cx, cy, cz = VEL[p]
            at = far - cx - 1
            came[p] = shift_pair((next_ref[p, at, 0], next_ref[p, at, 1]), cy, cz, GHOST[p])
        for t in range(2):
            for i, part in enumerate(moment_sums({p: came[p][t] for p in came})):
                ref[FAR_PART + i, t] = part


def last_kernel(
    f_ref, solid_ref, surface_ref, own_ref, side_ref, state_ref, next_ref, up_ref, down_ref,
    low_ref, high_ref, adjoint_ref, sensitivity_ref, c1_ref, s1_ref, a1_ref, field_ref,
):
    place = lax.axis_index("stream")
    first = place == 0
    last = place == lax.axis_size("stream") - 1

    def outside(x):
        return first if x < 0 else last if x > 3 else None

    def masked(x, value, fill):
        flag = outside(x)
        return value if flag is None else jnp.where(flag, fill, value)

    def message(x):
        return (low_ref, UP) if x < 0 else (high_ref, DOWN)

    def c0(p, x):
        if 0 <= x <= 3:
            return (own_ref[p, x], side_ref[p, x])
        ref, inward = message(x)
        if x in (-1, 4):
            at = NEAR + inward.index(p) if p in inward else NEAR_FLAT + FLAT.index(p)
        else:
            at = FAR + inward.index(p)
        return tuple(masked(x, ref[at, t], GHOST[p]) for t in range(2))

    def layer_of(x, which, near_at, far_at=None):
        if 0 <= x <= 3:
            return (own_ref[which, x], side_ref[which, x])
        ref, _ = message(x)
        at = near_at if x in (-1, 4) else far_at
        return (ref[at, 0], ref[at, 1])

    for x in (1, 2):
        for p in range(19):
            for t in range(2):
                s1_ref[p, x + 1, t] = state_ref[p, x - 1, t]
                c1_ref[p, x + 2, t] = next_ref[p, x - 1, t]
    for x in (-2, 5):
        ref, inward = message(x)
        for i, p in enumerate(inward):
            for t in range(2):
                c1_ref[p, x + 2, t] = masked(x, ref[FAR_NEXT + i, t], GHOST[p])
    for x in (-1, 0, 3, 4):
        f = []
        for p in range(19):
            cx, cy, cz = VEL[p]
            f.append(shift_pair(c0(p, x - cx), cy, cz, GHOST[p]))
        blend = layer_of(x, BLEND, NEAR_BLEND)
        for t in range(2):
            tiles = [f[p][t] for p in range(19)]
            out = collide(tiles, blend[t])
            for p in range(19):
                s1_ref[p, x + 1, t] = tiles[p]
                c1_ref[p, x + 2, t] = masked(x, out[p], GHOST[p])

    for x in range(-2, 6):
        parts, pops = None, list(range(19))
        if x in (-2, 2):
            parts = low_ref if x == -2 else up_ref
            pops = DOWN
        if x in (1, 5):
            parts = high_ref if x == 5 else down_ref
            pops = UP
        came = {}
        for p in pops:
            cx, cy, cz = VEL[p]
            at = x - cx + 2
            came[p] = shift_pair((c1_ref[p, at, 0], c1_ref[p, at, 1]), cy, cz, GHOST[p])
        weight = layer_of(x, WEIGHT, NEAR_WEIGHT, FAR_WEIGHT)
        for t in range(2):
            total = moment_sums({p: came[p][t] for p in came})
            if parts is not None:
                total = [total[i] + parts[FAR_PART + i, t] for i in range(4)]
            inverse = 1.0 / total[0]
            u = [total[i] * inverse for i in range(1, 4)]
            kinetic = 0.5 * (u[0] * u[0] + u[1] * u[1] + u[2] * u[2])
            for i, value in enumerate(u + [kinetic]):
                field_ref[i, x + 2, t] = masked(x, weight[t] * value, 0.0)

    def cotangent(p, x):
        cx, cy, cz = VEL[p]
        pair = []
        for t in range(2):
            value = -field_ref[3, x + cx + 2, t]
            for k in range(3):
                if VEL[p][k] == 1:
                    value = value + field_ref[k, x + cx + 2, t]
                if VEL[p][k] == -1:
                    value = value - field_ref[k, x + cx + 2, t]
            pair.append(value)
        return shift_pair(tuple(pair), -cy, -cz, 0.0)

    parts = {}
    for x in range(-1, 5):
        h = [cotangent(p, x) for p in range(19)]
        blend = layer_of(x, BLEND, NEAR_BLEND)
        for t in range(2):
            wanted = set(range(19) if 0 <= x <= 3 else DOWN if x < 0 else UP)
            if t == 1:
                wanted = {p for p in wanted if VEL[p][1] != 0}
            out, part = adjoint_collide(
                [s1_ref[p, x + 1, t] for p in range(19)],
                blend[t],
                [h[p][t] for p in range(19)],
                wanted,
                t == 0 and 0 <= x <= 3,
            )
            for p, value in out.items():
                a1_ref[p, x + 1, t] = masked(x, value, 0.0)
            if part is not None:
                parts[x] = part
    for x in range(4):
        sensitivity_ref[x] = parts[x]

    for x in range(4):
        h = []
        for p in range(19):
            cx, cy, cz = VEL[p]
            at = x + cx + 1
            tile = a1_ref[p, at, 0]
            if cy:
                tile = shift_y((tile, a1_ref[p, at, 1]), -cy)[0]
            h.append(shift_z(tile, -cz, 0.0))
        out, part = adjoint_collide(
            [f_ref[p, x] for p in range(19)], own_ref[BLEND, x], h, set(range(19)), True
        )
        for p in range(19):
            adjoint_ref[p, x] = out[p]
        design = (solid_ref[x] == 0) & (surface_ref[x] == 1)
        sensitivity_ref[x] = jnp.where(design, sensitivity_ref[x] + part, 0.0)


def call(kernel, inputs, shapes, scratch=()):
    vmem = pl.BlockSpec(memory_space=pltpu.VMEM)
    return pl.pallas_call(
        kernel,
        out_shape=[jax.ShapeDtypeStruct(shape, jnp.float32) for shape in shapes],
        in_specs=[vmem] * len(inputs),
        out_specs=[vmem] * len(shapes),
        scratch_shapes=[pltpu.VMEM(shape, jnp.float32) for shape in scratch],
        compiler_params=pltpu.CompilerParams(vmem_limit_bytes=24 * 1024 * 1024),
    )(*inputs)


def shards(checkpoint, porosity, deposit_weight, solid_mask, surface_mask):
    stream, span = lax.axis_size("stream"), lax.axis_size("span")
    tile = (8, 128)
    block, half = (21, 4) + tile, (21, 2) + tile
    own, mine = call(
        start_kernel,
        (checkpoint, porosity, deposit_weight, solid_mask, surface_mask),
        [block, half],
    )
    cores = [[i, i + 1] for i in range(0, span, 2)]
    chips = [(i, (i + 1) % span) for i in range(1, span, 2)]
    came = lax.ppermute(mine, "span", chips + [(b, a) for a, b in chips])
    both = lax.all_gather(own, "span", axis_index_groups=cores)
    rows = (19, 2, 2) + tile
    message = (LAYERS, 2) + tile
    side, state, following, up, down = call(
        inner_kernel, (own, both, came), [block, rows, rows, message, message]
    )
    low = lax.ppermute(up, "stream", [(i, (i + 1) % stream) for i in range(stream)])
    high = lax.ppermute(down, "stream", [((i + 1) % stream, i) for i in range(stream)])
    adjoint, sensitivity = call(
        last_kernel,
        (
            checkpoint, solid_mask, surface_mask, own, side, state, following, up, down,
            low, high,
        ),
        [(19, 4) + tile, (4,) + tile],
        [(19, 8, 2) + tile, (19, 6, 2) + tile, (19, 6, 2) + tile, (4, 8, 2) + tile],
    )
    return (adjoint, sensitivity)


def solution(mesh):
    placed = (
        P(None, "stream", "span", None),
        P("stream", "span", None),
        P("stream", "span", None),
        P("stream", "span", None),
        P("stream", "span", None),
    )
    return jax.shard_map(
        shards,
        mesh=mesh,
        in_specs=placed,
        out_specs=(P(None, "stream", "span", None), P("stream", "span", None)),
        check_vma=False,
    )
```

```python
import functools

import jax
import jax.numpy as jnp
import numpy as np
from jax import lax
from jax.experimental import pallas as pl
from jax.experimental.pallas import tpu as pltpu
from jax.sharding import PartitionSpec as P

VELOCITY = np.array(
    [
        [0, 0, 0],
        [1, 0, 0],
        [-1, 0, 0],
        [0, 1, 0],
        [0, -1, 0],
        [0, 0, 1],
        [0, 0, -1],
        [1, 1, 0],
        [-1, -1, 0],
        [1, -1, 0],
        [-1, 1, 0],
        [1, 0, 1],
        [-1, 0, -1],
        [1, 0, -1],
        [-1, 0, 1],
        [0, 1, 1],
        [0, -1, -1],
        [0, 1, -1],
        [0, -1, 1],
    ]
)
WEIGHTS = np.array([1.0 / 3.0] + [1.0 / 18.0] * 6 + [1.0 / 36.0] * 12)
GHOST_DENSITY = 18.0
INFLOW_SPEED = 0.08
GHOST_STATE = (
    WEIGHTS
    * GHOST_DENSITY
    * (
        1.0
        + 3.0 * VELOCITY[:, 0] * INFLOW_SPEED
        + 4.5 * (VELOCITY[:, 0] * INFLOW_SPEED) ** 2
        - 1.5 * INFLOW_SPEED**2
    )
)
GHOST = [float(value) for value in GHOST_STATE]
VEL = [tuple(int(part) for part in row) for row in VELOCITY]
CX = [row[0] for row in VEL]
UP = [p for p in range(19) if CX[p] == 1]
DOWN = [p for p in range(19) if CX[p] == -1]
FLAT = [p for p in range(19) if CX[p] == 0]
OPP = [0] + [p + 1 if p % 2 else p - 1 for p in range(1, 19)]
BLEND, WEIGHT = 19, 20
STATE, MOMENTS, NEAR_BLEND, WIDE = 0, 5, 9, 10
SUM_FAR, SUM_NEAR, SUM_OWN, WEIGHT_FAR, WEIGHT_NEAR, LAYERS = 10, 14, 18, 21, 22, 23
TILES = LAYERS + WIDE + (LAYERS - WIDE + 1) // 2


def sublane(tile):
    return lax.broadcasted_iota(jnp.int32, tile.shape, len(tile.shape) - 2)


def lane(tile):
    return lax.broadcasted_iota(jnp.int32, tile.shape, len(tile.shape) - 1)


def shift_z(tile, step, fill):
    if step == 0:
        return tile
    rolled = pltpu.roll(tile, step % 128, 1)
    return jnp.where(lane(tile) == (0 if step == 1 else 127), fill, rolled)


def shift_y(pair, step):
    if step == 0:
        return pair
    own, side = (pltpu.roll(tile, step % 8, 0) for tile in pair)
    edge = sublane(own) == (0 if step == 1 else 7)
    return (jnp.where(edge, side, own), jnp.where(edge, own, side))


def shift_pair(pair, stepy, stepz, fill):
    return tuple(shift_z(tile, stepz, fill) for tile in shift_y(pair, stepy))


def pairs_of(f):
    sums = [f[2 * i + 1] + f[2 * i + 2] for i in range(9)]
    diffs = [f[2 * i + 1] - f[2 * i + 2] for i in range(9)]
    return sums, diffs


def along_axes(v):
    return (
        v[0] + v[3] + v[4] + v[5] + v[6],
        v[1] + v[3] - v[4] + v[7] + v[8],
        v[2] + v[5] - v[6] + v[7] - v[8],
    )


def dots(u):
    x, y, z = u
    return [x, y, z, x + y, x - y, x + z, x - z, y + z, y - z]


def flow(f0, sums, diffs):
    density = f0 + sum(sums[1:], sums[0])
    inverse = 1.0 / density
    u = [m * inverse for m in along_axes(diffs)]
    square = u[0] * u[0] + u[1] * u[1] + u[2] * u[2]
    return density, u, square


def collide(f, b):
    sums, diffs = pairs_of(f)
    density, u, square = flow(f[0], sums, diffs)
    keep = 1.0 - b
    j = 0.1 * keep
    alpha, beta = 0.5 * (j + b), 0.5 * (j - b)
    scaled = (0.9 * keep) * density
    rest = scaled * (1.0 - 1.5 * square)
    flux = dots([scaled * part for part in u])
    out = [(j + b) * f[0] + (1.0 / 3.0) * rest]
    rest_axis, rest_diag = rest * (1.0 / 18.0), rest * (1.0 / 36.0)
    for i, along in enumerate(dots(u)):
        w = 1.0 / 18.0 if i < 3 else 1.0 / 36.0
        even = alpha * sums[i] + (rest_axis if i < 3 else rest_diag) + flux[i] * along * (4.5 * w)
        odd = beta * diffs[i] + flux[i] * (3.0 * w)
        out += [even + odd, even - odd]
    return out


def adjoint_values(u, square, b, h, wanted):
    s, d = pairs_of(h)
    w = [1.0 / 18.0] * 3 + [1.0 / 36.0] * 6
    t = [s[i] * w[i] for i in range(9)]
    h0 = h[0] * (1.0 / 3.0) + sum(t[1:], t[0])
    h1 = along_axes([d[i] * w[i] for i in range(9)])
    xx = t[0] + t[3] + t[4] + t[5] + t[6]
    yy = t[1] + t[3] + t[4] + t[7] + t[8]
    zz = t[2] + t[5] + t[6] + t[7] + t[8]
    xy, xz, yz = t[3] - t[4], t[5] - t[6], t[7] - t[8]
    v = (
        xx * u[0] + xy * u[1] + xz * u[2],
        xy * u[0] + yy * u[1] + yz * u[2],
        xz * u[0] + yz * u[1] + zz * u[2],
    )
    quad = u[0] * v[0] + u[1] * v[1] + u[2] * v[2]
    keep = 1.0 - b
    j, k = 0.1 * keep, 0.9 * keep
    alpha, beta = 0.5 * (j + b), 0.5 * (j - b)
    base = k * (h0 * (1.0 + 1.5 * square) - 4.5 * quad)
    push = dots([k * (3.0 * h1[i] + 9.0 * v[i] - 3.0 * u[i] * h0) for i in range(3)])
    out = {}
    if 0 in wanted:
        out[0] = (j + b) * h[0] + base
    for i in range(9):
        first, second = 2 * i + 1, 2 * i + 2
        if first in wanted or second in wanted:
            even = alpha * s[i] + base
            odd = beta * d[i] + push[i]
            if first in wanted:
                out[first] = even + odd
            if second in wanted:
                out[second] = even - odd
    return out, s, d, h0, h1, quad


def adjoint_collide(f, b, h, wanted, blend_part):
    fsums, fdiffs = pairs_of(f)
    density, u, square = flow(f[0], fsums, fdiffs)
    out, s, d, h0, h1, quad = adjoint_values(u, square, b, h, wanted)
    part = None
    if blend_part:
        equil = h0 * (1.0 - 1.5 * square) + 4.5 * quad
        equil = equil + 3.0 * (u[0] * h1[0] + u[1] * h1[1] + u[2] * h1[2])
        evens = sum((s[i] * fsums[i] for i in range(1, 9)), s[0] * fsums[0])
        odds = sum((d[i] * fdiffs[i] for i in range(1, 9)), d[0] * fdiffs[0])
        part = 0.9 * h[0] * f[0] + 0.45 * evens - 0.55 * odds - 0.9 * density * equil
    return out, part


def moment_sums(values):
    density = functools.reduce(lambda a, b: a + b, values.values())
    momentum = []
    for k in range(3):
        total = None
        for p, value in values.items():
            if VEL[p][k] == 1:
                total = value if total is None else total + value
        for p, value in values.items():
            if VEL[p][k] == -1:
                total = -value if total is None else total - value
        momentum.append(total)
    return [density] + momentum


def add(*totals):
    return [functools.reduce(lambda a, b: a + b, parts) for parts in zip(*totals)]


def put_message(ref, layers):
    for i, pair in enumerate(layers):
        ref[i] = pair[0]
    for i in range(WIDE):
        ref[LAYERS + i] = layers[i][1]
    for i in range(WIDE, LAYERS, 2):
        tile = layers[i][1]
        if i + 1 < LAYERS:
            at = sublane(tile)
            tile = jnp.where((at < 2) | (at > 5), tile, pltpu.roll(layers[i + 1][1], 4, 0))
        ref[LAYERS + WIDE + (i - WIDE) // 2] = tile


def get_message(ref, i):
    if i < WIDE:
        return (ref[i], ref[LAYERS + i])
    tile = ref[LAYERS + WIDE + (i - WIDE) // 2]
    return (ref[i], pltpu.roll(tile, 4, 0) if (i - WIDE) % 2 else tile)


def start_kernel(
    f_hbm, porosity_hbm, weight_hbm, solid_hbm, surface_hbm, own_ref, half_ref,
    f_ref, porosity_ref, weight_ref, solid_ref, surface_ref, sems,
):
    copies = [
        pltpu.make_async_copy(source, target, sems.at[i])
        for i, (source, target) in enumerate(
            (
                (solid_hbm, solid_ref),
                (surface_hbm, surface_ref),
                (porosity_hbm, porosity_ref),
                (weight_hbm, weight_ref),
                (f_hbm, f_ref),
            )
        )
    ]
    for copy in copies:
        copy.start()
    for copy in copies:
        copy.wait()
    core = lax.rem(lax.axis_index("span"), 2)
    for x in range(4):
        porosity = porosity_ref[x]
        blend = jnp.where(
            solid_ref[x] == 1, 1.0, jnp.where(surface_ref[x] == 1, porosity, 0.0)
        )
        out = collide([f_ref[p, x] for p in range(19)], blend)
        for p in range(19):
            own_ref[p, x] = out[p]
        own_ref[BLEND, x] = blend
        own_ref[WEIGHT, x] = weight_ref[x]
    for layer in range(21):
        for pair in range(2):
            first, second = own_ref[layer, 2 * pair], own_ref[layer, 2 * pair + 1]
            low = (sublane(first) < 4) == (core == 0)
            half_ref[layer, pair] = jnp.where(low, first, pltpu.roll(second, 4, 0))


def inner_kernel(own_ref, both_ref, half_ref, side_ref, state_ref, next_ref, up_ref, down_ref):
    core = lax.rem(lax.axis_index("span"), 2)
    for layer in range(21):
        for pair in range(2):
            came = half_ref[layer, pair]
            low = (sublane(came) < 4) == (core == 0)
            for x, tile in ((2 * pair, came), (2 * pair + 1, pltpu.roll(came, 4, 0))):
                side_ref[layer, x] = jnp.where(low, both_ref[1 - core, layer, x], tile)

    def c0(p, x):
        return (own_ref[p, x], side_ref[p, x])

    def moved(p, pair):
        return shift_pair(pair, VEL[p][1], VEL[p][2], GHOST[p])

    for x in (1, 2):
        f = [moved(p, c0(p, x - CX[p])) for p in range(19)]
        blend = c0(BLEND, x)
        for t in range(2):
            tiles = [f[p][t] for p in range(19)]
            out = collide(tiles, blend[t])
            for p in range(19):
                state_ref[p, x - 1, t] = tiles[p]
                next_ref[p, x - 1, t] = out[p]

    def c1(p, x):
        return (next_ref[p, x - 1, 0], next_ref[p, x - 1, 1])

    for ref, near, far, inward, outward in (
        (up_ref, 3, 2, UP, DOWN),
        (down_ref, 0, 1, DOWN, UP),
    ):
        step = far - near
        enter = [moved(p, c0(p, near)) for p in inward]
        known = {p: moved(p, c0(p, near if p in FLAT else far)) for p in inward + FLAT}
        blend = c0(BLEND, near)
        j = [0.1 * (1.0 - part) for part in blend]
        layers = [None] * LAYERS
        layers[STATE : STATE + 5] = enter
        halves = [moment_sums({p: known[p][t] for p in known}) for t in range(2)]
        layers[MOMENTS : MOMENTS + 4] = list(zip(*halves))
        layers[NEAR_BLEND] = blend
        came = {p: moved(p, c1(p, far + step)) for p in inward}
        came.update({p: moved(p, c1(p, far)) for p in FLAT})
        for p in outward:
            came[p] = moved(p, tuple(blend[t] * known[OPP[p]][t] for t in range(2)))
        halves = [moment_sums({p: came[p][t] for p in came}) for t in range(2)]
        layers[SUM_FAR : SUM_FAR + 4] = list(zip(*halves))
        came = {p: moved(p, c1(p, far)) for p in inward}
        for p in FLAT:
            came[p] = moved(
                p,
                tuple(j[t] * known[p][t] + blend[t] * known[OPP[p]][t] for t in range(2)),
            )
        halves = [moment_sums({p: came[p][t] for p in came}) for t in range(2)]
        layers[SUM_NEAR : SUM_NEAR + 4] = list(zip(*halves))
        came = {p: moved(p, tuple(j[t] * known[p][t] for t in range(2))) for p in inward}
        halves = [moment_sums({p: came[p][t] for p in came}) for t in range(2)]
        halves = [[half[0], half[2], half[3]] for half in halves]
        layers[SUM_OWN : SUM_OWN + 3] = list(zip(*halves))
        layers[WEIGHT_FAR] = c0(WEIGHT, far)
        layers[WEIGHT_NEAR] = c0(WEIGHT, near)
        put_message(ref, layers)


def last_kernel(
    f_ref, solid_ref, surface_ref, own_ref, side_ref, state_ref, next_ref, low_ref, high_ref,
    adjoint_ref, sensitivity_ref, s1_ref, c1_ref, sum_ref, flow_ref, a1_ref, field_ref,
):
    place = lax.axis_index("stream")
    at_start = place == 0
    at_end = place == lax.axis_size("stream") - 1
    ends = (
        (low_ref, at_start, 0, -1, UP, DOWN),
        (high_ref, at_end, 3, 1, DOWN, UP),
    )

    def moved(p, pair, fill=None):
        return shift_pair(pair, VEL[p][1], VEL[p][2], GHOST[p] if fill is None else fill)

    def c0(p, x):
        return (own_ref[p, x], side_ref[p, x])

    for x in (1, 2):
        for p in range(19):
            for t in range(2):
                s1_ref[p, x, t] = state_ref[p, x - 1, t]
                c1_ref[p, x, t] = next_ref[p, x - 1, t]
    for ref, end, x, out, inward, outward in ends:
        f = {p: moved(p, c0(p, x if p in FLAT else x - out)) for p in FLAT + outward}
        for i, p in enumerate(inward):
            f[p] = tuple(
                jnp.where(end, GHOST[p], part) for part in get_message(ref, STATE + i)
            )
        blend = c0(BLEND, x)
        for t in range(2):
            tiles = [f[p][t] for p in range(19)]
            after = collide(tiles, blend[t])
            for p in range(19):
                s1_ref[p, x, t] = tiles[p]
                c1_ref[p, x, t] = after[p]

    def c1(p, x):
        return (c1_ref[p, x, 0], c1_ref[p, x, 1])

    def save_field(x, t, total, weight, end=None):
        inverse = 1.0 / total[0]
        u = [total[i] * inverse for i in range(1, 4)]
        kinetic = 0.5 * (u[0] * u[0] + u[1] * u[1] + u[2] * u[2])
        for i, value in enumerate(u + [kinetic]):
            value = weight * value
            field_ref[i, x + 2, t] = value if end is None else jnp.where(end, 0.0, value)

    for side, (ref, end, x, out, inward, outward) in enumerate(ends):
        sent = [get_message(ref, i) for i in range(LAYERS)]
        blend = sent[NEAR_BLEND]
        leaving = {p: moved(p, c0(p, x)) for p in outward}
        to_far, to_near, to_own = {}, {}, {}
        for t in range(2):
            total = add(
                moment_sums({p: leaving[p][t] for p in outward}),
                [sent[MOMENTS + i][t] for i in range(4)],
            )
            density = total[0]
            inverse = 1.0 / density
            u = [part * inverse for part in total[1:]]
            square = u[0] * u[0] + u[1] * u[1] + u[2] * u[2]
            for i, value in enumerate(u + [square]):
                flow_ref[side, i, t] = value
            keep = 1.0 - blend[t]
            scaled = (0.9 * keep) * density
            rest = scaled * (1.0 - 1.5 * square)
            along = dots(u)
            for p in range(19):
                value = float(WEIGHTS[p]) * rest
                if p:
                    cu = along[(p - 1) // 2]
                    flux = scaled * cu
                    value = value + flux * cu * float(4.5 * WEIGHTS[p])
                    value = value + flux * float((3.0 if p % 2 else -3.0) * WEIGHTS[p])
                if p in outward:
                    to_far.setdefault(p, []).append(value + 0.1 * keep * leaving[p][t])
                elif p in inward:
                    to_own.setdefault(p, []).append(value + blend[t] * leaving[OPP[p]][t])
                else:
                    to_near.setdefault(p, []).append(value)
        to_far = {p: moved(p, tuple(pair), 0.0) for p, pair in to_far.items()}
        to_near = {p: moved(p, tuple(pair), 0.0) for p, pair in to_near.items()}
        to_own = {p: moved(p, tuple(pair), 0.0) for p, pair in to_own.items()}
        back = {p: moved(p, c1(p, x)) for p in outward}
        for t in range(2):
            total = add(
                moment_sums({p: to_far[p][t] for p in to_far}),
                [sent[SUM_FAR + i][t] for i in range(4)],
            )
            save_field(x + 2 * out, t, total, sent[WEIGHT_FAR][t], end)
            near = dict(to_near)
            near.update(back)
            total = add(
                moment_sums({p: near[p][t] for p in near}),
                [sent[SUM_NEAR + i][t] for i in range(4)],
            )
            save_field(x + out, t, total, sent[WEIGHT_NEAR][t], end)
            own = moment_sums({p: to_own[p][t] for p in to_own})
            ready = [sent[SUM_OWN + i][t] for i in range(3)]
            own = add(own, [ready[0], -out * ready[0], ready[1], ready[2]])
            ghost = moment_sums({p: GHOST[p] for p in inward})
            for i in range(4):
                sum_ref[side, i, t] = jnp.where(end, ghost[i], own[i])

    for x in range(4):
        pops, given = list(range(19)), None
        if x == 0:
            pops, given = FLAT + DOWN, 0
        if x == 3:
            pops, given = FLAT + UP, 1
        came = {p: moved(p, c1(p, x - CX[p])) for p in pops}
        weight = c0(WEIGHT, x)
        for t in range(2):
            total = moment_sums({p: came[p][t] for p in came})
            if given is not None:
                total = add(total, [sum_ref[given, i, t] for i in range(4)])
            save_field(x, t, total, weight[t])

    def cotangent(p, x):
        pair = []
        for t in range(2):
            value = -field_ref[3, x + CX[p] + 2, t]
            for k in range(3):
                if VEL[p][k] == 1:
                    value = value + field_ref[k, x + CX[p] + 2, t]
                if VEL[p][k] == -1:
                    value = value - field_ref[k, x + CX[p] + 2, t]
            pair.append(value)
        return shift_pair(tuple(pair), -VEL[p][1], -VEL[p][2], 0.0)

    for x in range(4):
        h = [cotangent(p, x) for p in range(19)]
        blend = c0(BLEND, x)
        for t in range(2):
            wanted = [p for p in range(19) if t == 0 or VEL[p][1] != 0]
            out, part = adjoint_collide(
                [s1_ref[p, x, t] for p in range(19)],
                blend[t],
                [h[p][t] for p in range(19)],
                wanted,
                t == 0,
            )
            for p, value in out.items():
                a1_ref[p, x + 1, t] = value
            if part is not None:
                sensitivity_ref[x] = part
    for side, (ref, end, x, out, inward, outward) in enumerate(ends):
        h = [cotangent(p, x + out) for p in range(19)]
        blend = get_message(ref, NEAR_BLEND)
        for t in range(2):
            u = [flow_ref[side, i, t] for i in range(3)]
            wanted = [p for p in outward if t == 0 or VEL[p][1] != 0]
            got = adjoint_values(
                u, flow_ref[side, 3, t], blend[t], [h[p][t] for p in range(19)], wanted
            )[0]
            for p, value in got.items():
                a1_ref[p, x + out + 1, t] = jnp.where(end, 0.0, value)

    for x in range(4):
        h = []
        for p in range(19):
            at = x + CX[p] + 1
            tile = a1_ref[p, at, 0]
            if VEL[p][1]:
                tile = shift_y((tile, a1_ref[p, at, 1]), -VEL[p][1])[0]
            h.append(shift_z(tile, -VEL[p][2], 0.0))
        out, part = adjoint_collide(
            [f_ref[p, x] for p in range(19)], own_ref[BLEND, x], h, list(range(19)), True
        )
        for p in range(19):
            adjoint_ref[p, x] = out[p]
        design = (solid_ref[x] == 0) & (surface_ref[x] == 1)
        sensitivity_ref[x] = jnp.where(design, sensitivity_ref[x] + part, 0.0)


def call(kernel, inputs, shapes, scratch=(), space=pltpu.VMEM):
    return pl.pallas_call(
        kernel,
        out_shape=[jax.ShapeDtypeStruct(shape, jnp.float32) for shape in shapes],
        in_specs=[pl.BlockSpec(memory_space=space)] * len(inputs),
        out_specs=[pl.BlockSpec(memory_space=pltpu.VMEM)] * len(shapes),
        scratch_shapes=scratch,
        compiler_params=pltpu.CompilerParams(vmem_limit_bytes=24 * 1024 * 1024),
    )(*inputs)


def shards(checkpoint, porosity, deposit_weight, solid_mask, surface_mask):
    stream, span = lax.axis_size("stream"), lax.axis_size("span")
    tile = (8, 128)
    block, half = (21, 4) + tile, (21, 2) + tile
    inputs = (checkpoint, porosity, deposit_weight, solid_mask, surface_mask)
    own, mine = call(
        start_kernel,
        inputs,
        [block, half],
        [pltpu.VMEM(value.shape, value.dtype) for value in inputs]
        + [pltpu.SemaphoreType.DMA((5,))],
        pltpu.HBM,
    )
    cores = [[i, i + 1] for i in range(0, span, 2)]
    chips = [(i, (i + 1) % span) for i in range(1, span, 2)]
    came = lax.ppermute(mine, "span", chips + [(b, a) for a, b in chips])
    both = lax.all_gather(own, "span", axis_index_groups=cores)
    rows = (19, 2, 2) + tile
    message = (TILES,) + tile
    side, state, following, up, down = call(
        inner_kernel, (own, both, came), [block, rows, rows, message, message]
    )
    low = lax.ppermute(up, "stream", [(i, i + 1) for i in range(stream - 1)])
    high = lax.ppermute(down, "stream", [(i + 1, i) for i in range(stream - 1)])
    scratch = [(19, 4, 2), (19, 4, 2), (2, 4, 2), (2, 4, 2), (19, 6, 2), (4, 8, 2)]
    adjoint, sensitivity = call(
        last_kernel,
        (checkpoint, solid_mask, surface_mask, own, side, state, following, low, high),
        [(19, 4) + tile, (4,) + tile],
        [pltpu.VMEM(shape + tile, jnp.float32) for shape in scratch],
    )
    return (adjoint, sensitivity)


def solution(mesh):
    placed = (
        P(None, "stream", "span", None),
        P("stream", "span", None),
        P("stream", "span", None),
        P("stream", "span", None),
        P("stream", "span", None),
    )
    return jax.shard_map(
        shards,
        mesh=mesh,
        in_specs=placed,
        out_specs=(P(None, "stream", "span", None), P("stream", "span", None)),
        check_vma=False,
    )
```

```python
import functools

import jax
import jax.numpy as jnp
import numpy as np
from jax import lax
from jax.experimental import pallas as pl
from jax.experimental.pallas import tpu as pltpu
from jax.sharding import PartitionSpec as P

VELOCITY = np.array(
    [
        [0, 0, 0],
        [1, 0, 0],
        [-1, 0, 0],
        [0, 1, 0],
        [0, -1, 0],
        [0, 0, 1],
        [0, 0, -1],
        [1, 1, 0],
        [-1, -1, 0],
        [1, -1, 0],
        [-1, 1, 0],
        [1, 0, 1],
        [-1, 0, -1],
        [1, 0, -1],
        [-1, 0, 1],
        [0, 1, 1],
        [0, -1, -1],
        [0, 1, -1],
        [0, -1, 1],
    ]
)
WEIGHTS = np.array([1.0 / 3.0] + [1.0 / 18.0] * 6 + [1.0 / 36.0] * 12)
GHOST_DENSITY = 18.0
INFLOW_SPEED = 0.08
GHOST_STATE = (
    WEIGHTS
    * GHOST_DENSITY
    * (
        1.0
        + 3.0 * VELOCITY[:, 0] * INFLOW_SPEED
        + 4.5 * (VELOCITY[:, 0] * INFLOW_SPEED) ** 2
        - 1.5 * INFLOW_SPEED**2
    )
)
GHOST = [float(value) for value in GHOST_STATE]
VEL = [tuple(int(part) for part in row) for row in VELOCITY]
CX = [row[0] for row in VEL]
UP = [p for p in range(19) if CX[p] == 1]
DOWN = [p for p in range(19) if CX[p] == -1]
FLAT = [p for p in range(19) if CX[p] == 0]
OPP = [0] + [p + 1 if p % 2 else p - 1 for p in range(1, 19)]
BLEND, WEIGHT = 19, 20
STATE, MOMENTS, NEAR_BLEND, WIDE = 0, 5, 9, 10
SUM_FAR, SUM_NEAR, SUM_OWN, WEIGHT_FAR, WEIGHT_NEAR, LAYERS = 10, 14, 18, 21, 22, 23
TILES = LAYERS + WIDE + (LAYERS - WIDE + 1) // 2


def sublane(tile):
    return lax.broadcasted_iota(jnp.int32, tile.shape, len(tile.shape) - 2)


def lane(tile):
    return lax.broadcasted_iota(jnp.int32, tile.shape, len(tile.shape) - 1)


def shift_z(tile, step, fill):
    if step == 0:
        return tile
    rolled = pltpu.roll(tile, step % 128, 1)
    return jnp.where(lane(tile) == (0 if step == 1 else 127), fill, rolled)


def shift_y(pair, step):
    if step == 0:
        return pair
    own, side = (pltpu.roll(tile, step % 8, 0) for tile in pair)
    edge = sublane(own) == (0 if step == 1 else 7)
    return (jnp.where(edge, side, own), jnp.where(edge, own, side))


def shift_pair(pair, stepy, stepz, fill):
    return tuple(shift_z(tile, stepz, fill) for tile in shift_y(pair, stepy))


def pairs_of(f):
    sums = [f[2 * i + 1] + f[2 * i + 2] for i in range(9)]
    diffs = [f[2 * i + 1] - f[2 * i + 2] for i in range(9)]
    return sums, diffs


def along_axes(v):
    return (
        v[0] + v[3] + v[4] + v[5] + v[6],
        v[1] + v[3] - v[4] + v[7] + v[8],
        v[2] + v[5] - v[6] + v[7] - v[8],
    )


def dots(u):
    x, y, z = u
    return [x, y, z, x + y, x - y, x + z, x - z, y + z, y - z]


def flow(f0, sums, diffs):
    density = f0 + sum(sums[1:], sums[0])
    inverse = 1.0 / density
    u = [m * inverse for m in along_axes(diffs)]
    square = u[0] * u[0] + u[1] * u[1] + u[2] * u[2]
    return density, u, square


def collide(f, b):
    sums, diffs = pairs_of(f)
    density, u, square = flow(f[0], sums, diffs)
    keep = 1.0 - b
    j = 0.1 * keep
    alpha, beta = 0.5 * (j + b), 0.5 * (j - b)
    scaled = (0.9 * keep) * density
    rest = scaled * (1.0 - 1.5 * square)
    flux = dots([scaled * part for part in u])
    out = [(j + b) * f[0] + (1.0 / 3.0) * rest]
    rest_axis, rest_diag = rest * (1.0 / 18.0), rest * (1.0 / 36.0)
    for i, along in enumerate(dots(u)):
        w = 1.0 / 18.0 if i < 3 else 1.0 / 36.0
        even = alpha * sums[i] + (rest_axis if i < 3 else rest_diag) + flux[i] * along * (4.5 * w)
        odd = beta * diffs[i] + flux[i] * (3.0 * w)
        out += [even + odd, even - odd]
    return out


def adjoint_values(u, square, b, h, wanted):
    s, d = pairs_of(h)
    w = [1.0 / 18.0] * 3 + [1.0 / 36.0] * 6
    t = [s[i] * w[i] for i in range(9)]
    h0 = h[0] * (1.0 / 3.0) + sum(t[1:], t[0])
    h1 = along_axes([d[i] * w[i] for i in range(9)])
    xx = t[0] + t[3] + t[4] + t[5] + t[6]
    yy = t[1] + t[3] + t[4] + t[7] + t[8]
    zz = t[2] + t[5] + t[6] + t[7] + t[8]
    xy, xz, yz = t[3] - t[4], t[5] - t[6], t[7] - t[8]
    v = (
        xx * u[0] + xy * u[1] + xz * u[2],
        xy * u[0] + yy * u[1] + yz * u[2],
        xz * u[0] + yz * u[1] + zz * u[2],
    )
    quad = u[0] * v[0] + u[1] * v[1] + u[2] * v[2]
    keep = 1.0 - b
    j, k = 0.1 * keep, 0.9 * keep
    alpha, beta = 0.5 * (j + b), 0.5 * (j - b)
    base = k * (h0 * (1.0 + 1.5 * square) - 4.5 * quad)
    push = dots([k * (3.0 * h1[i] + 9.0 * v[i] - 3.0 * u[i] * h0) for i in range(3)])
    out = {}
    if 0 in wanted:
        out[0] = (j + b) * h[0] + base
    for i in range(9):
        first, second = 2 * i + 1, 2 * i + 2
        if first in wanted or second in wanted:
            even = alpha * s[i] + base
            odd = beta * d[i] + push[i]
            if first in wanted:
                out[first] = even + odd
            if second in wanted:
                out[second] = even - odd
    return out, s, d, h0, h1, quad


def adjoint_collide(f, b, h, wanted, blend_part):
    fsums, fdiffs = pairs_of(f)
    density, u, square = flow(f[0], fsums, fdiffs)
    out, s, d, h0, h1, quad = adjoint_values(u, square, b, h, wanted)
    part = None
    if blend_part:
        equil = h0 * (1.0 - 1.5 * square) + 4.5 * quad
        equil = equil + 3.0 * (u[0] * h1[0] + u[1] * h1[1] + u[2] * h1[2])
        evens = sum((s[i] * fsums[i] for i in range(1, 9)), s[0] * fsums[0])
        odds = sum((d[i] * fdiffs[i] for i in range(1, 9)), d[0] * fdiffs[0])
        part = 0.9 * h[0] * f[0] + 0.45 * evens - 0.55 * odds - 0.9 * density * equil
    return out, part


def moment_sums(values):
    density = functools.reduce(lambda a, b: a + b, values.values())
    momentum = []
    for k in range(3):
        total = None
        for p, value in values.items():
            if VEL[p][k] == 1:
                total = value if total is None else total + value
        for p, value in values.items():
            if VEL[p][k] == -1:
                total = -value if total is None else total - value
        momentum.append(total)
    return [density] + momentum


def add(*totals):
    return [functools.reduce(lambda a, b: a + b, parts) for parts in zip(*totals)]


def put_message(ref, layers):
    for i, pair in enumerate(layers):
        ref[i] = pair[0]
    for i in range(WIDE):
        ref[LAYERS + i] = layers[i][1]
    for i in range(WIDE, LAYERS, 2):
        tile = layers[i][1]
        if i + 1 < LAYERS:
            at = sublane(tile)
            tile = jnp.where((at < 2) | (at > 5), tile, pltpu.roll(layers[i + 1][1], 4, 0))
        ref[LAYERS + WIDE + (i - WIDE) // 2] = tile


def get_message(ref, i):
    if i < WIDE:
        return (ref[i], ref[LAYERS + i])
    tile = ref[LAYERS + WIDE + (i - WIDE) // 2]
    return (ref[i], pltpu.roll(tile, 4, 0) if (i - WIDE) % 2 else tile)


def start_kernel(
    f_hbm, porosity_hbm, weight_hbm, solid_hbm, surface_hbm, own_ref, half_ref,
    f_ref, porosity_ref, weight_ref, solid_ref, surface_ref, sems,
):
    copies = [
        pltpu.make_async_copy(source, target, sems.at[i])
        for i, (source, target) in enumerate(
            (
                (solid_hbm, solid_ref),
                (surface_hbm, surface_ref),
                (porosity_hbm, porosity_ref),
                (weight_hbm, weight_ref),
                (f_hbm, f_ref),
            )
        )
    ]
    for copy in copies:
        copy.start()
    for copy in copies:
        copy.wait()
    core = lax.rem(lax.axis_index("span"), 2)
    for x in range(4):
        porosity = porosity_ref[x]
        blend = jnp.where(
            solid_ref[x] == 1, 1.0, jnp.where(surface_ref[x] == 1, porosity, 0.0)
        )
        out = collide([f_ref[p, x] for p in range(19)], blend)
        for p in range(19):
            own_ref[p, x] = out[p]
        own_ref[BLEND, x] = blend
        own_ref[WEIGHT, x] = weight_ref[x]
    for layer in range(21):
        for pair in range(2):
            first, second = own_ref[layer, 2 * pair], own_ref[layer, 2 * pair + 1]
            low = (sublane(first) < 4) == (core == 0)
            half_ref[layer, pair] = jnp.where(low, first, pltpu.roll(second, 4, 0))


def inner_kernel(own_ref, both_ref, half_ref, side_ref, state_ref, next_ref, up_ref, down_ref):
    core = lax.rem(lax.axis_index("span"), 2)
    for layer in range(21):
        for pair in range(2):
            came = half_ref[layer, pair]
            low = (sublane(came) < 4) == (core == 0)
            for x, tile in ((2 * pair, came), (2 * pair + 1, pltpu.roll(came, 4, 0))):
                side_ref[layer, x] = jnp.where(low, both_ref[1 - core, layer, x], tile)

    def c0(p, x):
        return (own_ref[p, x], side_ref[p, x])

    def moved(p, pair):
        return shift_pair(pair, VEL[p][1], VEL[p][2], GHOST[p])

    for x in (1, 2):
        f = [moved(p, c0(p, x - CX[p])) for p in range(19)]
        blend = c0(BLEND, x)
        for t in range(2):
            tiles = [f[p][t] for p in range(19)]
            out = collide(tiles, blend[t])
            for p in range(19):
                state_ref[p, x - 1, t] = tiles[p]
                next_ref[p, x - 1, t] = out[p]

    def c1(p, x):
        return (next_ref[p, x - 1, 0], next_ref[p, x - 1, 1])

    for ref, near, far, inward, outward in (
        (up_ref, 3, 2, UP, DOWN),
        (down_ref, 0, 1, DOWN, UP),
    ):
        step = far - near
        enter = [moved(p, c0(p, near)) for p in inward]
        known = {p: moved(p, c0(p, near if p in FLAT else far)) for p in inward + FLAT}
        blend = c0(BLEND, near)
        j = [0.1 * (1.0 - part) for part in blend]
        layers = [None] * LAYERS
        layers[STATE : STATE + 5] = enter
        halves = [moment_sums({p: known[p][t] for p in known}) for t in range(2)]
        layers[MOMENTS : MOMENTS + 4] = list(zip(*halves))
        layers[NEAR_BLEND] = blend
        came = {p: moved(p, c1(p, far + step)) for p in inward}
        came.update({p: moved(p, c1(p, far)) for p in FLAT})
        for p in outward:
            came[p] = moved(p, tuple(blend[t] * known[OPP[p]][t] for t in range(2)))
        halves = [moment_sums({p: came[p][t] for p in came}) for t in range(2)]
        layers[SUM_FAR : SUM_FAR + 4] = list(zip(*halves))
        came = {p: moved(p, c1(p, far)) for p in inward}
        for p in FLAT:
            came[p] = moved(
                p,
                tuple(j[t] * known[p][t] + blend[t] * known[OPP[p]][t] for t in range(2)),
            )
        halves = [moment_sums({p: came[p][t] for p in came}) for t in range(2)]
        layers[SUM_NEAR : SUM_NEAR + 4] = list(zip(*halves))
        came = {p: moved(p, tuple(j[t] * known[p][t] for t in range(2))) for p in inward}
        halves = [moment_sums({p: came[p][t] for p in came}) for t in range(2)]
        halves = [[half[0], half[2], half[3]] for half in halves]
        layers[SUM_OWN : SUM_OWN + 3] = list(zip(*halves))
        layers[WEIGHT_FAR] = c0(WEIGHT, far)
        layers[WEIGHT_NEAR] = c0(WEIGHT, near)
        put_message(ref, layers)


def last_kernel(
    f_ref, solid_ref, surface_ref, own_ref, side_ref, state_ref, next_ref, low_ref, high_ref,
    adjoint_ref, sensitivity_ref, s1_ref, c1_ref, sum_ref, flow_ref, a1_ref, field_ref,
):
    place = lax.axis_index("stream")
    at_start = place == 0
    at_end = place == lax.axis_size("stream") - 1
    ends = (
        (low_ref, at_start, 0, -1, UP, DOWN),
        (high_ref, at_end, 3, 1, DOWN, UP),
    )

    def moved(p, pair, fill=None):
        return shift_pair(pair, VEL[p][1], VEL[p][2], GHOST[p] if fill is None else fill)

    def c0(p, x):
        return (own_ref[p, x], side_ref[p, x])

    for x in (1, 2):
        for p in range(19):
            for t in range(2):
                s1_ref[p, x, t] = state_ref[p, x - 1, t]
                c1_ref[p, x, t] = next_ref[p, x - 1, t]
    for ref, end, x, out, inward, outward in ends:
        f = {p: moved(p, c0(p, x if p in FLAT else x - out)) for p in FLAT + outward}
        for i, p in enumerate(inward):
            f[p] = tuple(
                jnp.where(end, GHOST[p], part) for part in get_message(ref, STATE + i)
            )
        blend = c0(BLEND, x)
        for t in range(2):
            tiles = [f[p][t] for p in range(19)]
            after = collide(tiles, blend[t])
            for p in range(19):
                s1_ref[p, x, t] = tiles[p]
                c1_ref[p, x, t] = after[p]

    def c1(p, x):
        return (c1_ref[p, x, 0], c1_ref[p, x, 1])

    def save_field(x, t, total, weight, end=None):
        inverse = 1.0 / total[0]
        u = [total[i] * inverse for i in range(1, 4)]
        kinetic = 0.5 * (u[0] * u[0] + u[1] * u[1] + u[2] * u[2])
        for i, value in enumerate(u + [kinetic]):
            value = weight * value
            field_ref[i, x + 2, t] = value if end is None else jnp.where(end, 0.0, value)

    for side, (ref, end, x, out, inward, outward) in enumerate(ends):
        sent = [get_message(ref, i) for i in range(LAYERS)]
        blend = sent[NEAR_BLEND]
        leaving = {p: moved(p, c0(p, x)) for p in outward}
        to_far, to_near, to_own = {}, {}, {}
        for t in range(2):
            total = add(
                moment_sums({p: leaving[p][t] for p in outward}),
                [sent[MOMENTS + i][t] for i in range(4)],
            )
            density = total[0]
            inverse = 1.0 / density
            u = [part * inverse for part in total[1:]]
            square = u[0] * u[0] + u[1] * u[1] + u[2] * u[2]
            for i, value in enumerate(u + [square]):
                flow_ref[side, i, t] = value
            keep = 1.0 - blend[t]
            scaled = (0.9 * keep) * density
            rest = scaled * (1.0 - 1.5 * square)
            along = dots(u)
            for p in range(19):
                value = float(WEIGHTS[p]) * rest
                if p:
                    cu = along[(p - 1) // 2]
                    flux = scaled * cu
                    value = value + flux * cu * float(4.5 * WEIGHTS[p])
                    value = value + flux * float((3.0 if p % 2 else -3.0) * WEIGHTS[p])
                if p in outward:
                    to_far.setdefault(p, []).append(value + 0.1 * keep * leaving[p][t])
                elif p in inward:
                    to_own.setdefault(p, []).append(value + blend[t] * leaving[OPP[p]][t])
                else:
                    to_near.setdefault(p, []).append(value)
        to_far = {p: moved(p, tuple(pair), 0.0) for p, pair in to_far.items()}
        to_near = {p: moved(p, tuple(pair), 0.0) for p, pair in to_near.items()}
        to_own = {p: moved(p, tuple(pair), 0.0) for p, pair in to_own.items()}
        back = {p: moved(p, c1(p, x)) for p in outward}
        for t in range(2):
            total = add(
                moment_sums({p: to_far[p][t] for p in to_far}),
                [sent[SUM_FAR + i][t] for i in range(4)],
            )
            save_field(x + 2 * out, t, total, sent[WEIGHT_FAR][t], end)
            near = dict(to_near)
            near.update(back)
            total = add(
                moment_sums({p: near[p][t] for p in near}),
                [sent[SUM_NEAR + i][t] for i in range(4)],
            )
            save_field(x + out, t, total, sent[WEIGHT_NEAR][t], end)
            own = moment_sums({p: to_own[p][t] for p in to_own})
            ready = [sent[SUM_OWN + i][t] for i in range(3)]
            own = add(own, [ready[0], -out * ready[0], ready[1], ready[2]])
            ghost = moment_sums({p: GHOST[p] for p in inward})
            for i in range(4):
                sum_ref[side, i, t] = jnp.where(end, ghost[i], own[i])

    for x in range(4):
        pops, given = list(range(19)), None
        if x == 0:
            pops, given = FLAT + DOWN, 0
        if x == 3:
            pops, given = FLAT + UP, 1
        came = {p: moved(p, c1(p, x - CX[p])) for p in pops}
        weight = c0(WEIGHT, x)
        for t in range(2):
            total = moment_sums({p: came[p][t] for p in came})
            if given is not None:
                total = add(total, [sum_ref[given, i, t] for i in range(4)])
            save_field(x, t, total, weight[t])

    def cotangent(p, x):
        pair = []
        for t in range(2):
            value = -field_ref[3, x + CX[p] + 2, t]
            for k in range(3):
                if VEL[p][k] == 1:
                    value = value + field_ref[k, x + CX[p] + 2, t]
                if VEL[p][k] == -1:
                    value = value - field_ref[k, x + CX[p] + 2, t]
            pair.append(value)
        return shift_pair(tuple(pair), -VEL[p][1], -VEL[p][2], 0.0)

    for x in range(4):
        h = [cotangent(p, x) for p in range(19)]
        blend = c0(BLEND, x)
        for t in range(2):
            wanted = [p for p in range(19) if t == 0 or VEL[p][1] != 0]
            out, part = adjoint_collide(
                [s1_ref[p, x, t] for p in range(19)],
                blend[t],
                [h[p][t] for p in range(19)],
                wanted,
                t == 0,
            )
            for p, value in out.items():
                a1_ref[p, x + 1, t] = value
            if part is not None:
                sensitivity_ref[x] = part
    for side, (ref, end, x, out, inward, outward) in enumerate(ends):
        h = [cotangent(p, x + out) for p in range(19)]
        blend = get_message(ref, NEAR_BLEND)
        for t in range(2):
            u = [flow_ref[side, i, t] for i in range(3)]
            wanted = [p for p in outward if t == 0 or VEL[p][1] != 0]
            got = adjoint_values(
                u, flow_ref[side, 3, t], blend[t], [h[p][t] for p in range(19)], wanted
            )[0]
            for p, value in got.items():
                a1_ref[p, x + out + 1, t] = jnp.where(end, 0.0, value)

    for x in range(4):
        h = []
        for p in range(19):
            at = x + CX[p] + 1
            tile = a1_ref[p, at, 0]
            if VEL[p][1]:
                tile = shift_y((tile, a1_ref[p, at, 1]), -VEL[p][1])[0]
            h.append(shift_z(tile, -VEL[p][2], 0.0))
        out, part = adjoint_collide(
            [f_ref[p, x] for p in range(19)], own_ref[BLEND, x], h, list(range(19)), True
        )
        for p in range(19):
            adjoint_ref[p, x] = out[p]
        design = (solid_ref[x] == 0) & (surface_ref[x] == 1)
        sensitivity_ref[x] = jnp.where(design, sensitivity_ref[x] + part, 0.0)


def call(kernel, inputs, shapes, scratch=(), space=pltpu.VMEM):
    return pl.pallas_call(
        kernel,
        out_shape=[jax.ShapeDtypeStruct(shape, jnp.float32) for shape in shapes],
        in_specs=[pl.BlockSpec(memory_space=space)] * len(inputs),
        out_specs=[pl.BlockSpec(memory_space=pltpu.VMEM)] * len(shapes),
        scratch_shapes=scratch,
        compiler_params=pltpu.CompilerParams(vmem_limit_bytes=24 * 1024 * 1024),
    )(*inputs)


def shards(checkpoint, porosity, deposit_weight, solid_mask, surface_mask):
    stream, span = lax.axis_size("stream"), lax.axis_size("span")
    tile = (8, 128)
    block, half = (21, 4) + tile, (21, 2) + tile
    inputs = tuple(
        pltpu.with_memory_space_constraint(value, pltpu.HBM)
        for value in (checkpoint, porosity, deposit_weight, solid_mask, surface_mask)
    )
    own, mine = call(
        start_kernel,
        inputs,
        [block, half],
        [pltpu.VMEM(value.shape, value.dtype) for value in inputs]
        + [pltpu.SemaphoreType.DMA((5,))],
        pltpu.HBM,
    )
    cores = [[i, i + 1] for i in range(0, span, 2)]
    chips = [(i, (i + 1) % span) for i in range(1, span, 2)]
    came = lax.ppermute(mine, "span", chips + [(b, a) for a, b in chips])
    both = lax.all_gather(own, "span", axis_index_groups=cores)
    rows = (19, 2, 2) + tile
    message = (TILES,) + tile
    side, state, following, up, down = call(
        inner_kernel, (own, both, came), [block, rows, rows, message, message]
    )
    low = lax.ppermute(up, "stream", [(i, i + 1) for i in range(stream - 1)])
    high = lax.ppermute(down, "stream", [(i + 1, i) for i in range(stream - 1)])
    scratch = [(19, 4, 2), (19, 4, 2), (2, 4, 2), (2, 4, 2), (19, 6, 2), (4, 8, 2)]
    adjoint, sensitivity = call(
        last_kernel,
        (checkpoint, solid_mask, surface_mask, own, side, state, following, low, high),
        [(19, 4) + tile, (4,) + tile],
        [pltpu.VMEM(shape + tile, jnp.float32) for shape in scratch],
    )
    return (adjoint, sensitivity)


def solution(mesh):
    placed = (
        P(None, "stream", "span", None),
        P("stream", "span", None),
        P("stream", "span", None),
        P("stream", "span", None),
        P("stream", "span", None),
    )
    return jax.shard_map(
        shards,
        mesh=mesh,
        in_specs=placed,
        out_specs=(P(None, "stream", "span", None), P("stream", "span", None)),
        check_vma=False,
    )
```

```python
import functools

import jax
import jax.numpy as jnp
import numpy as np
from jax import lax
from jax.experimental import pallas as pl
from jax.experimental.pallas import tpu as pltpu
from jax.sharding import PartitionSpec as P

VELOCITY = np.array(
    [
        [0, 0, 0],
        [1, 0, 0],
        [-1, 0, 0],
        [0, 1, 0],
        [0, -1, 0],
        [0, 0, 1],
        [0, 0, -1],
        [1, 1, 0],
        [-1, -1, 0],
        [1, -1, 0],
        [-1, 1, 0],
        [1, 0, 1],
        [-1, 0, -1],
        [1, 0, -1],
        [-1, 0, 1],
        [0, 1, 1],
        [0, -1, -1],
        [0, 1, -1],
        [0, -1, 1],
    ]
)
WEIGHTS = np.array([1.0 / 3.0] + [1.0 / 18.0] * 6 + [1.0 / 36.0] * 12)
GHOST_DENSITY = 18.0
INFLOW_SPEED = 0.08
GHOST_STATE = (
    WEIGHTS
    * GHOST_DENSITY
    * (
        1.0
        + 3.0 * VELOCITY[:, 0] * INFLOW_SPEED
        + 4.5 * (VELOCITY[:, 0] * INFLOW_SPEED) ** 2
        - 1.5 * INFLOW_SPEED**2
    )
)
GHOST = [float(value) for value in GHOST_STATE]
VEL = [tuple(int(part) for part in row) for row in VELOCITY]
CX = [row[0] for row in VEL]
UP = [p for p in range(19) if CX[p] == 1]
DOWN = [p for p in range(19) if CX[p] == -1]
FLAT = [p for p in range(19) if CX[p] == 0]
LEFT = [p for p in range(19) if VEL[p][1] == -1]
RIGHT = [p for p in range(19) if VEL[p][1] == 1]
ALONG = [p for p in range(19) if VEL[p][1] == 0]
OPP = [0] + [p + 1 if p % 2 else p - 1 for p in range(1, 19)]
BLEND, WEIGHT = 19, 20
SPAN_WIDE = 15
SPAN_TILES = 2 * SPAN_WIDE + 6
STATE, MOMENTS, NEAR_BLEND, WIDE = 0, 5, 9, 10
SUM_FAR, SUM_NEAR, SUM_OWN, WEIGHT_FAR, WEIGHT_NEAR, LAYERS = 10, 14, 18, 21, 22, 23
TILES = LAYERS + WIDE + (LAYERS - WIDE + 1) // 2


def sublane(tile):
    return lax.broadcasted_iota(jnp.int32, tile.shape, len(tile.shape) - 2)


def lane(tile):
    return lax.broadcasted_iota(jnp.int32, tile.shape, len(tile.shape) - 1)


def shift_z(tile, step, fill):
    if step == 0:
        return tile
    rolled = pltpu.roll(tile, step % 128, 1)
    return jnp.where(lane(tile) == (0 if step == 1 else 127), fill, rolled)


def shift_y(pair, step):
    if step == 0:
        return pair
    own, side = (pltpu.roll(tile, step % 8, 0) for tile in pair)
    edge = sublane(own) == (0 if step == 1 else 7)
    return (jnp.where(edge, side, own), jnp.where(edge, own, side))


def shift_pair(pair, stepy, stepz, fill):
    return tuple(shift_z(tile, stepz, fill) for tile in shift_y(pair, stepy))


def pairs_of(f):
    sums = [f[2 * i + 1] + f[2 * i + 2] for i in range(9)]
    diffs = [f[2 * i + 1] - f[2 * i + 2] for i in range(9)]
    return sums, diffs


def along_axes(v):
    return (
        v[0] + v[3] + v[4] + v[5] + v[6],
        v[1] + v[3] - v[4] + v[7] + v[8],
        v[2] + v[5] - v[6] + v[7] - v[8],
    )


def dots(u):
    x, y, z = u
    return [x, y, z, x + y, x - y, x + z, x - z, y + z, y - z]


def flow(f0, sums, diffs):
    density = f0 + sum(sums[1:], sums[0])
    inverse = 1.0 / density
    u = [m * inverse for m in along_axes(diffs)]
    square = u[0] * u[0] + u[1] * u[1] + u[2] * u[2]
    return density, u, square


def collide(f, b):
    sums, diffs = pairs_of(f)
    density, u, square = flow(f[0], sums, diffs)
    keep = 1.0 - b
    j = 0.1 * keep
    alpha, beta = 0.5 * (j + b), 0.5 * (j - b)
    scaled = (0.9 * keep) * density
    rest = scaled * (1.0 - 1.5 * square)
    flux = dots([scaled * part for part in u])
    out = [(j + b) * f[0] + (1.0 / 3.0) * rest]
    rest_axis, rest_diag = rest * (1.0 / 18.0), rest * (1.0 / 36.0)
    for i, along in enumerate(dots(u)):
        w = 1.0 / 18.0 if i < 3 else 1.0 / 36.0
        even = alpha * sums[i] + (rest_axis if i < 3 else rest_diag) + flux[i] * along * (4.5 * w)
        odd = beta * diffs[i] + flux[i] * (3.0 * w)
        out += [even + odd, even - odd]
    return out


def adjoint_values(u, square, b, h, wanted):
    s, d = pairs_of(h)
    w = [1.0 / 18.0] * 3 + [1.0 / 36.0] * 6
    t = [s[i] * w[i] for i in range(9)]
    h0 = h[0] * (1.0 / 3.0) + sum(t[1:], t[0])
    h1 = along_axes([d[i] * w[i] for i in range(9)])
    xx = t[0] + t[3] + t[4] + t[5] + t[6]
    yy = t[1] + t[3] + t[4] + t[7] + t[8]
    zz = t[2] + t[5] + t[6] + t[7] + t[8]
    xy, xz, yz = t[3] - t[4], t[5] - t[6], t[7] - t[8]
    v = (
        xx * u[0] + xy * u[1] + xz * u[2],
        xy * u[0] + yy * u[1] + yz * u[2],
        xz * u[0] + yz * u[1] + zz * u[2],
    )
    quad = u[0] * v[0] + u[1] * v[1] + u[2] * v[2]
    keep = 1.0 - b
    j, k = 0.1 * keep, 0.9 * keep
    alpha, beta = 0.5 * (j + b), 0.5 * (j - b)
    base = k * (h0 * (1.0 + 1.5 * square) - 4.5 * quad)
    push = dots([k * (3.0 * h1[i] + 9.0 * v[i] - 3.0 * u[i] * h0) for i in range(3)])
    out = {}
    if 0 in wanted:
        out[0] = (j + b) * h[0] + base
    for i in range(9):
        first, second = 2 * i + 1, 2 * i + 2
        if first in wanted or second in wanted:
            even = alpha * s[i] + base
            odd = beta * d[i] + push[i]
            if first in wanted:
                out[first] = even + odd
            if second in wanted:
                out[second] = even - odd
    return out, s, d, h0, h1, quad


def adjoint_collide(f, b, h, wanted, blend_part):
    fsums, fdiffs = pairs_of(f)
    density, u, square = flow(f[0], fsums, fdiffs)
    out, s, d, h0, h1, quad = adjoint_values(u, square, b, h, wanted)
    part = None
    if blend_part:
        equil = h0 * (1.0 - 1.5 * square) + 4.5 * quad
        equil = equil + 3.0 * (u[0] * h1[0] + u[1] * h1[1] + u[2] * h1[2])
        evens = sum((s[i] * fsums[i] for i in range(1, 9)), s[0] * fsums[0])
        odds = sum((d[i] * fdiffs[i] for i in range(1, 9)), d[0] * fdiffs[0])
        part = 0.9 * h[0] * f[0] + 0.45 * evens - 0.55 * odds - 0.9 * density * equil
    return out, part


def moment_sums(values):
    density = functools.reduce(lambda a, b: a + b, values.values())
    momentum = []
    for k in range(3):
        total = None
        for p, value in values.items():
            if VEL[p][k] == 1:
                total = value if total is None else total + value
        for p, value in values.items():
            if VEL[p][k] == -1:
                total = -value if total is None else total - value
        momentum.append(total)
    return [density] + momentum


def add(*totals):
    return [functools.reduce(lambda a, b: a + b, parts) for parts in zip(*totals)]


def put_message(ref, layers):
    for i, pair in enumerate(layers):
        ref[i] = pair[0]
    for i in range(WIDE):
        ref[LAYERS + i] = layers[i][1]
    for i in range(WIDE, LAYERS, 2):
        tile = layers[i][1]
        if i + 1 < LAYERS:
            at = sublane(tile)
            tile = jnp.where((at < 2) | (at > 5), tile, pltpu.roll(layers[i + 1][1], 4, 0))
        ref[LAYERS + WIDE + (i - WIDE) // 2] = tile


def get_message(read, i):
    if i < WIDE:
        return (read(i), read(LAYERS + i))
    tile = read(LAYERS + WIDE + (i - WIDE) // 2)
    return (read(i), pltpu.roll(tile, 4, 0) if (i - WIDE) % 2 else tile)


def wide_layers(core):
    towards = [jnp.where(core == 0, a, b) for a, b in zip(LEFT, RIGHT)]
    return towards + ALONG + [BLEND]


def narrow_layers(core):
    return [jnp.where(core == 0, b, a) for a, b in zip(LEFT, RIGHT)] + [WEIGHT]


def start_kernel(
    f_hbm, porosity_hbm, weight_hbm, solid_hbm, surface_hbm, own_ref, half_ref,
    f_ref, porosity_ref, weight_ref, solid_ref, surface_ref, sems,
):
    copies = [
        pltpu.make_async_copy(source, target, sems.at[i])
        for i, (source, target) in enumerate(
            (
                (solid_hbm, solid_ref),
                (surface_hbm, surface_ref),
                (porosity_hbm, porosity_ref),
                (weight_hbm, weight_ref),
                (f_hbm, f_ref),
            )
        )
    ]
    for copy in copies:
        copy.start()
    for copy in copies:
        copy.wait()
    core = lax.rem(lax.axis_index("span"), 2)
    for x in range(4):
        porosity = porosity_ref[x]
        blend = jnp.where(
            solid_ref[x] == 1, 1.0, jnp.where(surface_ref[x] == 1, porosity, 0.0)
        )
        out = collide([f_ref[p, x] for p in range(19)], blend)
        for p in range(19):
            own_ref[p, x] = out[p]
        own_ref[BLEND, x] = blend
        own_ref[WEIGHT, x] = weight_ref[x]
    at = sublane(own_ref[0, 0])
    low = (at < 4) == (core == 0)
    for i, layer in enumerate(wide_layers(core)):
        for pair in range(2):
            first, second = own_ref[layer, 2 * pair], own_ref[layer, 2 * pair + 1]
            half_ref[2 * i + pair] = jnp.where(low, first, pltpu.roll(second, 4, 0))
    for i, layer in enumerate(narrow_layers(core)):
        tile = own_ref[layer, 0]
        for x in range(1, 4):
            here = lax.rem(at + 8 - 2 * x + 2 * core, 8) < 2
            tile = jnp.where(here, pltpu.roll(own_ref[layer, x], 2 * x, 0), tile)
        half_ref[2 * SPAN_WIDE + i] = tile


def inner_kernel(
    own_ref, both_ref, half_ref, side_ref, state_ref, next_ref, odd_ref, even_ref, message_ref
):
    core = lax.rem(lax.axis_index("span"), 2)
    odd = lax.rem(lax.axis_index("stream"), 2)
    low = (sublane(half_ref[0]) < 4) == (core == 0)
    for i, layer in enumerate(wide_layers(1 - core)):
        for x in range(4):
            tile = half_ref[2 * i + x // 2]
            tile = pltpu.roll(tile, 4, 0) if x % 2 else tile
            side_ref[layer, x] = jnp.where(low, both_ref[1 - core, layer, x], tile)
    for i, layer in enumerate(narrow_layers(1 - core)):
        for x in range(4):
            tile = half_ref[2 * SPAN_WIDE + i]
            tile = pltpu.roll(tile, 8 - 2 * x, 0) if x else tile
            side_ref[layer, x] = jnp.where(low, both_ref[1 - core, layer, x], tile)

    def c0(p, x):
        return (own_ref[p, x], side_ref[p, x])

    def moved(p, pair):
        return shift_pair(pair, VEL[p][1], VEL[p][2], GHOST[p])

    for x in (1, 2):
        f = [moved(p, c0(p, x - CX[p])) for p in range(19)]
        blend = c0(BLEND, x)
        for t in range(2):
            tiles = [f[p][t] for p in range(19)]
            out = collide(tiles, blend[t])
            for p in range(19):
                state_ref[p, x - 1, t] = tiles[p]
                next_ref[p, x - 1, t] = out[p]

    def c1(p, x):
        return (next_ref[p, x - 1, 0], next_ref[p, x - 1, 1])

    for side, near, far, inward, outward in ((0, 3, 2, UP, DOWN), (1, 0, 1, DOWN, UP)):
        step = far - near
        enter = [moved(p, c0(p, near)) for p in inward]
        known = {p: moved(p, c0(p, near if p in FLAT else far)) for p in inward + FLAT}
        blend = c0(BLEND, near)
        j = [0.1 * (1.0 - part) for part in blend]
        layers = [None] * LAYERS
        layers[STATE : STATE + 5] = enter
        halves = [moment_sums({p: known[p][t] for p in known}) for t in range(2)]
        layers[MOMENTS : MOMENTS + 4] = list(zip(*halves))
        layers[NEAR_BLEND] = blend
        came = {p: moved(p, c1(p, far + step)) for p in inward}
        came.update({p: moved(p, c1(p, far)) for p in FLAT})
        for p in outward:
            came[p] = moved(p, tuple(blend[t] * known[OPP[p]][t] for t in range(2)))
        halves = [moment_sums({p: came[p][t] for p in came}) for t in range(2)]
        layers[SUM_FAR : SUM_FAR + 4] = list(zip(*halves))
        came = {p: moved(p, c1(p, far)) for p in inward}
        for p in FLAT:
            came[p] = moved(
                p,
                tuple(j[t] * known[p][t] + blend[t] * known[OPP[p]][t] for t in range(2)),
            )
        halves = [moment_sums({p: came[p][t] for p in came}) for t in range(2)]
        layers[SUM_NEAR : SUM_NEAR + 4] = list(zip(*halves))
        came = {p: moved(p, tuple(j[t] * known[p][t] for t in range(2))) for p in inward}
        halves = [moment_sums({p: came[p][t] for p in came}) for t in range(2)]
        halves = [[half[0], half[2], half[3]] for half in halves]
        layers[SUM_OWN : SUM_OWN + 3] = list(zip(*halves))
        layers[WEIGHT_FAR] = c0(WEIGHT, far)
        layers[WEIGHT_NEAR] = c0(WEIGHT, near)
        put_message(message_ref.at[side], layers)
    for i in range(TILES):
        odd_ref[i] = message_ref[1 - odd, i]
        even_ref[i] = message_ref[odd, i]


def last_kernel(
    f_ref, solid_ref, surface_ref, own_ref, side_ref, state_ref, next_ref, odd_ref, even_ref,
    adjoint_ref, sensitivity_ref, s1_ref, c1_ref, sum_ref, flow_ref, a1_ref, field_ref,
):
    place = lax.axis_index("stream")
    at_start = place == 0
    at_end = place == lax.axis_size("stream") - 1
    odd = lax.rem(place, 2)

    def low(i):
        return jnp.where(odd == 1, even_ref[1 - odd, i], odd_ref[i])

    def high(i):
        return jnp.where(odd == 1, odd_ref[i], even_ref[1 - odd, i])

    ends = (
        (low, at_start, 0, -1, UP, DOWN),
        (high, at_end, 3, 1, DOWN, UP),
    )

    def moved(p, pair, fill=None):
        return shift_pair(pair, VEL[p][1], VEL[p][2], GHOST[p] if fill is None else fill)

    def c0(p, x):
        return (own_ref[p, x], side_ref[p, x])

    for x in (1, 2):
        for p in range(19):
            for t in range(2):
                s1_ref[p, x, t] = state_ref[p, x - 1, t]
                c1_ref[p, x, t] = next_ref[p, x - 1, t]
    for read, end, x, out, inward, outward in ends:
        f = {p: moved(p, c0(p, x if p in FLAT else x - out)) for p in FLAT + outward}
        for i, p in enumerate(inward):
            f[p] = tuple(
                jnp.where(end, GHOST[p], part) for part in get_message(read, STATE + i)
            )
        blend = c0(BLEND, x)
        for t in range(2):
            tiles = [f[p][t] for p in range(19)]
            after = collide(tiles, blend[t])
            for p in range(19):
                s1_ref[p, x, t] = tiles[p]
                c1_ref[p, x, t] = after[p]

    def c1(p, x):
        return (c1_ref[p, x, 0], c1_ref[p, x, 1])

    def save_field(x, t, total, weight, end=None):
        inverse = 1.0 / total[0]
        u = [total[i] * inverse for i in range(1, 4)]
        kinetic = 0.5 * (u[0] * u[0] + u[1] * u[1] + u[2] * u[2])
        for i, value in enumerate(u + [kinetic]):
            value = weight * value
            field_ref[i, x + 2, t] = value if end is None else jnp.where(end, 0.0, value)

    for side, (read, end, x, out, inward, outward) in enumerate(ends):
        sent = [get_message(read, i) for i in range(LAYERS)]
        blend = sent[NEAR_BLEND]
        leaving = {p: moved(p, c0(p, x)) for p in outward}
        to_far, to_near, to_own = {}, {}, {}
        for t in range(2):
            total = add(
                moment_sums({p: leaving[p][t] for p in outward}),
                [sent[MOMENTS + i][t] for i in range(4)],
            )
            density = total[0]
            inverse = 1.0 / density
            u = [part * inverse for part in total[1:]]
            square = u[0] * u[0] + u[1] * u[1] + u[2] * u[2]
            for i, value in enumerate(u + [square]):
                flow_ref[side, i, t] = value
            keep = 1.0 - blend[t]
            scaled = (0.9 * keep) * density
            rest = scaled * (1.0 - 1.5 * square)
            along = dots(u)
            for p in range(19):
                value = float(WEIGHTS[p]) * rest
                if p:
                    cu = along[(p - 1) // 2]
                    flux = scaled * cu
                    value = value + flux * cu * float(4.5 * WEIGHTS[p])
                    value = value + flux * float((3.0 if p % 2 else -3.0) * WEIGHTS[p])
                if p in outward:
                    to_far.setdefault(p, []).append(value + 0.1 * keep * leaving[p][t])
                elif p in inward:
                    to_own.setdefault(p, []).append(value + blend[t] * leaving[OPP[p]][t])
                else:
                    to_near.setdefault(p, []).append(value)
        to_far = {p: moved(p, tuple(pair), 0.0) for p, pair in to_far.items()}
        to_near = {p: moved(p, tuple(pair), 0.0) for p, pair in to_near.items()}
        to_own = {p: moved(p, tuple(pair), 0.0) for p, pair in to_own.items()}
        back = {p: moved(p, c1(p, x)) for p in outward}
        for t in range(2):
            total = add(
                moment_sums({p: to_far[p][t] for p in to_far}),
                [sent[SUM_FAR + i][t] for i in range(4)],
            )
            save_field(x + 2 * out, t, total, sent[WEIGHT_FAR][t], end)
            near = dict(to_near)
            near.update(back)
            total = add(
                moment_sums({p: near[p][t] for p in near}),
                [sent[SUM_NEAR + i][t] for i in range(4)],
            )
            save_field(x + out, t, total, sent[WEIGHT_NEAR][t], end)
            own = moment_sums({p: to_own[p][t] for p in to_own})
            ready = [sent[SUM_OWN + i][t] for i in range(3)]
            own = add(own, [ready[0], -out * ready[0], ready[1], ready[2]])
            ghost = moment_sums({p: GHOST[p] for p in inward})
            for i in range(4):
                sum_ref[side, i, t] = jnp.where(end, ghost[i], own[i])

    for x in range(4):
        pops, given = list(range(19)), None
        if x == 0:
            pops, given = FLAT + DOWN, 0
        if x == 3:
            pops, given = FLAT + UP, 1
        came = {p: moved(p, c1(p, x - CX[p])) for p in pops}
        weight = c0(WEIGHT, x)
        for t in range(2):
            total = moment_sums({p: came[p][t] for p in came})
            if given is not None:
                total = add(total, [sum_ref[given, i, t] for i in range(4)])
            save_field(x, t, total, weight[t])

    def cotangent(p, x):
        pair = []
        for t in range(2):
            value = -field_ref[3, x + CX[p] + 2, t]
            for k in range(3):
                if VEL[p][k] == 1:
                    value = value + field_ref[k, x + CX[p] + 2, t]
                if VEL[p][k] == -1:
                    value = value - field_ref[k, x + CX[p] + 2, t]
            pair.append(value)
        return shift_pair(tuple(pair), -VEL[p][1], -VEL[p][2], 0.0)

    for x in range(4):
        h = [cotangent(p, x) for p in range(19)]
        blend = c0(BLEND, x)
        for t in range(2):
            wanted = [p for p in range(19) if t == 0 or VEL[p][1] != 0]
            out, part = adjoint_collide(
                [s1_ref[p, x, t] for p in range(19)],
                blend[t],
                [h[p][t] for p in range(19)],
                wanted,
                t == 0,
            )
            for p, value in out.items():
                a1_ref[p, x + 1, t] = value
            if part is not None:
                sensitivity_ref[x] = part
    for side, (read, end, x, out, inward, outward) in enumerate(ends):
        h = [cotangent(p, x + out) for p in range(19)]
        blend = get_message(read, NEAR_BLEND)
        for t in range(2):
            u = [flow_ref[side, i, t] for i in range(3)]
            wanted = [p for p in outward if t == 0 or VEL[p][1] != 0]
            got = adjoint_values(
                u, flow_ref[side, 3, t], blend[t], [h[p][t] for p in range(19)], wanted
            )[0]
            for p, value in got.items():
                a1_ref[p, x + out + 1, t] = jnp.where(end, 0.0, value)

    for x in range(4):
        h = []
        for p in range(19):
            at = x + CX[p] + 1
            tile = a1_ref[p, at, 0]
            if VEL[p][1]:
                tile = shift_y((tile, a1_ref[p, at, 1]), -VEL[p][1])[0]
            h.append(shift_z(tile, -VEL[p][2], 0.0))
        out, part = adjoint_collide(
            [f_ref[p, x] for p in range(19)], own_ref[BLEND, x], h, list(range(19)), True
        )
        for p in range(19):
            adjoint_ref[p, x] = out[p]
        design = (solid_ref[x] == 0) & (surface_ref[x] == 1)
        sensitivity_ref[x] = jnp.where(design, sensitivity_ref[x] + part, 0.0)


def call(kernel, inputs, shapes, scratch=(), space=pltpu.VMEM):
    return pl.pallas_call(
        kernel,
        out_shape=[jax.ShapeDtypeStruct(shape, jnp.float32) for shape in shapes],
        in_specs=[pl.BlockSpec(memory_space=space)] * len(inputs),
        out_specs=[pl.BlockSpec(memory_space=pltpu.VMEM)] * len(shapes),
        scratch_shapes=scratch,
        compiler_params=pltpu.CompilerParams(vmem_limit_bytes=24 * 1024 * 1024),
    )(*inputs)


def shards(checkpoint, porosity, deposit_weight, solid_mask, surface_mask):
    stream, span = lax.axis_size("stream"), lax.axis_size("span")
    tile = (8, 128)
    block, half = (21, 4) + tile, (SPAN_TILES,) + tile
    inputs = tuple(
        pltpu.with_memory_space_constraint(value, pltpu.HBM)
        for value in (checkpoint, porosity, deposit_weight, solid_mask, surface_mask)
    )
    own, mine = call(
        start_kernel,
        inputs,
        [block, half],
        [pltpu.VMEM(value.shape, value.dtype) for value in inputs]
        + [pltpu.SemaphoreType.DMA((5,))],
        pltpu.HBM,
    )
    cores = [[i, i + 1] for i in range(0, span, 2)]
    chips = [(i, (i + 1) % span) for i in range(1, span, 2)]
    came = lax.ppermute(mine, "span", chips + [(b, a) for a, b in chips])
    both = lax.all_gather(own, "span", axis_index_groups=cores)
    rows = (19, 2, 2) + tile
    message = (TILES,) + tile
    side, state, following, first, second = call(
        inner_kernel,
        (own, both, came),
        [block, rows, rows, message, message],
        [pltpu.VMEM((2,) + message, jnp.float32)],
    )

    pairs = [(i, i + 1) for i in range(1, stream - 1, 2)]
    odd = lax.ppermute(first, "stream", pairs + [(b, a) for a, b in pairs])
    even = lax.all_gather(
        second, "stream", axis_index_groups=[[i, i + 1] for i in range(0, stream, 2)]
    )
    scratch = [(19, 4, 2), (19, 4, 2), (2, 4, 2), (2, 4, 2), (19, 6, 2), (4, 8, 2)]
    adjoint, sensitivity = call(
        last_kernel,
        (checkpoint, solid_mask, surface_mask, own, side, state, following, odd, even),
        [(19, 4) + tile, (4,) + tile],
        [pltpu.VMEM(shape + tile, jnp.float32) for shape in scratch],
    )
    return (adjoint, sensitivity)


def solution(mesh):
    placed = (
        P(None, "stream", "span", None),
        P("stream", "span", None),
        P("stream", "span", None),
        P("stream", "span", None),
        P("stream", "span", None),
    )
    return jax.shard_map(
        shards,
        mesh=mesh,
        in_specs=placed,
        out_specs=(P(None, "stream", "span", None), P("stream", "span", None)),
        check_vma=False,
    )
```

```python
import functools

import jax
import jax.numpy as jnp
import numpy as np
from jax import lax
from jax.experimental import pallas as pl
from jax.experimental.pallas import tpu as pltpu
from jax.sharding import PartitionSpec as P

VELOCITY = np.array(
    [
        [0, 0, 0],
        [1, 0, 0],
        [-1, 0, 0],
        [0, 1, 0],
        [0, -1, 0],
        [0, 0, 1],
        [0, 0, -1],
        [1, 1, 0],
        [-1, -1, 0],
        [1, -1, 0],
        [-1, 1, 0],
        [1, 0, 1],
        [-1, 0, -1],
        [1, 0, -1],
        [-1, 0, 1],
        [0, 1, 1],
        [0, -1, -1],
        [0, 1, -1],
        [0, -1, 1],
    ]
)
WEIGHTS = np.array([1.0 / 3.0] + [1.0 / 18.0] * 6 + [1.0 / 36.0] * 12)
GHOST_DENSITY = 18.0
INFLOW_SPEED = 0.08
GHOST_STATE = (
    WEIGHTS
    * GHOST_DENSITY
    * (
        1.0
        + 3.0 * VELOCITY[:, 0] * INFLOW_SPEED
        + 4.5 * (VELOCITY[:, 0] * INFLOW_SPEED) ** 2
        - 1.5 * INFLOW_SPEED**2
    )
)
GHOST = [float(value) for value in GHOST_STATE]
VEL = [tuple(int(part) for part in row) for row in VELOCITY]
CX = [row[0] for row in VEL]
UP = [p for p in range(19) if CX[p] == 1]
DOWN = [p for p in range(19) if CX[p] == -1]
FLAT = [p for p in range(19) if CX[p] == 0]
LEFT = [p for p in range(19) if VEL[p][1] == -1]
RIGHT = [p for p in range(19) if VEL[p][1] == 1]
ALONG = [p for p in range(19) if VEL[p][1] == 0]
OPP = [0] + [p + 1 if p % 2 else p - 1 for p in range(1, 19)]
BLEND, WEIGHT = 19, 20
SPAN_WIDE = 15
SPAN_TILES = 2 * SPAN_WIDE + 6
STATE, MOMENTS, NEAR_BLEND, WIDE = 0, 5, 9, 10
SUM_FAR, SUM_NEAR, SUM_OWN, WEIGHT_FAR, WEIGHT_NEAR, LAYERS = 10, 14, 18, 21, 22, 23
INSET = WIDE // 2
TILES = LAYERS + WIDE + (LAYERS - WIDE - INSET + 1) // 2


def sublane(tile):
    return lax.broadcasted_iota(jnp.int32, tile.shape, len(tile.shape) - 2)


def lane(tile):
    return lax.broadcasted_iota(jnp.int32, tile.shape, len(tile.shape) - 1)


def shift_z(tile, step, fill):
    if step == 0:
        return tile
    rolled = pltpu.roll(tile, step % 128, 1)
    return jnp.where(lane(tile) == (0 if step == 1 else 127), fill, rolled)


def shift_y(pair, step):
    if step == 0:
        return pair
    own, side = (pltpu.roll(tile, step % 8, 0) for tile in pair)
    edge = sublane(own) == (0 if step == 1 else 7)
    return (jnp.where(edge, side, own), jnp.where(edge, own, side))


def shift_pair(pair, stepy, stepz, fill):
    return tuple(shift_z(tile, stepz, fill) for tile in shift_y(pair, stepy))


def pairs_of(f):
    sums = [f[2 * i + 1] + f[2 * i + 2] for i in range(9)]
    diffs = [f[2 * i + 1] - f[2 * i + 2] for i in range(9)]
    return sums, diffs


def along_axes(v):
    return (
        v[0] + v[3] + v[4] + v[5] + v[6],
        v[1] + v[3] - v[4] + v[7] + v[8],
        v[2] + v[5] - v[6] + v[7] - v[8],
    )


def dots(u):
    x, y, z = u
    return [x, y, z, x + y, x - y, x + z, x - z, y + z, y - z]


def flow(f0, sums, diffs):
    density = f0 + sum(sums[1:], sums[0])
    inverse = 1.0 / density
    u = [m * inverse for m in along_axes(diffs)]
    square = u[0] * u[0] + u[1] * u[1] + u[2] * u[2]
    return density, u, square


def collide(f, b):
    sums, diffs = pairs_of(f)
    density, u, square = flow(f[0], sums, diffs)
    keep = 1.0 - b
    j = 0.1 * keep
    alpha, beta = 0.5 * (j + b), 0.5 * (j - b)
    scaled = (0.9 * keep) * density
    rest = scaled * (1.0 - 1.5 * square)
    flux = dots([scaled * part for part in u])
    out = [(j + b) * f[0] + (1.0 / 3.0) * rest]
    rest_axis, rest_diag = rest * (1.0 / 18.0), rest * (1.0 / 36.0)
    for i, along in enumerate(dots(u)):
        w = 1.0 / 18.0 if i < 3 else 1.0 / 36.0
        even = alpha * sums[i] + (rest_axis if i < 3 else rest_diag) + flux[i] * along * (4.5 * w)
        odd = beta * diffs[i] + flux[i] * (3.0 * w)
        out += [even + odd, even - odd]
    return out


def adjoint_values(u, square, b, h, wanted):
    s, d = pairs_of(h)
    w = [1.0 / 18.0] * 3 + [1.0 / 36.0] * 6
    t = [s[i] * w[i] for i in range(9)]
    h0 = h[0] * (1.0 / 3.0) + sum(t[1:], t[0])
    h1 = along_axes([d[i] * w[i] for i in range(9)])
    xx = t[0] + t[3] + t[4] + t[5] + t[6]
    yy = t[1] + t[3] + t[4] + t[7] + t[8]
    zz = t[2] + t[5] + t[6] + t[7] + t[8]
    xy, xz, yz = t[3] - t[4], t[5] - t[6], t[7] - t[8]
    v = (
        xx * u[0] + xy * u[1] + xz * u[2],
        xy * u[0] + yy * u[1] + yz * u[2],
        xz * u[0] + yz * u[1] + zz * u[2],
    )
    quad = u[0] * v[0] + u[1] * v[1] + u[2] * v[2]
    keep = 1.0 - b
    j, k = 0.1 * keep, 0.9 * keep
    alpha, beta = 0.5 * (j + b), 0.5 * (j - b)
    base = k * (h0 * (1.0 + 1.5 * square) - 4.5 * quad)
    push = dots([k * (3.0 * h1[i] + 9.0 * v[i] - 3.0 * u[i] * h0) for i in range(3)])
    out = {}
    if 0 in wanted:
        out[0] = (j + b) * h[0] + base
    for i in range(9):
        first, second = 2 * i + 1, 2 * i + 2
        if first in wanted or second in wanted:
            even = alpha * s[i] + base
            odd = beta * d[i] + push[i]
            if first in wanted:
                out[first] = even + odd
            if second in wanted:
                out[second] = even - odd
    return out, s, d, h0, h1, quad


def adjoint_collide(f, b, h, wanted, blend_part):
    fsums, fdiffs = pairs_of(f)
    density, u, square = flow(f[0], fsums, fdiffs)
    out, s, d, h0, h1, quad = adjoint_values(u, square, b, h, wanted)
    part = None
    if blend_part:
        equil = h0 * (1.0 - 1.5 * square) + 4.5 * quad
        equil = equil + 3.0 * (u[0] * h1[0] + u[1] * h1[1] + u[2] * h1[2])
        evens = sum((s[i] * fsums[i] for i in range(1, 9)), s[0] * fsums[0])
        odds = sum((d[i] * fdiffs[i] for i in range(1, 9)), d[0] * fdiffs[0])
        part = 0.9 * h[0] * f[0] + 0.45 * evens - 0.55 * odds - 0.9 * density * equil
    return out, part


def moment_sums(values):
    density = functools.reduce(lambda a, b: a + b, values.values())
    momentum = []
    for k in range(3):
        total = None
        for p, value in values.items():
            if VEL[p][k] == 1:
                total = value if total is None else total + value
        for p, value in values.items():
            if VEL[p][k] == -1:
                total = -value if total is None else total - value
        momentum.append(total)
    return [density] + momentum


def add(*totals):
    return [functools.reduce(lambda a, b: a + b, parts) for parts in zip(*totals)]


def put_message(ref, layers):
    for i, pair in enumerate(layers):
        ref[i] = pair[0]
    at = sublane(layers[0][1])
    for i in range(WIDE):
        tile = layers[i][1]
        if i // 2 < INSET:
            inset = pltpu.roll(layers[WIDE + i // 2][1], 5 if i % 2 else 3, 0)
            tile = jnp.where((at == 3) | (at == 4), inset, tile)
        ref[LAYERS + i] = tile
    for i in range(WIDE + INSET, LAYERS, 2):
        tile = layers[i][1]
        if i + 1 < LAYERS:
            tile = jnp.where((at < 2) | (at > 5), tile, pltpu.roll(layers[i + 1][1], 4, 0))
        ref[LAYERS + WIDE + (i - WIDE - INSET) // 2] = tile


def get_message(read, i):
    if i < WIDE:
        return (read(i), read(LAYERS + i))
    if i < WIDE + INSET:
        first, second = (read(LAYERS + 2 * (i - WIDE) + k) for k in range(2))
        first, second = pltpu.roll(first, 5, 0), pltpu.roll(second, 3, 0)
        return (read(i), jnp.where(sublane(first) < 4, first, second))
    tile = read(LAYERS + WIDE + (i - WIDE - INSET) // 2)
    return (read(i), pltpu.roll(tile, 4, 0) if (i - WIDE - INSET) % 2 else tile)


def wide_layers(core):
    towards = [jnp.where(core == 0, a, b) for a, b in zip(LEFT, RIGHT)]
    return towards + ALONG + [BLEND]


def narrow_layers(core):
    return [jnp.where(core == 0, b, a) for a, b in zip(LEFT, RIGHT)] + [WEIGHT]


def start_kernel(
    f_hbm, porosity_hbm, weight_hbm, solid_hbm, surface_hbm, own_ref, half_ref,
    f_ref, porosity_ref, weight_ref, solid_ref, surface_ref, sems,
):
    small = [
        pltpu.make_async_copy(source, target, sems.at[i])
        for i, (source, target) in enumerate(
            (
                (solid_hbm, solid_ref),
                (surface_hbm, surface_ref),
                (porosity_hbm, porosity_ref),
                (weight_hbm, weight_ref),
            )
        )
    ]
    rows = [
        pltpu.make_async_copy(f_hbm.at[:, x], f_ref.at[:, x], sems.at[4 + x]) for x in range(4)
    ]
    for copy in rows[:1] + small + rows[1:]:
        copy.start()
    core = lax.rem(lax.axis_index("span"), 2)
    at = lax.broadcasted_iota(jnp.int32, (8, 128), 0)
    low = (at < 4) == (core == 0)
    for copy in small:
        copy.wait()
    for x in range(4):
        porosity = porosity_ref[x]
        blend = jnp.where(
            solid_ref[x] == 1, 1.0, jnp.where(surface_ref[x] == 1, porosity, 0.0)
        )
        rows[x].wait()
        out = collide([f_ref[p, x] for p in range(19)], blend)
        for p in range(19):
            own_ref[p, x] = out[p]
        own_ref[BLEND, x] = blend
        own_ref[WEIGHT, x] = weight_ref[x]
        if x % 2:
            for i, layer in enumerate(wide_layers(core)):
                first, second = own_ref[layer, x - 1], own_ref[layer, x]
                half_ref[2 * i + x // 2] = jnp.where(low, first, pltpu.roll(second, 4, 0))
    for i, layer in enumerate(narrow_layers(core)):
        tile = own_ref[layer, 0]
        for x in range(1, 4):
            here = lax.rem(at + 8 - 2 * x + 2 * core, 8) < 2
            tile = jnp.where(here, pltpu.roll(own_ref[layer, x], 2 * x, 0), tile)
        half_ref[2 * SPAN_WIDE + i] = tile


def inner_kernel(
    own_ref, both_ref, half_ref, side_ref, state_ref, next_ref, odd_ref, even_ref, message_ref
):
    core = lax.rem(lax.axis_index("span"), 2)
    odd = lax.rem(lax.axis_index("stream"), 2)
    low = (sublane(half_ref[0]) < 4) == (core == 0)
    for i, layer in enumerate(wide_layers(1 - core)):
        for x in range(4):
            tile = half_ref[2 * i + x // 2]
            tile = pltpu.roll(tile, 4, 0) if x % 2 else tile
            side_ref[layer, x] = jnp.where(low, both_ref[1 - core, layer, x], tile)
    for i, layer in enumerate(narrow_layers(1 - core)):
        for x in range(4):
            tile = half_ref[2 * SPAN_WIDE + i]
            tile = pltpu.roll(tile, 8 - 2 * x, 0) if x else tile
            side_ref[layer, x] = jnp.where(low, both_ref[1 - core, layer, x], tile)

    def c0(p, x):
        return (own_ref[p, x], side_ref[p, x])

    def moved(p, pair):
        return shift_pair(pair, VEL[p][1], VEL[p][2], GHOST[p])

    for x in (1, 2):
        f = [moved(p, c0(p, x - CX[p])) for p in range(19)]
        blend = c0(BLEND, x)
        for t in range(2):
            tiles = [f[p][t] for p in range(19)]
            out = collide(tiles, blend[t])
            for p in range(19):
                state_ref[p, x - 1, t] = tiles[p]
                next_ref[p, x - 1, t] = out[p]

    def c1(p, x):
        return (next_ref[p, x - 1, 0], next_ref[p, x - 1, 1])

    for side, near, far, inward, outward in ((0, 3, 2, UP, DOWN), (1, 0, 1, DOWN, UP)):
        step = far - near
        enter = [moved(p, c0(p, near)) for p in inward]
        known = {p: moved(p, c0(p, near if p in FLAT else far)) for p in inward + FLAT}
        blend = c0(BLEND, near)
        j = [0.1 * (1.0 - part) for part in blend]
        layers = [None] * LAYERS
        layers[STATE : STATE + 5] = enter
        halves = [moment_sums({p: known[p][t] for p in known}) for t in range(2)]
        layers[MOMENTS : MOMENTS + 4] = list(zip(*halves))
        layers[NEAR_BLEND] = blend
        came = {p: moved(p, c1(p, far + step)) for p in inward}
        came.update({p: moved(p, c1(p, far)) for p in FLAT})
        for p in outward:
            came[p] = moved(p, tuple(blend[t] * known[OPP[p]][t] for t in range(2)))
        halves = [moment_sums({p: came[p][t] for p in came}) for t in range(2)]
        layers[SUM_FAR : SUM_FAR + 4] = list(zip(*halves))
        came = {p: moved(p, c1(p, far)) for p in inward}
        for p in FLAT:
            came[p] = moved(
                p,
                tuple(j[t] * known[p][t] + blend[t] * known[OPP[p]][t] for t in range(2)),
            )
        halves = [moment_sums({p: came[p][t] for p in came}) for t in range(2)]
        layers[SUM_NEAR : SUM_NEAR + 4] = list(zip(*halves))
        came = {p: moved(p, tuple(j[t] * known[p][t] for t in range(2))) for p in inward}
        halves = [moment_sums({p: came[p][t] for p in came}) for t in range(2)]
        halves = [[half[0], half[2], half[3]] for half in halves]
        layers[SUM_OWN : SUM_OWN + 3] = list(zip(*halves))
        layers[WEIGHT_FAR] = c0(WEIGHT, far)
        layers[WEIGHT_NEAR] = c0(WEIGHT, near)
        put_message(message_ref.at[side], layers)
    for i in range(TILES):
        odd_ref[i] = message_ref[1 - odd, i]
        even_ref[i] = message_ref[odd, i]


def last_kernel(
    f_ref, solid_ref, surface_ref, own_ref, side_ref, state_ref, next_ref, odd_ref, even_ref,
    adjoint_hbm, sensitivity_hbm, adjoint_ref, sensitivity_ref,
    s1_ref, c1_ref, sum_ref, flow_ref, a1_ref, field_ref, sems,
):
    place = lax.axis_index("stream")
    at_start = place == 0
    at_end = place == lax.axis_size("stream") - 1
    odd = lax.rem(place, 2)

    def low(i):
        return jnp.where(odd == 1, even_ref[1 - odd, i], odd_ref[i])

    def high(i):
        return jnp.where(odd == 1, odd_ref[i], even_ref[1 - odd, i])

    ends = (
        (low, at_start, 0, -1, UP, DOWN),
        (high, at_end, 3, 1, DOWN, UP),
    )

    def moved(p, pair, fill=None):
        return shift_pair(pair, VEL[p][1], VEL[p][2], GHOST[p] if fill is None else fill)

    def c0(p, x):
        return (own_ref[p, x], side_ref[p, x])

    for read, end, x, out, inward, outward in ends:
        f = {p: moved(p, c0(p, x if p in FLAT else x - out)) for p in FLAT + outward}
        for i, p in enumerate(inward):
            f[p] = tuple(
                jnp.where(end, GHOST[p], part) for part in get_message(read, STATE + i)
            )
        blend = c0(BLEND, x)
        for t in range(2):
            tiles = [f[p][t] for p in range(19)]
            after = collide(tiles, blend[t])
            for p in range(19):
                s1_ref[p, x // 3, t] = tiles[p]
                c1_ref[p, x // 3, t] = after[p]

    def s1(p, x, t):
        return state_ref[p, x - 1, t] if x in (1, 2) else s1_ref[p, x // 3, t]

    def c1(p, x):
        ref, at = (next_ref, x - 1) if x in (1, 2) else (c1_ref, x // 3)
        return (ref[p, at, 0], ref[p, at, 1])

    def save_field(x, t, total, weight, end=None):
        inverse = 1.0 / total[0]
        u = [total[i] * inverse for i in range(1, 4)]
        kinetic = 0.5 * (u[0] * u[0] + u[1] * u[1] + u[2] * u[2])
        for i, value in enumerate(u + [kinetic]):
            value = weight * value
            field_ref[i, x + 2, t] = value if end is None else jnp.where(end, 0.0, value)

    for side, (read, end, x, out, inward, outward) in enumerate(ends):
        sent = [get_message(read, i) for i in range(LAYERS)]
        blend = sent[NEAR_BLEND]
        leaving = {p: moved(p, c0(p, x)) for p in outward}
        to_far, to_near, to_own = {}, {}, {}
        for t in range(2):
            total = add(
                moment_sums({p: leaving[p][t] for p in outward}),
                [sent[MOMENTS + i][t] for i in range(4)],
            )
            density = total[0]
            inverse = 1.0 / density
            u = [part * inverse for part in total[1:]]
            square = u[0] * u[0] + u[1] * u[1] + u[2] * u[2]
            for i, value in enumerate(u + [square]):
                flow_ref[side, i, t] = value
            keep = 1.0 - blend[t]
            scaled = (0.9 * keep) * density
            rest = scaled * (1.0 - 1.5 * square)
            along = dots(u)
            for p in range(19):
                value = float(WEIGHTS[p]) * rest
                if p:
                    cu = along[(p - 1) // 2]
                    flux = scaled * cu
                    value = value + flux * cu * float(4.5 * WEIGHTS[p])
                    value = value + flux * float((3.0 if p % 2 else -3.0) * WEIGHTS[p])
                if p in outward:
                    to_far.setdefault(p, []).append(value + 0.1 * keep * leaving[p][t])
                elif p in inward:
                    to_own.setdefault(p, []).append(value + blend[t] * leaving[OPP[p]][t])
                else:
                    to_near.setdefault(p, []).append(value)
        to_far = {p: moved(p, tuple(pair), 0.0) for p, pair in to_far.items()}
        to_near = {p: moved(p, tuple(pair), 0.0) for p, pair in to_near.items()}
        to_own = {p: moved(p, tuple(pair), 0.0) for p, pair in to_own.items()}
        back = {p: moved(p, c1(p, x)) for p in outward}
        for t in range(2):
            total = add(
                moment_sums({p: to_far[p][t] for p in to_far}),
                [sent[SUM_FAR + i][t] for i in range(4)],
            )
            save_field(x + 2 * out, t, total, sent[WEIGHT_FAR][t], end)
            near = dict(to_near)
            near.update(back)
            total = add(
                moment_sums({p: near[p][t] for p in near}),
                [sent[SUM_NEAR + i][t] for i in range(4)],
            )
            save_field(x + out, t, total, sent[WEIGHT_NEAR][t], end)
            own = moment_sums({p: to_own[p][t] for p in to_own})
            ready = [sent[SUM_OWN + i][t] for i in range(3)]
            own = add(own, [ready[0], -out * ready[0], ready[1], ready[2]])
            ghost = moment_sums({p: GHOST[p] for p in inward})
            for i in range(4):
                sum_ref[side, i, t] = jnp.where(end, ghost[i], own[i])

    for x in range(4):
        pops, given = list(range(19)), None
        if x == 0:
            pops, given = FLAT + DOWN, 0
        if x == 3:
            pops, given = FLAT + UP, 1
        came = {p: moved(p, c1(p, x - CX[p])) for p in pops}
        weight = c0(WEIGHT, x)
        for t in range(2):
            total = moment_sums({p: came[p][t] for p in came})
            if given is not None:
                total = add(total, [sum_ref[given, i, t] for i in range(4)])
            save_field(x, t, total, weight[t])

    def cotangent(p, x):
        pair = []
        for t in range(2):
            value = -field_ref[3, x + CX[p] + 2, t]
            for k in range(3):
                if VEL[p][k] == 1:
                    value = value + field_ref[k, x + CX[p] + 2, t]
                if VEL[p][k] == -1:
                    value = value - field_ref[k, x + CX[p] + 2, t]
            pair.append(value)
        return shift_pair(tuple(pair), -VEL[p][1], -VEL[p][2], 0.0)

    for x in range(4):
        h = [cotangent(p, x) for p in range(19)]
        blend = c0(BLEND, x)
        for t in range(2):
            wanted = [p for p in range(19) if t == 0 or VEL[p][1] != 0]
            out, part = adjoint_collide(
                [s1(p, x, t) for p in range(19)],
                blend[t],
                [h[p][t] for p in range(19)],
                wanted,
                t == 0,
            )
            for p, value in out.items():
                a1_ref[p, x + 1, t] = value
            if part is not None:
                sensitivity_ref[x] = part
    for side, (read, end, x, out, inward, outward) in enumerate(ends):
        h = [cotangent(p, x + out) for p in range(19)]
        blend = get_message(read, NEAR_BLEND)
        for t in range(2):
            u = [flow_ref[side, i, t] for i in range(3)]
            wanted = [p for p in outward if t == 0 or VEL[p][1] != 0]
            got = adjoint_values(
                u, flow_ref[side, 3, t], blend[t], [h[p][t] for p in range(19)], wanted
            )[0]
            for p, value in got.items():
                a1_ref[p, x + out + 1, t] = jnp.where(end, 0.0, value)

    sent = []
    for x in range(4):
        h = []
        for p in range(19):
            at = x + CX[p] + 1
            tile = a1_ref[p, at, 0]
            if VEL[p][1]:
                tile = shift_y((tile, a1_ref[p, at, 1]), -VEL[p][1])[0]
            h.append(shift_z(tile, -VEL[p][2], 0.0))
        out, part = adjoint_collide(
            [f_ref[p, x] for p in range(19)], own_ref[BLEND, x], h, list(range(19)), True
        )
        for p in range(19):
            adjoint_ref[p, x] = out[p]
        sent.append(
            pltpu.make_async_copy(adjoint_ref.at[:, x], adjoint_hbm.at[:, x], sems.at[x])
        )
        sent[x].start()
        design = (solid_ref[x] == 0) & (surface_ref[x] == 1)
        sensitivity_ref[x] = jnp.where(design, sensitivity_ref[x] + part, 0.0)
    sent.append(pltpu.make_async_copy(sensitivity_ref, sensitivity_hbm, sems.at[4]))
    sent[4].start()
    for copy in sent:
        copy.wait()


def call(kernel, inputs, shapes, scratch=(), space=pltpu.VMEM, result=pltpu.VMEM):
    return pl.pallas_call(
        kernel,
        out_shape=[jax.ShapeDtypeStruct(shape, jnp.float32) for shape in shapes],
        in_specs=[pl.BlockSpec(memory_space=space)] * len(inputs),
        out_specs=[pl.BlockSpec(memory_space=result)] * len(shapes),
        scratch_shapes=scratch,
        compiler_params=pltpu.CompilerParams(vmem_limit_bytes=24 * 1024 * 1024),
    )(*inputs)


def shards(checkpoint, porosity, deposit_weight, solid_mask, surface_mask):
    stream, span = lax.axis_size("stream"), lax.axis_size("span")
    tile = (8, 128)
    block, half = (21, 4) + tile, (SPAN_TILES,) + tile
    inputs = tuple(
        pltpu.with_memory_space_constraint(value, pltpu.HBM)
        for value in (checkpoint, porosity, deposit_weight, solid_mask, surface_mask)
    )
    own, mine = call(
        start_kernel,
        inputs,
        [block, half],
        [pltpu.VMEM(value.shape, value.dtype) for value in inputs]
        + [pltpu.SemaphoreType.DMA((8,))],
        pltpu.HBM,
    )
    cores = [[i, i + 1] for i in range(0, span, 2)]
    chips = [(i, (i + 1) % span) for i in range(1, span, 2)]
    came = lax.ppermute(mine, "span", chips + [(b, a) for a, b in chips])
    both = lax.all_gather(own, "span", axis_index_groups=cores)
    rows = (19, 2, 2) + tile
    message = (TILES,) + tile
    side, state, following, first, second = call(
        inner_kernel,
        (own, both, came),
        [block, rows, rows, message, message],
        [pltpu.VMEM((2,) + message, jnp.float32)],
    )

    pairs = [(i, i + 1) for i in range(1, stream - 1, 2)]
    odd = lax.ppermute(first, "stream", pairs + [(b, a) for a, b in pairs])
    even = lax.all_gather(
        second, "stream", axis_index_groups=[[i, i + 1] for i in range(0, stream, 2)]
    )
    scratch = [
        (19, 4), (4,), (19, 2, 2), (19, 2, 2), (2, 4, 2), (2, 4, 2), (19, 6, 2), (4, 8, 2),
    ]
    adjoint, sensitivity = call(
        last_kernel,
        (checkpoint, solid_mask, surface_mask, own, side, state, following, odd, even),
        [(19, 4) + tile, (4,) + tile],
        [pltpu.VMEM(shape + tile, jnp.float32) for shape in scratch]
        + [pltpu.SemaphoreType.DMA((5,))],
        result=pl.ANY,
    )
    return (adjoint, sensitivity)


def solution(mesh):
    placed = (
        P(None, "stream", "span", None),
        P("stream", "span", None),
        P("stream", "span", None),
        P("stream", "span", None),
        P("stream", "span", None),
    )
    return jax.shard_map(
        shards,
        mesh=mesh,
        in_specs=placed,
        out_specs=(P(None, "stream", "span", None), P("stream", "span", None)),
        check_vma=False,
    )
```

```python
import functools

import jax
import jax.numpy as jnp
import numpy as np
from jax import lax
from jax.experimental import pallas as pl
from jax.experimental.pallas import tpu as pltpu
from jax.sharding import PartitionSpec as P

VELOCITY = np.array(
    [
        [0, 0, 0],
        [1, 0, 0],
        [-1, 0, 0],
        [0, 1, 0],
        [0, -1, 0],
        [0, 0, 1],
        [0, 0, -1],
        [1, 1, 0],
        [-1, -1, 0],
        [1, -1, 0],
        [-1, 1, 0],
        [1, 0, 1],
        [-1, 0, -1],
        [1, 0, -1],
        [-1, 0, 1],
        [0, 1, 1],
        [0, -1, -1],
        [0, 1, -1],
        [0, -1, 1],
    ]
)
WEIGHTS = np.array([1.0 / 3.0] + [1.0 / 18.0] * 6 + [1.0 / 36.0] * 12)
GHOST_DENSITY = 18.0
INFLOW_SPEED = 0.08
GHOST_STATE = (
    WEIGHTS
    * GHOST_DENSITY
    * (
        1.0
        + 3.0 * VELOCITY[:, 0] * INFLOW_SPEED
        + 4.5 * (VELOCITY[:, 0] * INFLOW_SPEED) ** 2
        - 1.5 * INFLOW_SPEED**2
    )
)
GHOST = [float(value) for value in GHOST_STATE]
VEL = [tuple(int(part) for part in row) for row in VELOCITY]
CX = [row[0] for row in VEL]
UP = [p for p in range(19) if CX[p] == 1]
DOWN = [p for p in range(19) if CX[p] == -1]
FLAT = [p for p in range(19) if CX[p] == 0]
LEFT = [p for p in range(19) if VEL[p][1] == -1]
RIGHT = [p for p in range(19) if VEL[p][1] == 1]
ALONG = [p for p in range(19) if VEL[p][1] == 0]
OPP = [0] + [p + 1 if p % 2 else p - 1 for p in range(1, 19)]
BLEND, WEIGHT = 19, 20
SPAN_WIDE = 15
SPAN_TILES = 2 * SPAN_WIDE + 6
STATE, MOMENTS, NEAR_BLEND, WIDE = 0, 5, 9, 10
SUM_FAR, SUM_NEAR, SUM_OWN, WEIGHT_FAR, WEIGHT_NEAR, LAYERS = 10, 14, 18, 21, 22, 23
INSET = WIDE // 2
TILES = LAYERS + WIDE + (LAYERS - WIDE - INSET + 1) // 2


def sublane(tile):
    return lax.broadcasted_iota(jnp.int32, tile.shape, len(tile.shape) - 2)


def lane(tile):
    return lax.broadcasted_iota(jnp.int32, tile.shape, len(tile.shape) - 1)


def shift_z(tile, step, fill):
    if step == 0:
        return tile
    rolled = pltpu.roll(tile, step % 128, 1)
    return jnp.where(lane(tile) == (0 if step == 1 else 127), fill, rolled)


def shift_y(pair, step):
    if step == 0:
        return pair
    own, side = (pltpu.roll(tile, step % 8, 0) for tile in pair)
    edge = sublane(own) == (0 if step == 1 else 7)
    return (jnp.where(edge, side, own), jnp.where(edge, own, side))


def shift_pair(pair, stepy, stepz, fill):
    return tuple(shift_z(tile, stepz, fill) for tile in shift_y(pair, stepy))


def pairs_of(f):
    sums = [f[2 * i + 1] + f[2 * i + 2] for i in range(9)]
    diffs = [f[2 * i + 1] - f[2 * i + 2] for i in range(9)]
    return sums, diffs


def along_axes(v):
    return (
        v[0] + v[3] + v[4] + v[5] + v[6],
        v[1] + v[3] - v[4] + v[7] + v[8],
        v[2] + v[5] - v[6] + v[7] - v[8],
    )


def dots(u):
    x, y, z = u
    return [x, y, z, x + y, x - y, x + z, x - z, y + z, y - z]


def flow(f0, sums, diffs):
    density = f0 + sum(sums[1:], sums[0])
    inverse = 1.0 / density
    u = [m * inverse for m in along_axes(diffs)]
    square = u[0] * u[0] + u[1] * u[1] + u[2] * u[2]
    return density, u, square


def collide(f, b):
    sums, diffs = pairs_of(f)
    density, u, square = flow(f[0], sums, diffs)
    keep = 1.0 - b
    j = 0.1 * keep
    alpha, beta = 0.5 * (j + b), 0.5 * (j - b)
    scaled = (0.9 * keep) * density
    rest = scaled * (1.0 - 1.5 * square)
    flux = dots([scaled * part for part in u])
    out = [(j + b) * f[0] + (1.0 / 3.0) * rest]
    rest_axis, rest_diag = rest * (1.0 / 18.0), rest * (1.0 / 36.0)
    for i, along in enumerate(dots(u)):
        w = 1.0 / 18.0 if i < 3 else 1.0 / 36.0
        even = alpha * sums[i] + (rest_axis if i < 3 else rest_diag) + flux[i] * along * (4.5 * w)
        odd = beta * diffs[i] + flux[i] * (3.0 * w)
        out += [even + odd, even - odd]
    return out


def adjoint_values(u, square, b, h, wanted):
    s, d = pairs_of(h)
    w = [1.0 / 18.0] * 3 + [1.0 / 36.0] * 6
    t = [s[i] * w[i] for i in range(9)]
    h0 = h[0] * (1.0 / 3.0) + sum(t[1:], t[0])
    h1 = along_axes([d[i] * w[i] for i in range(9)])
    xx = t[0] + t[3] + t[4] + t[5] + t[6]
    yy = t[1] + t[3] + t[4] + t[7] + t[8]
    zz = t[2] + t[5] + t[6] + t[7] + t[8]
    xy, xz, yz = t[3] - t[4], t[5] - t[6], t[7] - t[8]
    v = (
        xx * u[0] + xy * u[1] + xz * u[2],
        xy * u[0] + yy * u[1] + yz * u[2],
        xz * u[0] + yz * u[1] + zz * u[2],
    )
    quad = u[0] * v[0] + u[1] * v[1] + u[2] * v[2]
    keep = 1.0 - b
    j, k = 0.1 * keep, 0.9 * keep
    alpha, beta = 0.5 * (j + b), 0.5 * (j - b)
    base = k * (h0 * (1.0 + 1.5 * square) - 4.5 * quad)
    push = dots([k * (3.0 * h1[i] + 9.0 * v[i] - 3.0 * u[i] * h0) for i in range(3)])
    out = {}
    if 0 in wanted:
        out[0] = (j + b) * h[0] + base
    for i in range(9):
        first, second = 2 * i + 1, 2 * i + 2
        if first in wanted or second in wanted:
            even = alpha * s[i] + base
            odd = beta * d[i] + push[i]
            if first in wanted:
                out[first] = even + odd
            if second in wanted:
                out[second] = even - odd
    return out, s, d, h0, h1, quad


def adjoint_collide(f, b, h, wanted, blend_part):
    fsums, fdiffs = pairs_of(f)
    density, u, square = flow(f[0], fsums, fdiffs)
    out, s, d, h0, h1, quad = adjoint_values(u, square, b, h, wanted)
    part = None
    if blend_part:
        equil = h0 * (1.0 - 1.5 * square) + 4.5 * quad
        equil = equil + 3.0 * (u[0] * h1[0] + u[1] * h1[1] + u[2] * h1[2])
        evens = sum((s[i] * fsums[i] for i in range(1, 9)), s[0] * fsums[0])
        odds = sum((d[i] * fdiffs[i] for i in range(1, 9)), d[0] * fdiffs[0])
        part = 0.9 * h[0] * f[0] + 0.45 * evens - 0.55 * odds - 0.9 * density * equil
    return out, part


def moment_sums(values):
    density = functools.reduce(lambda a, b: a + b, values.values())
    momentum = []
    for k in range(3):
        total = None
        for p, value in values.items():
            if VEL[p][k] == 1:
                total = value if total is None else total + value
        for p, value in values.items():
            if VEL[p][k] == -1:
                total = -value if total is None else total - value
        momentum.append(total)
    return [density] + momentum


def add(*totals):
    return [functools.reduce(lambda a, b: a + b, parts) for parts in zip(*totals)]


def put_message(ref, layers):
    for i, pair in enumerate(layers):
        ref[i] = pair[0]
    at = sublane(layers[0][1])
    for i in range(WIDE):
        tile = layers[i][1]
        if i // 2 < INSET:
            inset = pltpu.roll(layers[WIDE + i // 2][1], 5 if i % 2 else 3, 0)
            tile = jnp.where((at == 3) | (at == 4), inset, tile)
        ref[LAYERS + i] = tile
    for i in range(WIDE + INSET, LAYERS, 2):
        tile = layers[i][1]
        if i + 1 < LAYERS:
            tile = jnp.where((at < 2) | (at > 5), tile, pltpu.roll(layers[i + 1][1], 4, 0))
        ref[LAYERS + WIDE + (i - WIDE - INSET) // 2] = tile


def get_message(read, i):
    if i < WIDE:
        return (read(i), read(LAYERS + i))
    if i < WIDE + INSET:
        first, second = (read(LAYERS + 2 * (i - WIDE) + k) for k in range(2))
        first, second = pltpu.roll(first, 5, 0), pltpu.roll(second, 3, 0)
        return (read(i), jnp.where(sublane(first) < 4, first, second))
    tile = read(LAYERS + WIDE + (i - WIDE - INSET) // 2)
    return (read(i), pltpu.roll(tile, 4, 0) if (i - WIDE - INSET) % 2 else tile)


def turn_of(column):
    return min(column // 2, 1) if isinstance(column, int) else jnp.minimum(column // 2, 1)


def wide_layers(core):
    towards = [jnp.where(core == 0, a, b) for a, b in zip(LEFT, RIGHT)]
    return towards + ALONG + [BLEND]


def narrow_layers(core):
    return [jnp.where(core == 0, b, a) for a, b in zip(LEFT, RIGHT)] + [WEIGHT]


def start_kernel(
    f_hbm, porosity_hbm, weight_hbm, solid_hbm, surface_hbm, own_ref, half_ref,
    f_ref, porosity_ref, weight_ref, solid_ref, surface_ref, sems,
):
    small = [
        pltpu.make_async_copy(source, target, sems.at[i])
        for i, (source, target) in enumerate(
            (
                (solid_hbm, solid_ref),
                (surface_hbm, surface_ref),
                (porosity_hbm, porosity_ref),
                (weight_hbm, weight_ref),
            )
        )
    ]
    rows = [
        pltpu.make_async_copy(f_hbm.at[:, x], f_ref.at[:, x], sems.at[4 + x]) for x in range(4)
    ]
    for copy in rows[:1] + small + rows[1:]:
        copy.start()
    core = lax.rem(lax.axis_index("span"), 2)
    at = lax.broadcasted_iota(jnp.int32, (8, 128), 0)
    low = (at < 4) == (core == 0)
    for copy in small:
        copy.wait()
    for x in range(4):
        porosity = porosity_ref[x]
        blend = jnp.where(
            solid_ref[x] == 1, 1.0, jnp.where(surface_ref[x] == 1, porosity, 0.0)
        )
        rows[x].wait()
        out = collide([f_ref[p, x] for p in range(19)], blend)
        for p in range(19):
            own_ref[p, x] = out[p]
        own_ref[BLEND, x] = blend
        own_ref[WEIGHT, x] = weight_ref[x]
        if x % 2:
            for i, layer in enumerate(wide_layers(core)):
                first, second = own_ref[layer, x - 1], own_ref[layer, x]
                half_ref[2 * i + x // 2] = jnp.where(low, first, pltpu.roll(second, 4, 0))
    for i, layer in enumerate(narrow_layers(core)):
        tile = own_ref[layer, 0]
        for x in range(1, 4):
            here = lax.rem(at + 8 - 2 * x + 2 * core, 8) < 2
            tile = jnp.where(here, pltpu.roll(own_ref[layer, x], 2 * x, 0), tile)
        half_ref[2 * SPAN_WIDE + i] = tile


def inner_kernel(
    own_ref, both_ref, half_ref, side_ref, state_ref, next_ref, first_ref, second_ref, message_ref
):
    core = lax.rem(lax.axis_index("span"), 2)
    odd = lax.rem(lax.axis_index("stream"), 2)
    low = (sublane(half_ref[0]) < 4) == (core == 0)
    for i, layer in enumerate(wide_layers(1 - core)):
        for x in range(4):
            tile = half_ref[2 * i + x // 2]
            tile = pltpu.roll(tile, 4, 0) if x % 2 else tile
            side_ref[layer, x] = jnp.where(low, both_ref[1 - core, layer, x], tile)
    for i, layer in enumerate(narrow_layers(1 - core)):
        for x in range(4):
            tile = half_ref[2 * SPAN_WIDE + i]
            tile = pltpu.roll(tile, 8 - 2 * x, 0) if x else tile
            side_ref[layer, x] = jnp.where(low, both_ref[1 - core, layer, x], tile)

    def c0(p, x):
        return (own_ref[p, x], side_ref[p, x])

    def moved(p, pair):
        return shift_pair(pair, VEL[p][1], VEL[p][2], GHOST[p])

    for x in (1, 2):
        f = [moved(p, c0(p, x - CX[p])) for p in range(19)]
        blend = c0(BLEND, x)
        for t in range(2):
            tiles = [f[p][t] for p in range(19)]
            out = collide(tiles, blend[t])
            for p in range(19):
                state_ref[p, x - 1, t] = tiles[p]
                next_ref[p, x - 1, t] = out[p]

    def c1(p, x):
        return (next_ref[p, x - 1, 0], next_ref[p, x - 1, 1])

    for side, near, far, inward, outward in ((0, 3, 2, UP, DOWN), (1, 0, 1, DOWN, UP)):
        step = far - near
        enter = [moved(p, c0(p, near)) for p in inward]
        known = {p: moved(p, c0(p, near if p in FLAT else far)) for p in inward + FLAT}
        blend = c0(BLEND, near)
        j = [0.1 * (1.0 - part) for part in blend]
        layers = [None] * LAYERS
        layers[STATE : STATE + 5] = enter
        halves = [moment_sums({p: known[p][t] for p in known}) for t in range(2)]
        layers[MOMENTS : MOMENTS + 4] = list(zip(*halves))
        layers[NEAR_BLEND] = blend
        came = {p: moved(p, c1(p, far + step)) for p in inward}
        came.update({p: moved(p, c1(p, far)) for p in FLAT})
        for p in outward:
            came[p] = moved(p, tuple(blend[t] * known[OPP[p]][t] for t in range(2)))
        halves = [moment_sums({p: came[p][t] for p in came}) for t in range(2)]
        layers[SUM_FAR : SUM_FAR + 4] = list(zip(*halves))
        came = {p: moved(p, c1(p, far)) for p in inward}
        for p in FLAT:
            came[p] = moved(
                p,
                tuple(j[t] * known[p][t] + blend[t] * known[OPP[p]][t] for t in range(2)),
            )
        halves = [moment_sums({p: came[p][t] for p in came}) for t in range(2)]
        layers[SUM_NEAR : SUM_NEAR + 4] = list(zip(*halves))
        came = {p: moved(p, tuple(j[t] * known[p][t] for t in range(2))) for p in inward}
        halves = [moment_sums({p: came[p][t] for p in came}) for t in range(2)]
        halves = [[half[0], half[2], half[3]] for half in halves]
        layers[SUM_OWN : SUM_OWN + 3] = list(zip(*halves))
        layers[WEIGHT_FAR] = c0(WEIGHT, far)
        layers[WEIGHT_NEAR] = c0(WEIGHT, near)
        put_message(message_ref.at[side], layers)
    towards = lax.rem(1 - odd + turn_of(lax.axis_index("span")), 2)
    for i in range(TILES):
        first_ref[i] = message_ref[towards, i]
        second_ref[i] = message_ref[1 - towards, i]


def last_kernel(
    f_ref, solid_ref, surface_ref, own_ref, side_ref, state_ref, next_ref, one_ref, two_ref,
    adjoint_hbm, sensitivity_hbm, adjoint_ref, sensitivity_ref,
    s1_ref, c1_ref, sum_ref, flow_ref, a1_ref, field_ref, sems,
):
    place = lax.axis_index("stream")
    at_start = place == 0
    at_end = place == lax.axis_size("stream") - 1
    origin = lax.rem(1 - lax.rem(place, 2) + turn_of(lax.axis_index("span")), 2)

    def low(i):
        return jnp.where(origin == 1, one_ref[i], two_ref[origin, i])

    def high(i):
        return jnp.where(origin == 0, one_ref[i], two_ref[origin, i])

    ends = (
        (low, at_start, 0, -1, UP, DOWN),
        (high, at_end, 3, 1, DOWN, UP),
    )

    def moved(p, pair, fill=None):
        return shift_pair(pair, VEL[p][1], VEL[p][2], GHOST[p] if fill is None else fill)

    def c0(p, x):
        return (own_ref[p, x], side_ref[p, x])

    for read, end, x, out, inward, outward in ends:
        f = {p: moved(p, c0(p, x if p in FLAT else x - out)) for p in FLAT + outward}
        for i, p in enumerate(inward):
            f[p] = tuple(
                jnp.where(end, GHOST[p], part) for part in get_message(read, STATE + i)
            )
        blend = c0(BLEND, x)
        for t in range(2):
            tiles = [f[p][t] for p in range(19)]
            after = collide(tiles, blend[t])
            for p in range(19):
                s1_ref[p, x // 3, t] = tiles[p]
                c1_ref[p, x // 3, t] = after[p]

    def s1(p, x, t):
        return state_ref[p, x - 1, t] if x in (1, 2) else s1_ref[p, x // 3, t]

    def c1(p, x):
        ref, at = (next_ref, x - 1) if x in (1, 2) else (c1_ref, x // 3)
        return (ref[p, at, 0], ref[p, at, 1])

    def save_field(x, t, total, weight, end=None):
        inverse = 1.0 / total[0]
        u = [total[i] * inverse for i in range(1, 4)]
        kinetic = 0.5 * (u[0] * u[0] + u[1] * u[1] + u[2] * u[2])
        for i, value in enumerate(u + [kinetic]):
            value = weight * value
            field_ref[i, x + 2, t] = value if end is None else jnp.where(end, 0.0, value)

    for side, (read, end, x, out, inward, outward) in enumerate(ends):
        sent = [get_message(read, i) for i in range(LAYERS)]
        blend = sent[NEAR_BLEND]
        leaving = {p: moved(p, c0(p, x)) for p in outward}
        to_far, to_near, to_own = {}, {}, {}
        for t in range(2):
            total = add(
                moment_sums({p: leaving[p][t] for p in outward}),
                [sent[MOMENTS + i][t] for i in range(4)],
            )
            density = total[0]
            inverse = 1.0 / density
            u = [part * inverse for part in total[1:]]
            square = u[0] * u[0] + u[1] * u[1] + u[2] * u[2]
            for i, value in enumerate(u + [square]):
                flow_ref[side, i, t] = value
            keep = 1.0 - blend[t]
            scaled = (0.9 * keep) * density
            rest = scaled * (1.0 - 1.5 * square)
            along = dots(u)
            for p in range(19):
                value = float(WEIGHTS[p]) * rest
                if p:
                    cu = along[(p - 1) // 2]
                    flux = scaled * cu
                    value = value + flux * cu * float(4.5 * WEIGHTS[p])
                    value = value + flux * float((3.0 if p % 2 else -3.0) * WEIGHTS[p])
                if p in outward:
                    to_far.setdefault(p, []).append(value + 0.1 * keep * leaving[p][t])
                elif p in inward:
                    to_own.setdefault(p, []).append(value + blend[t] * leaving[OPP[p]][t])
                else:
                    to_near.setdefault(p, []).append(value)
        to_far = {p: moved(p, tuple(pair), 0.0) for p, pair in to_far.items()}
        to_near = {p: moved(p, tuple(pair), 0.0) for p, pair in to_near.items()}
        to_own = {p: moved(p, tuple(pair), 0.0) for p, pair in to_own.items()}
        back = {p: moved(p, c1(p, x)) for p in outward}
        for t in range(2):
            total = add(
                moment_sums({p: to_far[p][t] for p in to_far}),
                [sent[SUM_FAR + i][t] for i in range(4)],
            )
            save_field(x + 2 * out, t, total, sent[WEIGHT_FAR][t], end)
            near = dict(to_near)
            near.update(back)
            total = add(
                moment_sums({p: near[p][t] for p in near}),
                [sent[SUM_NEAR + i][t] for i in range(4)],
            )
            save_field(x + out, t, total, sent[WEIGHT_NEAR][t], end)
            own = moment_sums({p: to_own[p][t] for p in to_own})
            ready = [sent[SUM_OWN + i][t] for i in range(3)]
            own = add(own, [ready[0], -out * ready[0], ready[1], ready[2]])
            ghost = moment_sums({p: GHOST[p] for p in inward})
            for i in range(4):
                sum_ref[side, i, t] = jnp.where(end, ghost[i], own[i])

    for x in range(4):
        pops, given = list(range(19)), None
        if x == 0:
            pops, given = FLAT + DOWN, 0
        if x == 3:
            pops, given = FLAT + UP, 1
        came = {p: moved(p, c1(p, x - CX[p])) for p in pops}
        weight = c0(WEIGHT, x)
        for t in range(2):
            total = moment_sums({p: came[p][t] for p in came})
            if given is not None:
                total = add(total, [sum_ref[given, i, t] for i in range(4)])
            save_field(x, t, total, weight[t])

    def cotangent(p, x):
        pair = []
        for t in range(2):
            value = -field_ref[3, x + CX[p] + 2, t]
            for k in range(3):
                if VEL[p][k] == 1:
                    value = value + field_ref[k, x + CX[p] + 2, t]
                if VEL[p][k] == -1:
                    value = value - field_ref[k, x + CX[p] + 2, t]
            pair.append(value)
        return shift_pair(tuple(pair), -VEL[p][1], -VEL[p][2], 0.0)

    for x in range(4):
        h = [cotangent(p, x) for p in range(19)]
        blend = c0(BLEND, x)
        for t in range(2):
            wanted = [p for p in range(19) if t == 0 or VEL[p][1] != 0]
            out, part = adjoint_collide(
                [s1(p, x, t) for p in range(19)],
                blend[t],
                [h[p][t] for p in range(19)],
                wanted,
                t == 0,
            )
            for p, value in out.items():
                a1_ref[p, x + 1, t] = value
            if part is not None:
                sensitivity_ref[x] = part
    for side, (read, end, x, out, inward, outward) in enumerate(ends):
        h = [cotangent(p, x + out) for p in range(19)]
        blend = get_message(read, NEAR_BLEND)
        for t in range(2):
            u = [flow_ref[side, i, t] for i in range(3)]
            wanted = [p for p in outward if t == 0 or VEL[p][1] != 0]
            got = adjoint_values(
                u, flow_ref[side, 3, t], blend[t], [h[p][t] for p in range(19)], wanted
            )[0]
            for p, value in got.items():
                a1_ref[p, x + out + 1, t] = jnp.where(end, 0.0, value)

    sent = []
    for x in range(4):
        h = []
        for p in range(19):
            at = x + CX[p] + 1
            tile = a1_ref[p, at, 0]
            if VEL[p][1]:
                tile = shift_y((tile, a1_ref[p, at, 1]), -VEL[p][1])[0]
            h.append(shift_z(tile, -VEL[p][2], 0.0))
        out, part = adjoint_collide(
            [f_ref[p, x] for p in range(19)], own_ref[BLEND, x], h, list(range(19)), True
        )
        for p in range(19):
            adjoint_ref[p, x] = out[p]
        sent.append(
            pltpu.make_async_copy(adjoint_ref.at[:, x], adjoint_hbm.at[:, x], sems.at[x])
        )
        sent[x].start()
        design = (solid_ref[x] == 0) & (surface_ref[x] == 1)
        sensitivity_ref[x] = jnp.where(design, sensitivity_ref[x] + part, 0.0)
    sent.append(pltpu.make_async_copy(sensitivity_ref, sensitivity_hbm, sems.at[4]))
    sent[4].start()
    for copy in sent:
        copy.wait()


def call(kernel, inputs, shapes, scratch=(), space=pltpu.VMEM, result=pltpu.VMEM):
    return pl.pallas_call(
        kernel,
        out_shape=[jax.ShapeDtypeStruct(shape, jnp.float32) for shape in shapes],
        in_specs=[pl.BlockSpec(memory_space=space)] * len(inputs),
        out_specs=[pl.BlockSpec(memory_space=result)] * len(shapes),
        scratch_shapes=scratch,
        compiler_params=pltpu.CompilerParams(vmem_limit_bytes=24 * 1024 * 1024),
    )(*inputs)


def shards(checkpoint, porosity, deposit_weight, solid_mask, surface_mask):
    stream, span = lax.axis_size("stream"), lax.axis_size("span")
    tile = (8, 128)
    block, half = (21, 4) + tile, (SPAN_TILES,) + tile
    inputs = tuple(
        pltpu.with_memory_space_constraint(value, pltpu.HBM)
        for value in (checkpoint, porosity, deposit_weight, solid_mask, surface_mask)
    )
    own, mine = call(
        start_kernel,
        inputs,
        [block, half],
        [pltpu.VMEM(value.shape, value.dtype) for value in inputs]
        + [pltpu.SemaphoreType.DMA((8,))],
        pltpu.HBM,
    )
    cores = [[i, i + 1] for i in range(0, span, 2)]
    chips = [(i, (i + 1) % span) for i in range(1, span, 2)]
    came = lax.ppermute(mine, "span", chips + [(b, a) for a, b in chips])
    both = lax.all_gather(own, "span", axis_index_groups=cores)
    rows = (19, 2, 2) + tile
    message = (TILES,) + tile
    side, state, following, first, second = call(
        inner_kernel,
        (own, both, came),
        [block, rows, rows, message, message],
        [pltpu.VMEM((2,) + message, jnp.float32)],
    )

    swaps, groups = [], []
    for j in range(span):
        turn = turn_of(j)
        swaps += [(i * span + j, (i + 1) * span + j) for i in range(1 - turn, stream - 1, 2)]
        groups += [[i * span + j, (i + 1) * span + j] for i in range(turn, stream - 1, 2)]
        if turn and j % 2:
            groups += [[i * span + j - 1, i * span + j] for i in (0, stream - 1)]
    axes = ("stream", "span")
    one = lax.ppermute(first, axes, swaps + [(b, a) for a, b in swaps])
    two = lax.all_gather(second, axes, axis_index_groups=groups)
    scratch = [
        (19, 4), (4,), (19, 2, 2), (19, 2, 2), (2, 4, 2), (2, 4, 2), (19, 6, 2), (4, 8, 2),
    ]
    adjoint, sensitivity = call(
        last_kernel,
        (checkpoint, solid_mask, surface_mask, own, side, state, following, one, two),
        [(19, 4) + tile, (4,) + tile],
        [pltpu.VMEM(shape + tile, jnp.float32) for shape in scratch]
        + [pltpu.SemaphoreType.DMA((5,))],
        result=pl.ANY,
    )
    return (adjoint, sensitivity)


def solution(mesh):
    placed = (
        P(None, "stream", "span", None),
        P("stream", "span", None),
        P("stream", "span", None),
        P("stream", "span", None),
        P("stream", "span", None),
    )
    return jax.shard_map(
        shards,
        mesh=mesh,
        in_specs=placed,
        out_specs=(P(None, "stream", "span", None), P("stream", "span", None)),
        check_vma=False,
    )
```

```python
import functools

import jax
import jax.numpy as jnp
import numpy as np
from jax import lax
from jax.experimental import pallas as pl
from jax.experimental.pallas import tpu as pltpu
from jax.sharding import PartitionSpec as P

VELOCITY = np.array(
    [
        [0, 0, 0],
        [1, 0, 0],
        [-1, 0, 0],
        [0, 1, 0],
        [0, -1, 0],
        [0, 0, 1],
        [0, 0, -1],
        [1, 1, 0],
        [-1, -1, 0],
        [1, -1, 0],
        [-1, 1, 0],
        [1, 0, 1],
        [-1, 0, -1],
        [1, 0, -1],
        [-1, 0, 1],
        [0, 1, 1],
        [0, -1, -1],
        [0, 1, -1],
        [0, -1, 1],
    ]
)
WEIGHTS = np.array([1.0 / 3.0] + [1.0 / 18.0] * 6 + [1.0 / 36.0] * 12)
GHOST_DENSITY = 18.0
INFLOW_SPEED = 0.08
GHOST_STATE = (
    WEIGHTS
    * GHOST_DENSITY
    * (
        1.0
        + 3.0 * VELOCITY[:, 0] * INFLOW_SPEED
        + 4.5 * (VELOCITY[:, 0] * INFLOW_SPEED) ** 2
        - 1.5 * INFLOW_SPEED**2
    )
)
GHOST = [float(value) for value in GHOST_STATE]
VEL = [tuple(int(part) for part in row) for row in VELOCITY]
CX = [row[0] for row in VEL]
UP = [p for p in range(19) if CX[p] == 1]
DOWN = [p for p in range(19) if CX[p] == -1]
FLAT = [p for p in range(19) if CX[p] == 0]
LEFT = [p for p in range(19) if VEL[p][1] == -1]
RIGHT = [p for p in range(19) if VEL[p][1] == 1]
ALONG = [p for p in range(19) if VEL[p][1] == 0]
OPP = [0] + [p + 1 if p % 2 else p - 1 for p in range(1, 19)]
BLEND, WEIGHT = 19, 20
SPAN_WIDE, SPAN_FREE = 15, 5
SPAN_TILES = 2 * SPAN_WIDE + 1
STATE, MOMENTS, NEAR_BLEND, WIDE = 0, 5, 9, 10
SUM_FAR, SUM_NEAR, SUM_OWN, WEIGHT_FAR, WEIGHT_NEAR, LAYERS = 10, 14, 18, 21, 22, 23
INSET = WIDE // 2
TILES = LAYERS + WIDE + (LAYERS - WIDE - INSET + 1) // 2


def sublane(tile):
    return lax.broadcasted_iota(jnp.int32, tile.shape, len(tile.shape) - 2)


def lane(tile):
    return lax.broadcasted_iota(jnp.int32, tile.shape, len(tile.shape) - 1)


def spin(tile, rows):
    return pltpu.roll(tile, rows % 8, 0) if rows % 8 else tile


def shift_z(tile, step, fill):
    if step == 0:
        return tile
    rolled = pltpu.roll(tile, step % 128, 1)
    return jnp.where(lane(tile) == (0 if step == 1 else 127), fill, rolled)


def shift_y(pair, step):
    if step == 0:
        return pair
    own, side = (pltpu.roll(tile, step % 8, 0) for tile in pair)
    edge = sublane(own) == (0 if step == 1 else 7)
    return (jnp.where(edge, side, own), jnp.where(edge, own, side))


def shift_pair(pair, stepy, stepz, fill):
    return tuple(shift_z(tile, stepz, fill) for tile in shift_y(pair, stepy))


def pairs_of(f):
    sums = [f[2 * i + 1] + f[2 * i + 2] for i in range(9)]
    diffs = [f[2 * i + 1] - f[2 * i + 2] for i in range(9)]
    return sums, diffs


def along_axes(v):
    return (
        v[0] + v[3] + v[4] + v[5] + v[6],
        v[1] + v[3] - v[4] + v[7] + v[8],
        v[2] + v[5] - v[6] + v[7] - v[8],
    )


def dots(u):
    x, y, z = u
    return [x, y, z, x + y, x - y, x + z, x - z, y + z, y - z]


def flow(f0, sums, diffs):
    density = f0 + sum(sums[1:], sums[0])
    inverse = 1.0 / density
    u = [m * inverse for m in along_axes(diffs)]
    square = u[0] * u[0] + u[1] * u[1] + u[2] * u[2]
    return density, u, square


def collide(f, b):
    sums, diffs = pairs_of(f)
    density, u, square = flow(f[0], sums, diffs)
    keep = 1.0 - b
    j = 0.1 * keep
    alpha, beta = 0.5 * (j + b), 0.5 * (j - b)
    scaled = (0.9 * keep) * density
    rest = scaled * (1.0 - 1.5 * square)
    flux = dots([scaled * part for part in u])
    out = [(j + b) * f[0] + (1.0 / 3.0) * rest]
    rest_axis, rest_diag = rest * (1.0 / 18.0), rest * (1.0 / 36.0)
    for i, along in enumerate(dots(u)):
        w = 1.0 / 18.0 if i < 3 else 1.0 / 36.0
        even = alpha * sums[i] + (rest_axis if i < 3 else rest_diag) + flux[i] * along * (4.5 * w)
        odd = beta * diffs[i] + flux[i] * (3.0 * w)
        out += [even + odd, even - odd]
    return out


def adjoint_values(u, square, b, h, wanted):
    s, d = pairs_of(h)
    w = [1.0 / 18.0] * 3 + [1.0 / 36.0] * 6
    t = [s[i] * w[i] for i in range(9)]
    h0 = h[0] * (1.0 / 3.0) + sum(t[1:], t[0])
    h1 = along_axes([d[i] * w[i] for i in range(9)])
    xx = t[0] + t[3] + t[4] + t[5] + t[6]
    yy = t[1] + t[3] + t[4] + t[7] + t[8]
    zz = t[2] + t[5] + t[6] + t[7] + t[8]
    xy, xz, yz = t[3] - t[4], t[5] - t[6], t[7] - t[8]
    v = (
        xx * u[0] + xy * u[1] + xz * u[2],
        xy * u[0] + yy * u[1] + yz * u[2],
        xz * u[0] + yz * u[1] + zz * u[2],
    )
    quad = u[0] * v[0] + u[1] * v[1] + u[2] * v[2]
    keep = 1.0 - b
    j, k = 0.1 * keep, 0.9 * keep
    alpha, beta = 0.5 * (j + b), 0.5 * (j - b)
    base = k * (h0 * (1.0 + 1.5 * square) - 4.5 * quad)
    push = dots([k * (3.0 * h1[i] + 9.0 * v[i] - 3.0 * u[i] * h0) for i in range(3)])
    out = {}
    if 0 in wanted:
        out[0] = (j + b) * h[0] + base
    for i in range(9):
        first, second = 2 * i + 1, 2 * i + 2
        if first in wanted or second in wanted:
            even = alpha * s[i] + base
            odd = beta * d[i] + push[i]
            if first in wanted:
                out[first] = even + odd
            if second in wanted:
                out[second] = even - odd
    return out, s, d, h0, h1, quad


def adjoint_collide(f, b, h, wanted, blend_part):
    fsums, fdiffs = pairs_of(f)
    density, u, square = flow(f[0], fsums, fdiffs)
    out, s, d, h0, h1, quad = adjoint_values(u, square, b, h, wanted)
    part = None
    if blend_part:
        equil = h0 * (1.0 - 1.5 * square) + 4.5 * quad
        equil = equil + 3.0 * (u[0] * h1[0] + u[1] * h1[1] + u[2] * h1[2])
        evens = sum((s[i] * fsums[i] for i in range(1, 9)), s[0] * fsums[0])
        odds = sum((d[i] * fdiffs[i] for i in range(1, 9)), d[0] * fdiffs[0])
        part = 0.9 * h[0] * f[0] + 0.45 * evens - 0.55 * odds - 0.9 * density * equil
    return out, part


def moment_sums(values):
    density = functools.reduce(lambda a, b: a + b, values.values())
    momentum = []
    for k in range(3):
        total = None
        for p, value in values.items():
            if VEL[p][k] == 1:
                total = value if total is None else total + value
        for p, value in values.items():
            if VEL[p][k] == -1:
                total = -value if total is None else total - value
        momentum.append(total)
    return [density] + momentum


def add(*totals):
    return [functools.reduce(lambda a, b: a + b, parts) for parts in zip(*totals)]


def put_message(ref, layers):
    for i, pair in enumerate(layers):
        ref[i] = pair[0]
    at = sublane(layers[0][1])
    for i in range(WIDE):
        tile = layers[i][1]
        if i // 2 < INSET:
            inset = pltpu.roll(layers[WIDE + i // 2][1], 5 if i % 2 else 3, 0)
            tile = jnp.where((at == 3) | (at == 4), inset, tile)
        ref[LAYERS + i] = tile
    for i in range(WIDE + INSET, LAYERS, 2):
        tile = layers[i][1]
        if i + 1 < LAYERS:
            tile = jnp.where((at < 2) | (at > 5), tile, pltpu.roll(layers[i + 1][1], 4, 0))
        ref[LAYERS + WIDE + (i - WIDE - INSET) // 2] = tile


def get_message(read, i):
    if i < WIDE:
        return (read(i), read(LAYERS + i))
    if i < WIDE + INSET:
        first, second = (read(LAYERS + 2 * (i - WIDE) + k) for k in range(2))
        first, second = pltpu.roll(first, 5, 0), pltpu.roll(second, 3, 0)
        return (read(i), jnp.where(sublane(first) < 4, first, second))
    tile = read(LAYERS + WIDE + (i - WIDE - INSET) // 2)
    return (read(i), pltpu.roll(tile, 4, 0) if (i - WIDE - INSET) % 2 else tile)


def turn_of(column):
    return min(column // 2, 1) if isinstance(column, int) else jnp.minimum(column // 2, 1)


def wide_layers(core):
    towards = [jnp.where(core == 0, a, b) for a, b in zip(LEFT, RIGHT)]
    return towards + ALONG + [BLEND]


def narrow_layers(core):
    return [jnp.where(core == 0, b, a) for a, b in zip(LEFT, RIGHT)] + [WEIGHT]


def start_kernel(
    f_hbm, porosity_hbm, weight_hbm, solid_hbm, surface_hbm, own_ref, half_ref,
    f_ref, porosity_ref, weight_ref, solid_ref, surface_ref, sems,
):
    small = [
        pltpu.make_async_copy(source, target, sems.at[i])
        for i, (source, target) in enumerate(
            (
                (solid_hbm, solid_ref),
                (surface_hbm, surface_ref),
                (porosity_hbm, porosity_ref),
                (weight_hbm, weight_ref),
            )
        )
    ]
    rows = [
        pltpu.make_async_copy(f_hbm.at[:, x], f_ref.at[:, x], sems.at[4 + x]) for x in range(4)
    ]
    for copy in rows[:1] + small + rows[1:]:
        copy.start()
    core = lax.rem(lax.axis_index("span"), 2)
    at = lax.broadcasted_iota(jnp.int32, (8, 128), 0)
    low = (at < 4) == (core == 0)
    for copy in small:
        copy.wait()
    for x in range(4):
        porosity = porosity_ref[x]
        blend = jnp.where(
            solid_ref[x] == 1, 1.0, jnp.where(surface_ref[x] == 1, porosity, 0.0)
        )
        rows[x].wait()
        out = collide([f_ref[p, x] for p in range(19)], blend)
        for p in range(19):
            own_ref[p, x] = out[p]
        own_ref[BLEND, x] = blend
        own_ref[WEIGHT, x] = weight_ref[x]
        if x % 2:
            for i, layer in enumerate(wide_layers(core)):
                first, second = own_ref[layer, x - 1], own_ref[layer, x]
                half_ref[2 * i + x // 2] = jnp.where(low, first, pltpu.roll(second, 4, 0))
    for i, layer in enumerate(narrow_layers(core)):
        tile = own_ref[layer, 0]
        for x in range(1, 4):
            here = lax.rem(at + 8 - 2 * x + 2 * core, 8) < 2
            tile = jnp.where(here, pltpu.roll(own_ref[layer, x], 2 * x, 0), tile)
        if i == 5:
            half_ref[2 * SPAN_WIDE] = tile
            continue
        for k in range(4):
            slot = 2 * SPAN_FREE + 4 * i + k
            piece = jnp.where(core == 0, spin(tile, 3 - k), spin(tile, -k))
            free = lax.rem(at, 4) == 3 * (1 - core)
            half_ref[slot] = jnp.where(free, piece, half_ref[slot])


def inner_kernel(
    own_ref, both_ref, half_ref, side_ref, state_ref, next_ref, first_ref, second_ref, message_ref
):
    core = lax.rem(lax.axis_index("span"), 2)
    odd = lax.rem(lax.axis_index("stream"), 2)
    at = lax.broadcasted_iota(jnp.int32, (8, 128), 0)
    low = (at < 4) == (core == 0)
    for i, layer in enumerate(wide_layers(1 - core)):
        for x in range(4):
            tile = half_ref[2 * i + x // 2]
            tile = pltpu.roll(tile, 4, 0) if x % 2 else tile
            side_ref[layer, x] = jnp.where(low, both_ref[1 - core, layer, x], tile)
    for i, layer in enumerate(narrow_layers(1 - core)):
        rows = half_ref[2 * SPAN_WIDE]
        for k in range(4 if i < 5 else 0):
            piece = half_ref[2 * SPAN_FREE + 4 * i + k]
            piece = jnp.where(core == 1, spin(piece, k - 3), spin(piece, k))
            rows = jnp.where(lax.rem(at, 4) == k, piece, rows) if k else piece
        for x in range(4):
            side_ref[layer, x] = jnp.where(low, both_ref[1 - core, layer, x], spin(rows, -2 * x))

    def c0(p, x):
        return (own_ref[p, x], side_ref[p, x])

    def moved(p, pair):
        return shift_pair(pair, VEL[p][1], VEL[p][2], GHOST[p])

    for x in (1, 2):
        f = [moved(p, c0(p, x - CX[p])) for p in range(19)]
        blend = c0(BLEND, x)
        for t in range(2):
            tiles = [f[p][t] for p in range(19)]
            out = collide(tiles, blend[t])
            for p in range(19):
                state_ref[p, x - 1, t] = tiles[p]
                next_ref[p, x - 1, t] = out[p]

    def c1(p, x):
        return (next_ref[p, x - 1, 0], next_ref[p, x - 1, 1])

    for side, near, far, inward, outward in ((0, 3, 2, UP, DOWN), (1, 0, 1, DOWN, UP)):
        step = far - near
        enter = [moved(p, c0(p, near)) for p in inward]
        known = {p: moved(p, c0(p, near if p in FLAT else far)) for p in inward + FLAT}
        blend = c0(BLEND, near)
        j = [0.1 * (1.0 - part) for part in blend]
        layers = [None] * LAYERS
        layers[STATE : STATE + 5] = enter
        halves = [moment_sums({p: known[p][t] for p in known}) for t in range(2)]
        layers[MOMENTS : MOMENTS + 4] = list(zip(*halves))
        layers[NEAR_BLEND] = blend
        came = {p: moved(p, c1(p, far + step)) for p in inward}
        came.update({p: moved(p, c1(p, far)) for p in FLAT})
        for p in outward:
            came[p] = moved(p, tuple(blend[t] * known[OPP[p]][t] for t in range(2)))
        halves = [moment_sums({p: came[p][t] for p in came}) for t in range(2)]
        layers[SUM_FAR : SUM_FAR + 4] = list(zip(*halves))
        came = {p: moved(p, c1(p, far)) for p in inward}
        for p in FLAT:
            came[p] = moved(
                p,
                tuple(j[t] * known[p][t] + blend[t] * known[OPP[p]][t] for t in range(2)),
            )
        halves = [moment_sums({p: came[p][t] for p in came}) for t in range(2)]
        layers[SUM_NEAR : SUM_NEAR + 4] = list(zip(*halves))
        came = {p: moved(p, tuple(j[t] * known[p][t] for t in range(2))) for p in inward}
        halves = [moment_sums({p: came[p][t] for p in came}) for t in range(2)]
        halves = [[half[0], half[2], half[3]] for half in halves]
        layers[SUM_OWN : SUM_OWN + 3] = list(zip(*halves))
        layers[WEIGHT_FAR] = c0(WEIGHT, far)
        layers[WEIGHT_NEAR] = c0(WEIGHT, near)
        put_message(message_ref.at[side], layers)
    towards = lax.rem(1 - odd + turn_of(lax.axis_index("span")), 2)
    for i in range(TILES):
        first_ref[i] = message_ref[towards, i]
        second_ref[i] = message_ref[1 - towards, i]


def last_kernel(
    f_ref, solid_ref, surface_ref, own_ref, side_ref, state_ref, next_ref, one_ref, two_ref,
    adjoint_hbm, sensitivity_hbm, adjoint_ref, sensitivity_ref,
    s1_ref, c1_ref, sum_ref, flow_ref, a1_ref, field_ref, sems,
):
    place = lax.axis_index("stream")
    at_start = place == 0
    at_end = place == lax.axis_size("stream") - 1
    origin = lax.rem(1 - lax.rem(place, 2) + turn_of(lax.axis_index("span")), 2)

    def low(i):
        return jnp.where(origin == 1, one_ref[i], two_ref[origin, i])

    def high(i):
        return jnp.where(origin == 0, one_ref[i], two_ref[origin, i])

    ends = (
        (low, at_start, 0, -1, UP, DOWN),
        (high, at_end, 3, 1, DOWN, UP),
    )

    def moved(p, pair, fill=None):
        return shift_pair(pair, VEL[p][1], VEL[p][2], GHOST[p] if fill is None else fill)

    def c0(p, x):
        return (own_ref[p, x], side_ref[p, x])

    for read, end, x, out, inward, outward in ends:
        f = {p: moved(p, c0(p, x if p in FLAT else x - out)) for p in FLAT + outward}
        for i, p in enumerate(inward):
            f[p] = tuple(
                jnp.where(end, GHOST[p], part) for part in get_message(read, STATE + i)
            )
        blend = c0(BLEND, x)
        for t in range(2):
            tiles = [f[p][t] for p in range(19)]
            after = collide(tiles, blend[t])
            for p in range(19):
                s1_ref[p, x // 3, t] = tiles[p]
                c1_ref[p, x // 3, t] = after[p]

    def s1(p, x, t):
        return state_ref[p, x - 1, t] if x in (1, 2) else s1_ref[p, x // 3, t]

    def c1(p, x):
        ref, at = (next_ref, x - 1) if x in (1, 2) else (c1_ref, x // 3)
        return (ref[p, at, 0], ref[p, at, 1])

    def save_field(x, t, total, weight, end=None):
        inverse = 1.0 / total[0]
        u = [total[i] * inverse for i in range(1, 4)]
        kinetic = 0.5 * (u[0] * u[0] + u[1] * u[1] + u[2] * u[2])
        for i, value in enumerate(u + [kinetic]):
            value = weight * value
            field_ref[i, x + 2, t] = value if end is None else jnp.where(end, 0.0, value)

    for side, (read, end, x, out, inward, outward) in enumerate(ends):
        sent = [get_message(read, i) for i in range(LAYERS)]
        blend = sent[NEAR_BLEND]
        leaving = {p: moved(p, c0(p, x)) for p in outward}
        to_far, to_near, to_own = {}, {}, {}
        for t in range(2):
            total = add(
                moment_sums({p: leaving[p][t] for p in outward}),
                [sent[MOMENTS + i][t] for i in range(4)],
            )
            density = total[0]
            inverse = 1.0 / density
            u = [part * inverse for part in total[1:]]
            square = u[0] * u[0] + u[1] * u[1] + u[2] * u[2]
            for i, value in enumerate(u + [square]):
                flow_ref[side, i, t] = value
            keep = 1.0 - blend[t]
            scaled = (0.9 * keep) * density
            rest = scaled * (1.0 - 1.5 * square)
            along = dots(u)
            for p in range(19):
                value = float(WEIGHTS[p]) * rest
                if p:
                    cu = along[(p - 1) // 2]
                    flux = scaled * cu
                    value = value + flux * cu * float(4.5 * WEIGHTS[p])
                    value = value + flux * float((3.0 if p % 2 else -3.0) * WEIGHTS[p])
                if p in outward:
                    to_far.setdefault(p, []).append(value + 0.1 * keep * leaving[p][t])
                elif p in inward:
                    to_own.setdefault(p, []).append(value + blend[t] * leaving[OPP[p]][t])
                else:
                    to_near.setdefault(p, []).append(value)
        to_far = {p: moved(p, tuple(pair), 0.0) for p, pair in to_far.items()}
        to_near = {p: moved(p, tuple(pair), 0.0) for p, pair in to_near.items()}
        to_own = {p: moved(p, tuple(pair), 0.0) for p, pair in to_own.items()}
        back = {p: moved(p, c1(p, x)) for p in outward}
        for t in range(2):
            total = add(
                moment_sums({p: to_far[p][t] for p in to_far}),
                [sent[SUM_FAR + i][t] for i in range(4)],
            )
            save_field(x + 2 * out, t, total, sent[WEIGHT_FAR][t], end)
            near = dict(to_near)
            near.update(back)
            total = add(
                moment_sums({p: near[p][t] for p in near}),
                [sent[SUM_NEAR + i][t] for i in range(4)],
            )
            save_field(x + out, t, total, sent[WEIGHT_NEAR][t], end)
            own = moment_sums({p: to_own[p][t] for p in to_own})
            ready = [sent[SUM_OWN + i][t] for i in range(3)]
            own = add(own, [ready[0], -out * ready[0], ready[1], ready[2]])
            ghost = moment_sums({p: GHOST[p] for p in inward})
            for i in range(4):
                sum_ref[side, i, t] = jnp.where(end, ghost[i], own[i])

    for x in range(4):
        pops, given = list(range(19)), None
        if x == 0:
            pops, given = FLAT + DOWN, 0
        if x == 3:
            pops, given = FLAT + UP, 1
        came = {p: moved(p, c1(p, x - CX[p])) for p in pops}
        weight = c0(WEIGHT, x)
        for t in range(2):
            total = moment_sums({p: came[p][t] for p in came})
            if given is not None:
                total = add(total, [sum_ref[given, i, t] for i in range(4)])
            save_field(x, t, total, weight[t])

    def cotangent(p, x):
        pair = []
        for t in range(2):
            value = -field_ref[3, x + CX[p] + 2, t]
            for k in range(3):
                if VEL[p][k] == 1:
                    value = value + field_ref[k, x + CX[p] + 2, t]
                if VEL[p][k] == -1:
                    value = value - field_ref[k, x + CX[p] + 2, t]
            pair.append(value)
        return shift_pair(tuple(pair), -VEL[p][1], -VEL[p][2], 0.0)

    for x in range(4):
        h = [cotangent(p, x) for p in range(19)]
        blend = c0(BLEND, x)
        for t in range(2):
            wanted = [p for p in range(19) if t == 0 or VEL[p][1] != 0]
            out, part = adjoint_collide(
                [s1(p, x, t) for p in range(19)],
                blend[t],
                [h[p][t] for p in range(19)],
                wanted,
                t == 0,
            )
            for p, value in out.items():
                a1_ref[p, x + 1, t] = value
            if part is not None:
                sensitivity_ref[x] = part
    for side, (read, end, x, out, inward, outward) in enumerate(ends):
        h = [cotangent(p, x + out) for p in range(19)]
        blend = get_message(read, NEAR_BLEND)
        for t in range(2):
            u = [flow_ref[side, i, t] for i in range(3)]
            wanted = [p for p in outward if t == 0 or VEL[p][1] != 0]
            got = adjoint_values(
                u, flow_ref[side, 3, t], blend[t], [h[p][t] for p in range(19)], wanted
            )[0]
            for p, value in got.items():
                a1_ref[p, x + out + 1, t] = jnp.where(end, 0.0, value)

    sent = []
    for x in range(4):
        h = []
        for p in range(19):
            at = x + CX[p] + 1
            tile = a1_ref[p, at, 0]
            if VEL[p][1]:
                tile = shift_y((tile, a1_ref[p, at, 1]), -VEL[p][1])[0]
            h.append(shift_z(tile, -VEL[p][2], 0.0))
        out, part = adjoint_collide(
            [f_ref[p, x] for p in range(19)], own_ref[BLEND, x], h, list(range(19)), True
        )
        for p in range(19):
            adjoint_ref[p, x] = out[p]
        sent.append(
            pltpu.make_async_copy(adjoint_ref.at[:, x], adjoint_hbm.at[:, x], sems.at[x])
        )
        sent[x].start()
        design = (solid_ref[x] == 0) & (surface_ref[x] == 1)
        sensitivity_ref[x] = jnp.where(design, sensitivity_ref[x] + part, 0.0)
    sent.append(pltpu.make_async_copy(sensitivity_ref, sensitivity_hbm, sems.at[4]))
    sent[4].start()
    for copy in sent:
        copy.wait()


def call(kernel, inputs, shapes, scratch=(), space=pltpu.VMEM, result=pltpu.VMEM):
    return pl.pallas_call(
        kernel,
        out_shape=[jax.ShapeDtypeStruct(shape, jnp.float32) for shape in shapes],
        in_specs=[pl.BlockSpec(memory_space=space)] * len(inputs),
        out_specs=[pl.BlockSpec(memory_space=result)] * len(shapes),
        scratch_shapes=scratch,
        compiler_params=pltpu.CompilerParams(vmem_limit_bytes=24 * 1024 * 1024),
    )(*inputs)


def shards(checkpoint, porosity, deposit_weight, solid_mask, surface_mask):
    stream, span = lax.axis_size("stream"), lax.axis_size("span")
    tile = (8, 128)
    block, half = (21, 4) + tile, (SPAN_TILES,) + tile
    inputs = tuple(
        pltpu.with_memory_space_constraint(value, pltpu.HBM)
        for value in (checkpoint, porosity, deposit_weight, solid_mask, surface_mask)
    )
    own, mine = call(
        start_kernel,
        inputs,
        [block, half],
        [pltpu.VMEM(value.shape, value.dtype) for value in inputs]
        + [pltpu.SemaphoreType.DMA((8,))],
        pltpu.HBM,
    )
    cores = [[i, i + 1] for i in range(0, span, 2)]
    chips = [(i, (i + 1) % span) for i in range(1, span, 2)]
    came = lax.ppermute(mine, "span", chips + [(b, a) for a, b in chips])
    both = lax.all_gather(own, "span", axis_index_groups=cores)
    rows = (19, 2, 2) + tile
    message = (TILES,) + tile
    side, state, following, first, second = call(
        inner_kernel,
        (own, both, came),
        [block, rows, rows, message, message],
        [pltpu.VMEM((2,) + message, jnp.float32)],
    )

    swaps, groups = [], []
    for j in range(span):
        turn = turn_of(j)
        swaps += [(i * span + j, (i + 1) * span + j) for i in range(1 - turn, stream - 1, 2)]
        groups += [[i * span + j, (i + 1) * span + j] for i in range(turn, stream - 1, 2)]
        if turn and j % 2:
            groups += [[i * span + j - 1, i * span + j] for i in (0, stream - 1)]
    axes = ("stream", "span")
    one = lax.ppermute(first, axes, swaps + [(b, a) for a, b in swaps])
    two = lax.all_gather(second, axes, axis_index_groups=groups)
    scratch = [
        (19, 4), (4,), (19, 2, 2), (19, 2, 2), (2, 4, 2), (2, 4, 2), (19, 6, 2), (4, 8, 2),
    ]
    adjoint, sensitivity = call(
        last_kernel,
        (checkpoint, solid_mask, surface_mask, own, side, state, following, one, two),
        [(19, 4) + tile, (4,) + tile],
        [pltpu.VMEM(shape + tile, jnp.float32) for shape in scratch]
        + [pltpu.SemaphoreType.DMA((5,))],
        result=pl.ANY,
    )
    return (adjoint, sensitivity)


def solution(mesh):
    placed = (
        P(None, "stream", "span", None),
        P("stream", "span", None),
        P("stream", "span", None),
        P("stream", "span", None),
        P("stream", "span", None),
    )
    return jax.shard_map(
        shards,
        mesh=mesh,
        in_specs=placed,
        out_specs=(P(None, "stream", "span", None), P("stream", "span", None)),
        check_vma=False,
    )
```

```python
import functools

import jax
import jax.numpy as jnp
import numpy as np
from jax import lax
from jax.experimental import pallas as pl
from jax.experimental.pallas import tpu as pltpu
from jax.sharding import PartitionSpec as P

VELOCITY = np.array(
    [
        [0, 0, 0],
        [1, 0, 0],
        [-1, 0, 0],
        [0, 1, 0],
        [0, -1, 0],
        [0, 0, 1],
        [0, 0, -1],
        [1, 1, 0],
        [-1, -1, 0],
        [1, -1, 0],
        [-1, 1, 0],
        [1, 0, 1],
        [-1, 0, -1],
        [1, 0, -1],
        [-1, 0, 1],
        [0, 1, 1],
        [0, -1, -1],
        [0, 1, -1],
        [0, -1, 1],
    ]
)
WEIGHTS = np.array([1.0 / 3.0] + [1.0 / 18.0] * 6 + [1.0 / 36.0] * 12)
GHOST_DENSITY = 18.0
INFLOW_SPEED = 0.08
GHOST_STATE = (
    WEIGHTS
    * GHOST_DENSITY
    * (
        1.0
        + 3.0 * VELOCITY[:, 0] * INFLOW_SPEED
        + 4.5 * (VELOCITY[:, 0] * INFLOW_SPEED) ** 2
        - 1.5 * INFLOW_SPEED**2
    )
)
GHOST = [float(value) for value in GHOST_STATE]
VEL = [tuple(int(part) for part in row) for row in VELOCITY]
CX = [row[0] for row in VEL]
UP = [p for p in range(19) if CX[p] == 1]
DOWN = [p for p in range(19) if CX[p] == -1]
FLAT = [p for p in range(19) if CX[p] == 0]
LEFT = [p for p in range(19) if VEL[p][1] == -1]
RIGHT = [p for p in range(19) if VEL[p][1] == 1]
ALONG = [p for p in range(19) if VEL[p][1] == 0]
OPP = [0] + [p + 1 if p % 2 else p - 1 for p in range(1, 19)]
BLEND, WEIGHT = 19, 20
SPAN_WIDE, SPAN_FREE = 15, 5
SPAN_TILES = 2 * SPAN_WIDE + 1
STATE, MOMENTS, NEAR_BLEND, WIDE = 0, 5, 9, 10
SUM_FAR, SUM_NEAR, SUM_OWN, WEIGHT_FAR, WEIGHT_NEAR, LAYERS = 10, 14, 18, 21, 22, 23
INSET = WIDE // 2
TILES = LAYERS + WIDE + (LAYERS - WIDE - INSET + 1) // 2


def sublane(tile):
    return lax.broadcasted_iota(jnp.int32, tile.shape, len(tile.shape) - 2)


def lane(tile):
    return lax.broadcasted_iota(jnp.int32, tile.shape, len(tile.shape) - 1)


def spin(tile, rows):
    return pltpu.roll(tile, rows % 8, 0) if rows % 8 else tile


def shift_z(tile, step, fill):
    if step == 0:
        return tile
    rolled = pltpu.roll(tile, step % 128, 1)
    return jnp.where(lane(tile) == (0 if step == 1 else 127), fill, rolled)


def shift_y(pair, step):
    if step == 0:
        return pair
    own, side = (pltpu.roll(tile, step % 8, 0) for tile in pair)
    edge = sublane(own) == (0 if step == 1 else 7)
    return (jnp.where(edge, side, own), jnp.where(edge, own, side))


def shift_pair(pair, stepy, stepz, fill):
    return tuple(shift_z(tile, stepz, fill) for tile in shift_y(pair, stepy))


def pairs_of(f):
    sums = [f[2 * i + 1] + f[2 * i + 2] for i in range(9)]
    diffs = [f[2 * i + 1] - f[2 * i + 2] for i in range(9)]
    return sums, diffs


def along_axes(v):
    return (
        v[0] + v[3] + v[4] + v[5] + v[6],
        v[1] + v[3] - v[4] + v[7] + v[8],
        v[2] + v[5] - v[6] + v[7] - v[8],
    )


def dots(u):
    x, y, z = u
    return [x, y, z, x + y, x - y, x + z, x - z, y + z, y - z]


def flow(f0, sums, diffs):
    density = f0 + sum(sums[1:], sums[0])
    inverse = 1.0 / density
    u = [m * inverse for m in along_axes(diffs)]
    square = u[0] * u[0] + u[1] * u[1] + u[2] * u[2]
    return density, u, square


def collide(f, b):
    sums, diffs = pairs_of(f)
    density, u, square = flow(f[0], sums, diffs)
    keep = 1.0 - b
    j = 0.1 * keep
    alpha, beta = 0.5 * (j + b), 0.5 * (j - b)
    scaled = (0.9 * keep) * density
    rest = scaled * (1.0 - 1.5 * square)
    flux = dots([scaled * part for part in u])
    out = [(j + b) * f[0] + (1.0 / 3.0) * rest]
    rest_axis, rest_diag = rest * (1.0 / 18.0), rest * (1.0 / 36.0)
    for i, along in enumerate(dots(u)):
        w = 1.0 / 18.0 if i < 3 else 1.0 / 36.0
        even = alpha * sums[i] + (rest_axis if i < 3 else rest_diag) + flux[i] * along * (4.5 * w)
        odd = beta * diffs[i] + flux[i] * (3.0 * w)
        out += [even + odd, even - odd]
    return out


def adjoint_values(u, square, b, h, wanted):
    s, d = pairs_of(h)
    w = [1.0 / 18.0] * 3 + [1.0 / 36.0] * 6
    t = [s[i] * w[i] for i in range(9)]
    h0 = h[0] * (1.0 / 3.0) + sum(t[1:], t[0])
    h1 = along_axes([d[i] * w[i] for i in range(9)])
    xx = t[0] + t[3] + t[4] + t[5] + t[6]
    yy = t[1] + t[3] + t[4] + t[7] + t[8]
    zz = t[2] + t[5] + t[6] + t[7] + t[8]
    xy, xz, yz = t[3] - t[4], t[5] - t[6], t[7] - t[8]
    v = (
        xx * u[0] + xy * u[1] + xz * u[2],
        xy * u[0] + yy * u[1] + yz * u[2],
        xz * u[0] + yz * u[1] + zz * u[2],
    )
    quad = u[0] * v[0] + u[1] * v[1] + u[2] * v[2]
    keep = 1.0 - b
    j, k = 0.1 * keep, 0.9 * keep
    alpha, beta = 0.5 * (j + b), 0.5 * (j - b)
    base = k * (h0 * (1.0 + 1.5 * square) - 4.5 * quad)
    push = dots([k * (3.0 * h1[i] + 9.0 * v[i] - 3.0 * u[i] * h0) for i in range(3)])
    out = {}
    if 0 in wanted:
        out[0] = (j + b) * h[0] + base
    for i in range(9):
        first, second = 2 * i + 1, 2 * i + 2
        if first in wanted or second in wanted:
            even = alpha * s[i] + base
            odd = beta * d[i] + push[i]
            if first in wanted:
                out[first] = even + odd
            if second in wanted:
                out[second] = even - odd
    return out, s, d, h0, h1, quad


def adjoint_collide(f, b, h, wanted, blend_part):
    fsums, fdiffs = pairs_of(f)
    density, u, square = flow(f[0], fsums, fdiffs)
    out, s, d, h0, h1, quad = adjoint_values(u, square, b, h, wanted)
    part = None
    if blend_part:
        equil = h0 * (1.0 - 1.5 * square) + 4.5 * quad
        equil = equil + 3.0 * (u[0] * h1[0] + u[1] * h1[1] + u[2] * h1[2])
        evens = sum((s[i] * fsums[i] for i in range(1, 9)), s[0] * fsums[0])
        odds = sum((d[i] * fdiffs[i] for i in range(1, 9)), d[0] * fdiffs[0])
        part = 0.9 * h[0] * f[0] + 0.45 * evens - 0.55 * odds - 0.9 * density * equil
    return out, part


def moment_sums(values):
    density = functools.reduce(lambda a, b: a + b, values.values())
    momentum = []
    for k in range(3):
        total = None
        for p, value in values.items():
            if VEL[p][k] == 1:
                total = value if total is None else total + value
        for p, value in values.items():
            if VEL[p][k] == -1:
                total = -value if total is None else total - value
        momentum.append(total)
    return [density] + momentum


def add(*totals):
    return [functools.reduce(lambda a, b: a + b, parts) for parts in zip(*totals)]


def put_message(ref, layers):
    for i, pair in enumerate(layers):
        ref[i] = pair[0]
    at = sublane(layers[0][1])
    for i in range(WIDE):
        tile = layers[i][1]
        if i // 2 < INSET:
            inset = pltpu.roll(layers[WIDE + i // 2][1], 5 if i % 2 else 3, 0)
            tile = jnp.where((at == 3) | (at == 4), inset, tile)
        ref[LAYERS + i] = tile
    for i in range(WIDE + INSET, LAYERS, 2):
        tile = layers[i][1]
        if i + 1 < LAYERS:
            tile = jnp.where((at < 2) | (at > 5), tile, pltpu.roll(layers[i + 1][1], 4, 0))
        ref[LAYERS + WIDE + (i - WIDE - INSET) // 2] = tile


def get_message(read, i):
    if i < WIDE:
        return (read(i), read(LAYERS + i))
    if i < WIDE + INSET:
        first, second = (read(LAYERS + 2 * (i - WIDE) + k) for k in range(2))
        first, second = pltpu.roll(first, 5, 0), pltpu.roll(second, 3, 0)
        return (read(i), jnp.where(sublane(first) < 4, first, second))
    tile = read(LAYERS + WIDE + (i - WIDE - INSET) // 2)
    return (read(i), pltpu.roll(tile, 4, 0) if (i - WIDE - INSET) % 2 else tile)


def turn_of(column):
    least = min if isinstance(column, int) else jnp.minimum
    return least(column % 4 // 2 + column // 8, 1)


def wide_layers(core):
    towards = [jnp.where(core == 0, a, b) for a, b in zip(LEFT, RIGHT)]
    return towards + ALONG + [BLEND]


def narrow_layers(core):
    return [jnp.where(core == 0, b, a) for a, b in zip(LEFT, RIGHT)] + [WEIGHT]


def start_kernel(
    f_hbm, porosity_hbm, weight_hbm, solid_hbm, surface_hbm, own_ref, half_ref,
    f_ref, porosity_ref, weight_ref, solid_ref, surface_ref, sems,
):
    small = [
        pltpu.make_async_copy(source, target, sems.at[i])
        for i, (source, target) in enumerate(
            (
                (solid_hbm, solid_ref),
                (surface_hbm, surface_ref),
                (porosity_hbm, porosity_ref),
                (weight_hbm, weight_ref),
            )
        )
    ]
    rows = [
        pltpu.make_async_copy(f_hbm.at[:, x], f_ref.at[:, x], sems.at[4 + x]) for x in range(4)
    ]
    for copy in rows[:1] + small + rows[1:]:
        copy.start()
    core = lax.rem(lax.axis_index("span"), 2)
    at = lax.broadcasted_iota(jnp.int32, (8, 128), 0)
    low = (at < 4) == (core == 0)
    for copy in small:
        copy.wait()
    for x in range(4):
        porosity = porosity_ref[x]
        blend = jnp.where(
            solid_ref[x] == 1, 1.0, jnp.where(surface_ref[x] == 1, porosity, 0.0)
        )
        rows[x].wait()
        out = collide([f_ref[p, x] for p in range(19)], blend)
        for p in range(19):
            own_ref[p, x] = out[p]
        own_ref[BLEND, x] = blend
        own_ref[WEIGHT, x] = weight_ref[x]
        if x % 2:
            for i, layer in enumerate(wide_layers(core)):
                first, second = own_ref[layer, x - 1], own_ref[layer, x]
                half_ref[2 * i + x // 2] = jnp.where(low, first, pltpu.roll(second, 4, 0))
    for i, layer in enumerate(narrow_layers(core)):
        tile = own_ref[layer, 0]
        for x in range(1, 4):
            here = lax.rem(at + 8 - 2 * x + 2 * core, 8) < 2
            tile = jnp.where(here, pltpu.roll(own_ref[layer, x], 2 * x, 0), tile)
        if i == 5:
            half_ref[2 * SPAN_WIDE] = tile
            continue
        for k in range(4):
            slot = 2 * SPAN_FREE + 4 * i + k
            piece = jnp.where(core == 0, spin(tile, 3 - k), spin(tile, -k))
            free = lax.rem(at, 4) == 3 * (1 - core)
            half_ref[slot] = jnp.where(free, piece, half_ref[slot])


def inner_kernel(
    own_ref, both_ref, half_ref, side_ref, state_ref, next_ref, first_ref, second_ref, message_ref
):
    core = lax.rem(lax.axis_index("span"), 2)
    odd = lax.rem(lax.axis_index("stream"), 2)
    at = lax.broadcasted_iota(jnp.int32, (8, 128), 0)
    low = (at < 4) == (core == 0)
    for i, layer in enumerate(wide_layers(1 - core)):
        for x in range(4):
            tile = half_ref[2 * i + x // 2]
            tile = pltpu.roll(tile, 4, 0) if x % 2 else tile
            side_ref[layer, x] = jnp.where(low, both_ref[1 - core, layer, x], tile)
    for i, layer in enumerate(narrow_layers(1 - core)):
        rows = half_ref[2 * SPAN_WIDE]
        for k in range(4 if i < 5 else 0):
            piece = half_ref[2 * SPAN_FREE + 4 * i + k]
            piece = jnp.where(core == 1, spin(piece, k - 3), spin(piece, k))
            rows = jnp.where(lax.rem(at, 4) == k, piece, rows) if k else piece
        for x in range(4):
            side_ref[layer, x] = jnp.where(low, both_ref[1 - core, layer, x], spin(rows, -2 * x))

    def c0(p, x):
        return (own_ref[p, x], side_ref[p, x])

    def moved(p, pair):
        return shift_pair(pair, VEL[p][1], VEL[p][2], GHOST[p])

    for x in (1, 2):
        f = [moved(p, c0(p, x - CX[p])) for p in range(19)]
        blend = c0(BLEND, x)
        for t in range(2):
            tiles = [f[p][t] for p in range(19)]
            out = collide(tiles, blend[t])
            for p in range(19):
                state_ref[p, x - 1, t] = tiles[p]
                next_ref[p, x - 1, t] = out[p]

    def c1(p, x):
        return (next_ref[p, x - 1, 0], next_ref[p, x - 1, 1])

    for side, near, far, inward, outward in ((0, 3, 2, UP, DOWN), (1, 0, 1, DOWN, UP)):
        step = far - near
        enter = [moved(p, c0(p, near)) for p in inward]
        known = {p: moved(p, c0(p, near if p in FLAT else far)) for p in inward + FLAT}
        blend = c0(BLEND, near)
        j = [0.1 * (1.0 - part) for part in blend]
        layers = [None] * LAYERS
        layers[STATE : STATE + 5] = enter
        halves = [moment_sums({p: known[p][t] for p in known}) for t in range(2)]
        layers[MOMENTS : MOMENTS + 4] = list(zip(*halves))
        layers[NEAR_BLEND] = blend
        came = {p: moved(p, c1(p, far + step)) for p in inward}
        came.update({p: moved(p, c1(p, far)) for p in FLAT})
        for p in outward:
            came[p] = moved(p, tuple(blend[t] * known[OPP[p]][t] for t in range(2)))
        halves = [moment_sums({p: came[p][t] for p in came}) for t in range(2)]
        layers[SUM_FAR : SUM_FAR + 4] = list(zip(*halves))
        came = {p: moved(p, c1(p, far)) for p in inward}
        for p in FLAT:
            came[p] = moved(
                p,
                tuple(j[t] * known[p][t] + blend[t] * known[OPP[p]][t] for t in range(2)),
            )
        halves = [moment_sums({p: came[p][t] for p in came}) for t in range(2)]
        layers[SUM_NEAR : SUM_NEAR + 4] = list(zip(*halves))
        came = {p: moved(p, tuple(j[t] * known[p][t] for t in range(2))) for p in inward}
        halves = [moment_sums({p: came[p][t] for p in came}) for t in range(2)]
        halves = [[half[0], half[2], half[3]] for half in halves]
        layers[SUM_OWN : SUM_OWN + 3] = list(zip(*halves))
        layers[WEIGHT_FAR] = c0(WEIGHT, far)
        layers[WEIGHT_NEAR] = c0(WEIGHT, near)
        put_message(message_ref.at[side], layers)
    towards = lax.rem(1 - odd + turn_of(lax.axis_index("span")), 2)
    for i in range(TILES):
        first_ref[i] = message_ref[towards, i]
        second_ref[i] = message_ref[1 - towards, i]


def last_kernel(
    f_ref, solid_ref, surface_ref, own_ref, side_ref, state_ref, next_ref, one_ref, two_ref,
    adjoint_hbm, sensitivity_hbm, adjoint_ref, sensitivity_ref,
    s1_ref, c1_ref, sum_ref, flow_ref, a1_ref, field_ref, sems,
):
    place = lax.axis_index("stream")
    at_start = place == 0
    at_end = place == lax.axis_size("stream") - 1
    origin = lax.rem(1 - lax.rem(place, 2) + turn_of(lax.axis_index("span")), 2)

    def low(i):
        return jnp.where(origin == 1, one_ref[i], two_ref[origin, i])

    def high(i):
        return jnp.where(origin == 0, one_ref[i], two_ref[origin, i])

    ends = (
        (low, at_start, 0, -1, UP, DOWN),
        (high, at_end, 3, 1, DOWN, UP),
    )

    def moved(p, pair, fill=None):
        return shift_pair(pair, VEL[p][1], VEL[p][2], GHOST[p] if fill is None else fill)

    def c0(p, x):
        return (own_ref[p, x], side_ref[p, x])

    for read, end, x, out, inward, outward in ends:
        f = {p: moved(p, c0(p, x if p in FLAT else x - out)) for p in FLAT + outward}
        for i, p in enumerate(inward):
            f[p] = tuple(
                jnp.where(end, GHOST[p], part) for part in get_message(read, STATE + i)
            )
        blend = c0(BLEND, x)
        for t in range(2):
            tiles = [f[p][t] for p in range(19)]
            after = collide(tiles, blend[t])
            for p in range(19):
                s1_ref[p, x // 3, t] = tiles[p]
                c1_ref[p, x // 3, t] = after[p]

    def s1(p, x, t):
        return state_ref[p, x - 1, t] if x in (1, 2) else s1_ref[p, x // 3, t]

    def c1(p, x):
        ref, at = (next_ref, x - 1) if x in (1, 2) else (c1_ref, x // 3)
        return (ref[p, at, 0], ref[p, at, 1])

    def save_field(x, t, total, weight, end=None):
        inverse = 1.0 / total[0]
        u = [total[i] * inverse for i in range(1, 4)]
        kinetic = 0.5 * (u[0] * u[0] + u[1] * u[1] + u[2] * u[2])
        for i, value in enumerate(u + [kinetic]):
            value = weight * value
            field_ref[i, x + 2, t] = value if end is None else jnp.where(end, 0.0, value)

    for side, (read, end, x, out, inward, outward) in enumerate(ends):
        sent = [get_message(read, i) for i in range(LAYERS)]
        blend = sent[NEAR_BLEND]
        leaving = {p: moved(p, c0(p, x)) for p in outward}
        to_far, to_near, to_own = {}, {}, {}
        for t in range(2):
            total = add(
                moment_sums({p: leaving[p][t] for p in outward}),
                [sent[MOMENTS + i][t] for i in range(4)],
            )
            density = total[0]
            inverse = 1.0 / density
            u = [part * inverse for part in total[1:]]
            square = u[0] * u[0] + u[1] * u[1] + u[2] * u[2]
            for i, value in enumerate(u + [square]):
                flow_ref[side, i, t] = value
            keep = 1.0 - blend[t]
            scaled = (0.9 * keep) * density
            rest = scaled * (1.0 - 1.5 * square)
            along = dots(u)
            for p in range(19):
                value = float(WEIGHTS[p]) * rest
                if p:
                    cu = along[(p - 1) // 2]
                    flux = scaled * cu
                    value = value + flux * cu * float(4.5 * WEIGHTS[p])
                    value = value + flux * float((3.0 if p % 2 else -3.0) * WEIGHTS[p])
                if p in outward:
                    to_far.setdefault(p, []).append(value + 0.1 * keep * leaving[p][t])
                elif p in inward:
                    to_own.setdefault(p, []).append(value + blend[t] * leaving[OPP[p]][t])
                else:
                    to_near.setdefault(p, []).append(value)
        to_far = {p: moved(p, tuple(pair), 0.0) for p, pair in to_far.items()}
        to_near = {p: moved(p, tuple(pair), 0.0) for p, pair in to_near.items()}
        to_own = {p: moved(p, tuple(pair), 0.0) for p, pair in to_own.items()}
        back = {p: moved(p, c1(p, x)) for p in outward}
        for t in range(2):
            total = add(
                moment_sums({p: to_far[p][t] for p in to_far}),
                [sent[SUM_FAR + i][t] for i in range(4)],
            )
            save_field(x + 2 * out, t, total, sent[WEIGHT_FAR][t], end)
            near = dict(to_near)
            near.update(back)
            total = add(
                moment_sums({p: near[p][t] for p in near}),
                [sent[SUM_NEAR + i][t] for i in range(4)],
            )
            save_field(x + out, t, total, sent[WEIGHT_NEAR][t], end)
            own = moment_sums({p: to_own[p][t] for p in to_own})
            ready = [sent[SUM_OWN + i][t] for i in range(3)]
            own = add(own, [ready[0], -out * ready[0], ready[1], ready[2]])
            ghost = moment_sums({p: GHOST[p] for p in inward})
            for i in range(4):
                sum_ref[side, i, t] = jnp.where(end, ghost[i], own[i])

    for x in range(4):
        pops, given = list(range(19)), None
        if x == 0:
            pops, given = FLAT + DOWN, 0
        if x == 3:
            pops, given = FLAT + UP, 1
        came = {p: moved(p, c1(p, x - CX[p])) for p in pops}
        weight = c0(WEIGHT, x)
        for t in range(2):
            total = moment_sums({p: came[p][t] for p in came})
            if given is not None:
                total = add(total, [sum_ref[given, i, t] for i in range(4)])
            save_field(x, t, total, weight[t])

    def cotangent(p, x):
        pair = []
        for t in range(2):
            value = -field_ref[3, x + CX[p] + 2, t]
            for k in range(3):
                if VEL[p][k] == 1:
                    value = value + field_ref[k, x + CX[p] + 2, t]
                if VEL[p][k] == -1:
                    value = value - field_ref[k, x + CX[p] + 2, t]
            pair.append(value)
        return shift_pair(tuple(pair), -VEL[p][1], -VEL[p][2], 0.0)

    for x in range(4):
        h = [cotangent(p, x) for p in range(19)]
        blend = c0(BLEND, x)
        for t in range(2):
            wanted = [p for p in range(19) if t == 0 or VEL[p][1] != 0]
            out, part = adjoint_collide(
                [s1(p, x, t) for p in range(19)],
                blend[t],
                [h[p][t] for p in range(19)],
                wanted,
                t == 0,
            )
            for p, value in out.items():
                a1_ref[p, x + 1, t] = value
            if part is not None:
                sensitivity_ref[x] = part
    for side, (read, end, x, out, inward, outward) in enumerate(ends):
        h = [cotangent(p, x + out) for p in range(19)]
        blend = get_message(read, NEAR_BLEND)
        for t in range(2):
            u = [flow_ref[side, i, t] for i in range(3)]
            wanted = [p for p in outward if t == 0 or VEL[p][1] != 0]
            got = adjoint_values(
                u, flow_ref[side, 3, t], blend[t], [h[p][t] for p in range(19)], wanted
            )[0]
            for p, value in got.items():
                a1_ref[p, x + out + 1, t] = jnp.where(end, 0.0, value)

    sent = []
    for x in range(4):
        h = []
        for p in range(19):
            at = x + CX[p] + 1
            tile = a1_ref[p, at, 0]
            if VEL[p][1]:
                tile = shift_y((tile, a1_ref[p, at, 1]), -VEL[p][1])[0]
            h.append(shift_z(tile, -VEL[p][2], 0.0))
        out, part = adjoint_collide(
            [f_ref[p, x] for p in range(19)], own_ref[BLEND, x], h, list(range(19)), True
        )
        for p in range(19):
            adjoint_ref[p, x] = out[p]
        sent.append(
            pltpu.make_async_copy(adjoint_ref.at[:, x], adjoint_hbm.at[:, x], sems.at[x])
        )
        sent[x].start()
        design = (solid_ref[x] == 0) & (surface_ref[x] == 1)
        sensitivity_ref[x] = jnp.where(design, sensitivity_ref[x] + part, 0.0)
    sent.append(pltpu.make_async_copy(sensitivity_ref, sensitivity_hbm, sems.at[4]))
    sent[4].start()
    for copy in sent:
        copy.wait()


def call(kernel, inputs, shapes, scratch=(), space=pltpu.VMEM, result=pltpu.VMEM):
    return pl.pallas_call(
        kernel,
        out_shape=[jax.ShapeDtypeStruct(shape, jnp.float32) for shape in shapes],
        in_specs=[pl.BlockSpec(memory_space=space)] * len(inputs),
        out_specs=[pl.BlockSpec(memory_space=result)] * len(shapes),
        scratch_shapes=scratch,
        compiler_params=pltpu.CompilerParams(vmem_limit_bytes=24 * 1024 * 1024),
    )(*inputs)


def shards(checkpoint, porosity, deposit_weight, solid_mask, surface_mask):
    stream, span = lax.axis_size("stream"), lax.axis_size("span")
    tile = (8, 128)
    block, half = (21, 4) + tile, (SPAN_TILES,) + tile
    inputs = tuple(
        pltpu.with_memory_space_constraint(value, pltpu.HBM)
        for value in (checkpoint, porosity, deposit_weight, solid_mask, surface_mask)
    )
    own, mine = call(
        start_kernel,
        inputs,
        [block, half],
        [pltpu.VMEM(value.shape, value.dtype) for value in inputs]
        + [pltpu.SemaphoreType.DMA((8,))],
        pltpu.HBM,
    )
    cores = [[i, i + 1] for i in range(0, span, 2)]
    chips = [(i, (i + 1) % span) for i in range(1, span, 2)]
    came = lax.ppermute(mine, "span", chips + [(b, a) for a, b in chips])
    both = lax.all_gather(own, "span", axis_index_groups=cores)
    rows = (19, 2, 2) + tile
    message = (TILES,) + tile
    side, state, following, first, second = call(
        inner_kernel,
        (own, both, came),
        [block, rows, rows, message, message],
        [pltpu.VMEM((2,) + message, jnp.float32)],
    )

    swaps, groups = [], []
    for j in range(span):
        turn = turn_of(j)
        swaps += [(i * span + j, (i + 1) * span + j) for i in range(1 - turn, stream - 1, 2)]
        groups += [[i * span + j, (i + 1) * span + j] for i in range(turn, stream - 1, 2)]
        if turn and j % 2:
            groups += [[i * span + j - 1, i * span + j] for i in (0, stream - 1)]
    axes = ("stream", "span")
    one = lax.ppermute(first, axes, swaps + [(b, a) for a, b in swaps])
    two = lax.all_gather(second, axes, axis_index_groups=groups)
    scratch = [
        (19, 4), (4,), (19, 2, 2), (19, 2, 2), (2, 4, 2), (2, 4, 2), (19, 6, 2), (4, 8, 2),
    ]
    adjoint, sensitivity = call(
        last_kernel,
        (checkpoint, solid_mask, surface_mask, own, side, state, following, one, two),
        [(19, 4) + tile, (4,) + tile],
        [pltpu.VMEM(shape + tile, jnp.float32) for shape in scratch]
        + [pltpu.SemaphoreType.DMA((5,))],
        result=pl.ANY,
    )
    return (adjoint, sensitivity)


def solution(mesh):
    placed = (
        P(None, "stream", "span", None),
        P("stream", "span", None),
        P("stream", "span", None),
        P("stream", "span", None),
        P("stream", "span", None),
    )
    return jax.shard_map(
        shards,
        mesh=mesh,
        in_specs=placed,
        out_specs=(P(None, "stream", "span", None), P("stream", "span", None)),
        check_vma=False,
    )
```

```python
import functools

import jax
import jax.numpy as jnp
import numpy as np
from jax import lax
from jax.experimental import pallas as pl
from jax.experimental.pallas import tpu as pltpu
from jax.sharding import PartitionSpec as P

VELOCITY = np.array(
    [
        [0, 0, 0],
        [1, 0, 0],
        [-1, 0, 0],
        [0, 1, 0],
        [0, -1, 0],
        [0, 0, 1],
        [0, 0, -1],
        [1, 1, 0],
        [-1, -1, 0],
        [1, -1, 0],
        [-1, 1, 0],
        [1, 0, 1],
        [-1, 0, -1],
        [1, 0, -1],
        [-1, 0, 1],
        [0, 1, 1],
        [0, -1, -1],
        [0, 1, -1],
        [0, -1, 1],
    ]
)
WEIGHTS = np.array([1.0 / 3.0] + [1.0 / 18.0] * 6 + [1.0 / 36.0] * 12)
GHOST_DENSITY = 18.0
INFLOW_SPEED = 0.08
GHOST_STATE = (
    WEIGHTS
    * GHOST_DENSITY
    * (
        1.0
        + 3.0 * VELOCITY[:, 0] * INFLOW_SPEED
        + 4.5 * (VELOCITY[:, 0] * INFLOW_SPEED) ** 2
        - 1.5 * INFLOW_SPEED**2
    )
)
GHOST = [float(value) for value in GHOST_STATE]
VEL = [tuple(int(part) for part in row) for row in VELOCITY]
CX = [row[0] for row in VEL]
UP = [p for p in range(19) if CX[p] == 1]
DOWN = [p for p in range(19) if CX[p] == -1]
FLAT = [p for p in range(19) if CX[p] == 0]
LEFT = [p for p in range(19) if VEL[p][1] == -1]
RIGHT = [p for p in range(19) if VEL[p][1] == 1]
ALONG = [p for p in range(19) if VEL[p][1] == 0]
OPP = [0] + [p + 1 if p % 2 else p - 1 for p in range(1, 19)]
BLEND, WEIGHT = 19, 20
SPAN_WIDE, SPAN_FREE = 15, 5
SPAN_TILES = 2 * SPAN_WIDE + 1
STATE, MOMENTS, NEAR_BLEND, WIDE = 0, 5, 9, 10
SUM_FAR, SUM_NEAR, SUM_OWN, WEIGHT_FAR, WEIGHT_NEAR, LAYERS = 10, 14, 18, 21, 22, 23
INSET = WIDE // 2
TILES = LAYERS + WIDE + (LAYERS - WIDE - INSET + 1) // 2


def sublane(tile):
    return lax.broadcasted_iota(jnp.int32, tile.shape, len(tile.shape) - 2)


def lane(tile):
    return lax.broadcasted_iota(jnp.int32, tile.shape, len(tile.shape) - 1)


def spin(tile, rows):
    return pltpu.roll(tile, rows % 8, 0) if rows % 8 else tile


def shift_z(tile, step, fill):
    if step == 0:
        return tile
    rolled = pltpu.roll(tile, step % 128, 1)
    return jnp.where(lane(tile) == (0 if step == 1 else 127), fill, rolled)


def shift_y(pair, step):
    if step == 0:
        return pair
    own, side = (pltpu.roll(tile, step % 8, 0) for tile in pair)
    edge = sublane(own) == (0 if step == 1 else 7)
    return (jnp.where(edge, side, own), jnp.where(edge, own, side))


def shift_pair(pair, stepy, stepz, fill):
    return tuple(shift_z(tile, stepz, fill) for tile in shift_y(pair, stepy))


def pairs_of(f):
    sums = [f[2 * i + 1] + f[2 * i + 2] for i in range(9)]
    diffs = [f[2 * i + 1] - f[2 * i + 2] for i in range(9)]
    return sums, diffs


def along_axes(v):
    return (
        v[0] + v[3] + v[4] + v[5] + v[6],
        v[1] + v[3] - v[4] + v[7] + v[8],
        v[2] + v[5] - v[6] + v[7] - v[8],
    )


def dots(u):
    x, y, z = u
    return [x, y, z, x + y, x - y, x + z, x - z, y + z, y - z]


def flow(f0, sums, diffs):
    density = f0 + sum(sums[1:], sums[0])
    inverse = 1.0 / density
    u = [m * inverse for m in along_axes(diffs)]
    square = u[0] * u[0] + u[1] * u[1] + u[2] * u[2]
    return density, u, square


def collide(f, b):
    sums, diffs = pairs_of(f)
    density, u, square = flow(f[0], sums, diffs)
    keep = 1.0 - b
    j = 0.1 * keep
    alpha, beta = 0.5 * (j + b), 0.5 * (j - b)
    scaled = (0.9 * keep) * density
    rest = scaled * (1.0 - 1.5 * square)
    flux = dots([scaled * part for part in u])
    out = [(j + b) * f[0] + (1.0 / 3.0) * rest]
    rest_axis, rest_diag = rest * (1.0 / 18.0), rest * (1.0 / 36.0)
    for i, along in enumerate(dots(u)):
        w = 1.0 / 18.0 if i < 3 else 1.0 / 36.0
        even = alpha * sums[i] + (rest_axis if i < 3 else rest_diag) + flux[i] * along * (4.5 * w)
        odd = beta * diffs[i] + flux[i] * (3.0 * w)
        out += [even + odd, even - odd]
    return out


def adjoint_values(u, square, b, h, wanted):
    s, d = pairs_of(h)
    w = [1.0 / 18.0] * 3 + [1.0 / 36.0] * 6
    t = [s[i] * w[i] for i in range(9)]
    h0 = h[0] * (1.0 / 3.0) + sum(t[1:], t[0])
    h1 = along_axes([d[i] * w[i] for i in range(9)])
    xx = t[0] + t[3] + t[4] + t[5] + t[6]
    yy = t[1] + t[3] + t[4] + t[7] + t[8]
    zz = t[2] + t[5] + t[6] + t[7] + t[8]
    xy, xz, yz = t[3] - t[4], t[5] - t[6], t[7] - t[8]
    v = (
        xx * u[0] + xy * u[1] + xz * u[2],
        xy * u[0] + yy * u[1] + yz * u[2],
        xz * u[0] + yz * u[1] + zz * u[2],
    )
    quad = u[0] * v[0] + u[1] * v[1] + u[2] * v[2]
    keep = 1.0 - b
    j, k = 0.1 * keep, 0.9 * keep
    alpha, beta = 0.5 * (j + b), 0.5 * (j - b)
    base = k * (h0 * (1.0 + 1.5 * square) - 4.5 * quad)
    push = dots([k * (3.0 * h1[i] + 9.0 * v[i] - 3.0 * u[i] * h0) for i in range(3)])
    out = {}
    if 0 in wanted:
        out[0] = (j + b) * h[0] + base
    for i in range(9):
        first, second = 2 * i + 1, 2 * i + 2
        if first in wanted or second in wanted:
            even = alpha * s[i] + base
            odd = beta * d[i] + push[i]
            if first in wanted:
                out[first] = even + odd
            if second in wanted:
                out[second] = even - odd
    return out, s, d, h0, h1, quad


def adjoint_collide(f, b, h, wanted, blend_part):
    fsums, fdiffs = pairs_of(f)
    density, u, square = flow(f[0], fsums, fdiffs)
    out, s, d, h0, h1, quad = adjoint_values(u, square, b, h, wanted)
    part = None
    if blend_part:
        equil = h0 * (1.0 - 1.5 * square) + 4.5 * quad
        equil = equil + 3.0 * (u[0] * h1[0] + u[1] * h1[1] + u[2] * h1[2])
        evens = sum((s[i] * fsums[i] for i in range(1, 9)), s[0] * fsums[0])
        odds = sum((d[i] * fdiffs[i] for i in range(1, 9)), d[0] * fdiffs[0])
        part = 0.9 * h[0] * f[0] + 0.45 * evens - 0.55 * odds - 0.9 * density * equil
    return out, part


def moment_sums(values):
    density = functools.reduce(lambda a, b: a + b, values.values())
    momentum = []
    for k in range(3):
        total = None
        for p, value in values.items():
            if VEL[p][k] == 1:
                total = value if total is None else total + value
        for p, value in values.items():
            if VEL[p][k] == -1:
                total = -value if total is None else total - value
        momentum.append(total)
    return [density] + momentum


def add(*totals):
    return [functools.reduce(lambda a, b: a + b, parts) for parts in zip(*totals)]


def put_message(ref, layers):
    for i, pair in enumerate(layers):
        ref[i] = pair[0]
    at = sublane(layers[0][1])
    for i in range(WIDE):
        tile = layers[i][1]
        if i // 2 < INSET:
            inset = pltpu.roll(layers[WIDE + i // 2][1], 5 if i % 2 else 3, 0)
            tile = jnp.where((at == 3) | (at == 4), inset, tile)
        ref[LAYERS + i] = tile
    for i in range(WIDE + INSET, LAYERS, 2):
        tile = layers[i][1]
        if i + 1 < LAYERS:
            tile = jnp.where((at < 2) | (at > 5), tile, pltpu.roll(layers[i + 1][1], 4, 0))
        ref[LAYERS + WIDE + (i - WIDE - INSET) // 2] = tile


def get_message(read, i):
    if i < WIDE:
        return (read(i), read(LAYERS + i))
    if i < WIDE + INSET:
        first, second = (read(LAYERS + 2 * (i - WIDE) + k) for k in range(2))
        first, second = pltpu.roll(first, 5, 0), pltpu.roll(second, 3, 0)
        return (read(i), jnp.where(sublane(first) < 4, first, second))
    tile = read(LAYERS + WIDE + (i - WIDE - INSET) // 2)
    return (read(i), pltpu.roll(tile, 4, 0) if (i - WIDE - INSET) % 2 else tile)


def turn_of(column):
    return min(column // 2, 1) if isinstance(column, int) else jnp.minimum(column // 2, 1)


def wide_layers(core):
    towards = [jnp.where(core == 0, a, b) for a, b in zip(LEFT, RIGHT)]
    return towards + ALONG + [BLEND]


def narrow_layers(core):
    return [jnp.where(core == 0, b, a) for a, b in zip(LEFT, RIGHT)] + [WEIGHT]


def start_kernel(
    f_hbm, porosity_hbm, weight_hbm, solid_hbm, surface_hbm, own_ref, half_ref,
    f_ref, porosity_ref, weight_ref, solid_ref, surface_ref, sems,
):
    small = [
        pltpu.make_async_copy(source, target, sems.at[i])
        for i, (source, target) in enumerate(
            (
                (solid_hbm, solid_ref),
                (surface_hbm, surface_ref),
                (porosity_hbm, porosity_ref),
                (weight_hbm, weight_ref),
            )
        )
    ]
    rows = [
        pltpu.make_async_copy(f_hbm.at[:, x], f_ref.at[:, x], sems.at[4 + x]) for x in range(4)
    ]
    for copy in rows[:1] + small + rows[1:]:
        copy.start()
    core = lax.rem(lax.axis_index("span"), 2)
    at = lax.broadcasted_iota(jnp.int32, (8, 128), 0)
    low = (at < 4) == (core == 0)
    for copy in small:
        copy.wait()
    for x in range(4):
        porosity = porosity_ref[x]
        blend = jnp.where(
            solid_ref[x] == 1, 1.0, jnp.where(surface_ref[x] == 1, porosity, 0.0)
        )
        rows[x].wait()
        out = collide([f_ref[p, x] for p in range(19)], blend)
        for p in range(19):
            own_ref[p, x] = out[p]
        own_ref[BLEND, x] = blend
        own_ref[WEIGHT, x] = weight_ref[x]
        if x % 2:
            for i, layer in enumerate(wide_layers(core)):
                first, second = own_ref[layer, x - 1], own_ref[layer, x]
                half_ref[2 * i + x // 2] = jnp.where(low, first, pltpu.roll(second, 4, 0))
    for i, layer in enumerate(narrow_layers(core)):
        tile = own_ref[layer, 0]
        for x in range(1, 4):
            here = lax.rem(at + 8 - 2 * x + 2 * core, 8) < 2
            tile = jnp.where(here, pltpu.roll(own_ref[layer, x], 2 * x, 0), tile)
        if i == 5:
            half_ref[2 * SPAN_WIDE] = tile
            continue
        for k in range(4):
            slot = 2 * SPAN_FREE + 4 * i + k
            piece = jnp.where(core == 0, spin(tile, 3 - k), spin(tile, -k))
            free = lax.rem(at, 4) == 3 * (1 - core)
            half_ref[slot] = jnp.where(free, piece, half_ref[slot])


def inner_kernel(
    own_ref, both_ref, half_ref, side_ref, state_ref, next_ref, first_ref, second_ref, message_ref
):
    core = lax.rem(lax.axis_index("span"), 2)
    odd = lax.rem(lax.axis_index("stream"), 2)
    at = lax.broadcasted_iota(jnp.int32, (8, 128), 0)
    low = (at < 4) == (core == 0)
    for i, layer in enumerate(wide_layers(1 - core)):
        for x in range(4):
            tile = half_ref[2 * i + x // 2]
            tile = pltpu.roll(tile, 4, 0) if x % 2 else tile
            side_ref[layer, x] = jnp.where(low, both_ref[1 - core, layer, x], tile)
    for i, layer in enumerate(narrow_layers(1 - core)):
        rows = half_ref[2 * SPAN_WIDE]
        for k in range(4 if i < 5 else 0):
            piece = half_ref[2 * SPAN_FREE + 4 * i + k]
            piece = jnp.where(core == 1, spin(piece, k - 3), spin(piece, k))
            rows = jnp.where(lax.rem(at, 4) == k, piece, rows) if k else piece
        for x in range(4):
            side_ref[layer, x] = jnp.where(low, both_ref[1 - core, layer, x], spin(rows, -2 * x))

    def c0(p, x):
        return (own_ref[p, x], side_ref[p, x])

    def moved(p, pair):
        return shift_pair(pair, VEL[p][1], VEL[p][2], GHOST[p])

    for x in (1, 2):
        f = [moved(p, c0(p, x - CX[p])) for p in range(19)]
        blend = c0(BLEND, x)
        for t in range(2):
            tiles = [f[p][t] for p in range(19)]
            out = collide(tiles, blend[t])
            for p in range(19):
                state_ref[p, x - 1, t] = tiles[p]
                next_ref[p, x - 1, t] = out[p]

    def c1(p, x):
        return (next_ref[p, x - 1, 0], next_ref[p, x - 1, 1])

    for side, near, far, inward, outward in ((0, 3, 2, UP, DOWN), (1, 0, 1, DOWN, UP)):
        step = far - near
        enter = [moved(p, c0(p, near)) for p in inward]
        known = {p: moved(p, c0(p, near if p in FLAT else far)) for p in inward + FLAT}
        blend = c0(BLEND, near)
        j = [0.1 * (1.0 - part) for part in blend]
        layers = [None] * LAYERS
        layers[STATE : STATE + 5] = enter
        halves = [moment_sums({p: known[p][t] for p in known}) for t in range(2)]
        layers[MOMENTS : MOMENTS + 4] = list(zip(*halves))
        layers[NEAR_BLEND] = blend
        came = {p: moved(p, c1(p, far + step)) for p in inward}
        came.update({p: moved(p, c1(p, far)) for p in FLAT})
        for p in outward:
            came[p] = moved(p, tuple(blend[t] * known[OPP[p]][t] for t in range(2)))
        halves = [moment_sums({p: came[p][t] for p in came}) for t in range(2)]
        layers[SUM_FAR : SUM_FAR + 4] = list(zip(*halves))
        came = {p: moved(p, c1(p, far)) for p in inward}
        for p in FLAT:
            came[p] = moved(
                p,
                tuple(j[t] * known[p][t] + blend[t] * known[OPP[p]][t] for t in range(2)),
            )
        halves = [moment_sums({p: came[p][t] for p in came}) for t in range(2)]
        layers[SUM_NEAR : SUM_NEAR + 4] = list(zip(*halves))
        came = {p: moved(p, tuple(j[t] * known[p][t] for t in range(2))) for p in inward}
        halves = [moment_sums({p: came[p][t] for p in came}) for t in range(2)]
        halves = [[half[0], half[2], half[3]] for half in halves]
        layers[SUM_OWN : SUM_OWN + 3] = list(zip(*halves))
        layers[WEIGHT_FAR] = c0(WEIGHT, far)
        layers[WEIGHT_NEAR] = c0(WEIGHT, near)
        put_message(message_ref.at[side], layers)
    towards = lax.rem(1 - odd + turn_of(lax.axis_index("span")), 2)
    for i in range(TILES):
        first_ref[i] = message_ref[towards, i]
        second_ref[i] = message_ref[1 - towards, i]


def last_kernel(
    f_ref, solid_ref, surface_ref, own_ref, side_ref, state_ref, next_ref, one_ref, two_ref,
    adjoint_hbm, sensitivity_hbm, adjoint_ref, sensitivity_ref,
    s1_ref, c1_ref, sum_ref, flow_ref, a1_ref, field_ref, came_ref, sems,
):
    place = lax.axis_index("stream")
    at_start = place == 0
    at_end = place == lax.axis_size("stream") - 1
    origin = lax.rem(1 - lax.rem(place, 2) + turn_of(lax.axis_index("span")), 2)

    for i in range(TILES):
        came_ref[1 - origin, i] = one_ref[i]
        came_ref[origin, i] = two_ref[origin, i]

    def low(i):
        return came_ref[0, i]

    def high(i):
        return came_ref[1, i]

    ends = (
        (low, at_start, 0, -1, UP, DOWN),
        (high, at_end, 3, 1, DOWN, UP),
    )

    def moved(p, pair, fill=None):
        return shift_pair(pair, VEL[p][1], VEL[p][2], GHOST[p] if fill is None else fill)

    def c0(p, x):
        return (own_ref[p, x], side_ref[p, x])

    for read, end, x, out, inward, outward in ends:
        f = {p: moved(p, c0(p, x if p in FLAT else x - out)) for p in FLAT + outward}
        for i, p in enumerate(inward):
            f[p] = tuple(
                jnp.where(end, GHOST[p], part) for part in get_message(read, STATE + i)
            )
        blend = c0(BLEND, x)
        for t in range(2):
            tiles = [f[p][t] for p in range(19)]
            after = collide(tiles, blend[t])
            for p in range(19):
                s1_ref[p, x // 3, t] = tiles[p]
                c1_ref[p, x // 3, t] = after[p]

    def s1(p, x, t):
        return state_ref[p, x - 1, t] if x in (1, 2) else s1_ref[p, x // 3, t]

    def c1(p, x):
        ref, at = (next_ref, x - 1) if x in (1, 2) else (c1_ref, x // 3)
        return (ref[p, at, 0], ref[p, at, 1])

    def save_field(x, t, total, weight, end=None):
        inverse = 1.0 / total[0]
        u = [total[i] * inverse for i in range(1, 4)]
        kinetic = 0.5 * (u[0] * u[0] + u[1] * u[1] + u[2] * u[2])
        for i, value in enumerate(u + [kinetic]):
            value = weight * value
            field_ref[i, x + 2, t] = value if end is None else jnp.where(end, 0.0, value)

    for side, (read, end, x, out, inward, outward) in enumerate(ends):
        sent = [get_message(read, i) for i in range(LAYERS)]
        blend = sent[NEAR_BLEND]
        leaving = {p: moved(p, c0(p, x)) for p in outward}
        to_far, to_near, to_own = {}, {}, {}
        for t in range(2):
            total = add(
                moment_sums({p: leaving[p][t] for p in outward}),
                [sent[MOMENTS + i][t] for i in range(4)],
            )
            density = total[0]
            inverse = 1.0 / density
            u = [part * inverse for part in total[1:]]
            square = u[0] * u[0] + u[1] * u[1] + u[2] * u[2]
            for i, value in enumerate(u + [square]):
                flow_ref[side, i, t] = value
            keep = 1.0 - blend[t]
            scaled = (0.9 * keep) * density
            rest = scaled * (1.0 - 1.5 * square)
            along = dots(u)
            for p in range(19):
                value = float(WEIGHTS[p]) * rest
                if p:
                    cu = along[(p - 1) // 2]
                    flux = scaled * cu
                    value = value + flux * cu * float(4.5 * WEIGHTS[p])
                    value = value + flux * float((3.0 if p % 2 else -3.0) * WEIGHTS[p])
                if p in outward:
                    to_far.setdefault(p, []).append(value + 0.1 * keep * leaving[p][t])
                elif p in inward:
                    to_own.setdefault(p, []).append(value + blend[t] * leaving[OPP[p]][t])
                else:
                    to_near.setdefault(p, []).append(value)
        to_far = {p: moved(p, tuple(pair), 0.0) for p, pair in to_far.items()}
        to_near = {p: moved(p, tuple(pair), 0.0) for p, pair in to_near.items()}
        to_own = {p: moved(p, tuple(pair), 0.0) for p, pair in to_own.items()}
        back = {p: moved(p, c1(p, x)) for p in outward}
        for t in range(2):
            total = add(
                moment_sums({p: to_far[p][t] for p in to_far}),
                [sent[SUM_FAR + i][t] for i in range(4)],
            )
            save_field(x + 2 * out, t, total, sent[WEIGHT_FAR][t], end)
            near = dict(to_near)
            near.update(back)
            total = add(
                moment_sums({p: near[p][t] for p in near}),
                [sent[SUM_NEAR + i][t] for i in range(4)],
            )
            save_field(x + out, t, total, sent[WEIGHT_NEAR][t], end)
            own = moment_sums({p: to_own[p][t] for p in to_own})
            ready = [sent[SUM_OWN + i][t] for i in range(3)]
            own = add(own, [ready[0], -out * ready[0], ready[1], ready[2]])
            ghost = moment_sums({p: GHOST[p] for p in inward})
            for i in range(4):
                sum_ref[side, i, t] = jnp.where(end, ghost[i], own[i])

    for x in range(4):
        pops, given = list(range(19)), None
        if x == 0:
            pops, given = FLAT + DOWN, 0
        if x == 3:
            pops, given = FLAT + UP, 1
        came = {p: moved(p, c1(p, x - CX[p])) for p in pops}
        weight = c0(WEIGHT, x)
        for t in range(2):
            total = moment_sums({p: came[p][t] for p in came})
            if given is not None:
                total = add(total, [sum_ref[given, i, t] for i in range(4)])
            save_field(x, t, total, weight[t])

    def cotangent(p, x):
        pair = []
        for t in range(2):
            value = -field_ref[3, x + CX[p] + 2, t]
            for k in range(3):
                if VEL[p][k] == 1:
                    value = value + field_ref[k, x + CX[p] + 2, t]
                if VEL[p][k] == -1:
                    value = value - field_ref[k, x + CX[p] + 2, t]
            pair.append(value)
        return shift_pair(tuple(pair), -VEL[p][1], -VEL[p][2], 0.0)

    for x in range(4):
        h = [cotangent(p, x) for p in range(19)]
        blend = c0(BLEND, x)
        for t in range(2):
            wanted = [p for p in range(19) if t == 0 or VEL[p][1] != 0]
            out, part = adjoint_collide(
                [s1(p, x, t) for p in range(19)],
                blend[t],
                [h[p][t] for p in range(19)],
                wanted,
                t == 0,
            )
            for p, value in out.items():
                a1_ref[p, x + 1, t] = value
            if part is not None:
                sensitivity_ref[x] = part
    for side, (read, end, x, out, inward, outward) in enumerate(ends):
        h = [cotangent(p, x + out) for p in range(19)]
        blend = get_message(read, NEAR_BLEND)
        for t in range(2):
            u = [flow_ref[side, i, t] for i in range(3)]
            wanted = [p for p in outward if t == 0 or VEL[p][1] != 0]
            got = adjoint_values(
                u, flow_ref[side, 3, t], blend[t], [h[p][t] for p in range(19)], wanted
            )[0]
            for p, value in got.items():
                a1_ref[p, x + out + 1, t] = jnp.where(end, 0.0, value)

    sent = []
    for x in range(4):
        h = []
        for p in range(19):
            at = x + CX[p] + 1
            tile = a1_ref[p, at, 0]
            if VEL[p][1]:
                tile = shift_y((tile, a1_ref[p, at, 1]), -VEL[p][1])[0]
            h.append(shift_z(tile, -VEL[p][2], 0.0))
        out, part = adjoint_collide(
            [f_ref[p, x] for p in range(19)], own_ref[BLEND, x], h, list(range(19)), True
        )
        for p in range(19):
            adjoint_ref[p, x] = out[p]
        sent.append(
            pltpu.make_async_copy(adjoint_ref.at[:, x], adjoint_hbm.at[:, x], sems.at[x])
        )
        sent[x].start()
        design = (solid_ref[x] == 0) & (surface_ref[x] == 1)
        sensitivity_ref[x] = jnp.where(design, sensitivity_ref[x] + part, 0.0)
    sent.append(pltpu.make_async_copy(sensitivity_ref, sensitivity_hbm, sems.at[4]))
    sent[4].start()
    for copy in sent:
        copy.wait()


def call(kernel, inputs, shapes, scratch=(), space=pltpu.VMEM, result=pltpu.VMEM):
    return pl.pallas_call(
        kernel,
        out_shape=[jax.ShapeDtypeStruct(shape, jnp.float32) for shape in shapes],
        in_specs=[pl.BlockSpec(memory_space=space)] * len(inputs),
        out_specs=[pl.BlockSpec(memory_space=result)] * len(shapes),
        scratch_shapes=scratch,
        compiler_params=pltpu.CompilerParams(vmem_limit_bytes=24 * 1024 * 1024),
    )(*inputs)


def shards(checkpoint, porosity, deposit_weight, solid_mask, surface_mask):
    stream, span = lax.axis_size("stream"), lax.axis_size("span")
    tile = (8, 128)
    block, half = (21, 4) + tile, (SPAN_TILES,) + tile
    inputs = tuple(
        pltpu.with_memory_space_constraint(value, pltpu.HBM)
        for value in (checkpoint, porosity, deposit_weight, solid_mask, surface_mask)
    )
    own, mine = call(
        start_kernel,
        inputs,
        [block, half],
        [pltpu.VMEM(value.shape, value.dtype) for value in inputs]
        + [pltpu.SemaphoreType.DMA((8,))],
        pltpu.HBM,
    )
    cores = [[i, i + 1] for i in range(0, span, 2)]
    chips = [(i, (i + 1) % span) for i in range(1, span, 2)]
    came = lax.ppermute(mine, "span", chips + [(b, a) for a, b in chips])
    both = lax.all_gather(own, "span", axis_index_groups=cores)
    rows = (19, 2, 2) + tile
    message = (TILES,) + tile
    side, state, following, first, second = call(
        inner_kernel,
        (own, both, came),
        [block, rows, rows, message, message],
        [pltpu.VMEM((2,) + message, jnp.float32)],
    )

    swaps, groups = [], []
    for j in range(span):
        turn = turn_of(j)
        swaps += [(i * span + j, (i + 1) * span + j) for i in range(1 - turn, stream - 1, 2)]
        groups += [[i * span + j, (i + 1) * span + j] for i in range(turn, stream - 1, 2)]
        if turn and j % 2:
            groups += [[i * span + j - 1, i * span + j] for i in (0, stream - 1)]
    axes = ("stream", "span")
    one = lax.ppermute(first, axes, swaps + [(b, a) for a, b in swaps])
    two = lax.all_gather(second, axes, axis_index_groups=groups)
    scratch = [
        (19, 4), (4,), (19, 2, 2), (19, 2, 2), (2, 4, 2), (2, 4, 2), (19, 6, 2), (4, 8, 2),
        (2, TILES),
    ]
    adjoint, sensitivity = call(
        last_kernel,
        (checkpoint, solid_mask, surface_mask, own, side, state, following, one, two),
        [(19, 4) + tile, (4,) + tile],
        [pltpu.VMEM(shape + tile, jnp.float32) for shape in scratch]
        + [pltpu.SemaphoreType.DMA((5,))],
        result=pl.ANY,
    )
    return (adjoint, sensitivity)


def solution(mesh):
    placed = (
        P(None, "stream", "span", None),
        P("stream", "span", None),
        P("stream", "span", None),
        P("stream", "span", None),
        P("stream", "span", None),
    )
    return jax.shard_map(
        shards,
        mesh=mesh,
        in_specs=placed,
        out_specs=(P(None, "stream", "span", None), P("stream", "span", None)),
        check_vma=False,
    )
```

```python
import functools

import jax
import jax.numpy as jnp
import numpy as np
from jax import lax
from jax.experimental import pallas as pl
from jax.experimental.pallas import tpu as pltpu
from jax.sharding import PartitionSpec as P

VELOCITY = np.array(
    [
        [0, 0, 0],
        [1, 0, 0],
        [-1, 0, 0],
        [0, 1, 0],
        [0, -1, 0],
        [0, 0, 1],
        [0, 0, -1],
        [1, 1, 0],
        [-1, -1, 0],
        [1, -1, 0],
        [-1, 1, 0],
        [1, 0, 1],
        [-1, 0, -1],
        [1, 0, -1],
        [-1, 0, 1],
        [0, 1, 1],
        [0, -1, -1],
        [0, 1, -1],
        [0, -1, 1],
    ]
)
WEIGHTS = np.array([1.0 / 3.0] + [1.0 / 18.0] * 6 + [1.0 / 36.0] * 12)
GHOST_DENSITY = 18.0
INFLOW_SPEED = 0.08
GHOST_STATE = (
    WEIGHTS
    * GHOST_DENSITY
    * (
        1.0
        + 3.0 * VELOCITY[:, 0] * INFLOW_SPEED
        + 4.5 * (VELOCITY[:, 0] * INFLOW_SPEED) ** 2
        - 1.5 * INFLOW_SPEED**2
    )
)
GHOST = [float(value) for value in GHOST_STATE]
VEL = [tuple(int(part) for part in row) for row in VELOCITY]
CX = [row[0] for row in VEL]
UP = [p for p in range(19) if CX[p] == 1]
DOWN = [p for p in range(19) if CX[p] == -1]
FLAT = [p for p in range(19) if CX[p] == 0]
LEFT = [p for p in range(19) if VEL[p][1] == -1]
RIGHT = [p for p in range(19) if VEL[p][1] == 1]
ALONG = [p for p in range(19) if VEL[p][1] == 0]
OPP = [0] + [p + 1 if p % 2 else p - 1 for p in range(1, 19)]
BLEND, WEIGHT = 19, 20
SPAN_WIDE, SPAN_FREE = 15, 5
SPAN_TILES = 2 * SPAN_WIDE + 1
STATE, MOMENTS, NEAR_BLEND, WIDE = 0, 5, 9, 10
SUM_FAR, SUM_NEAR, SUM_OWN, WEIGHT_FAR, WEIGHT_NEAR, LAYERS = 10, 14, 18, 21, 22, 23
INSET = WIDE // 2
TILES = LAYERS + WIDE + (LAYERS - WIDE - INSET + 1) // 2


def sublane(tile):
    return lax.broadcasted_iota(jnp.int32, tile.shape, len(tile.shape) - 2)


def lane(tile):
    return lax.broadcasted_iota(jnp.int32, tile.shape, len(tile.shape) - 1)


def spin(tile, rows):
    return pltpu.roll(tile, rows % 8, 0) if rows % 8 else tile


def shift_z(tile, step, fill):
    if step == 0:
        return tile
    rolled = pltpu.roll(tile, step % 128, 1)
    return jnp.where(lane(tile) == (0 if step == 1 else 127), fill, rolled)


def shift_y(pair, step):
    if step == 0:
        return pair
    own, side = (pltpu.roll(tile, step % 8, 0) for tile in pair)
    edge = sublane(own) == (0 if step == 1 else 7)
    return (jnp.where(edge, side, own), jnp.where(edge, own, side))


def shift_pair(pair, stepy, stepz, fill):
    return tuple(shift_z(tile, stepz, fill) for tile in shift_y(pair, stepy))


def pairs_of(f):
    sums = [f[2 * i + 1] + f[2 * i + 2] for i in range(9)]
    diffs = [f[2 * i + 1] - f[2 * i + 2] for i in range(9)]
    return sums, diffs


def along_axes(v):
    return (
        v[0] + v[3] + v[4] + v[5] + v[6],
        v[1] + v[3] - v[4] + v[7] + v[8],
        v[2] + v[5] - v[6] + v[7] - v[8],
    )


def dots(u):
    x, y, z = u
    return [x, y, z, x + y, x - y, x + z, x - z, y + z, y - z]


def flow(f0, sums, diffs):
    density = f0 + sum(sums[1:], sums[0])
    inverse = 1.0 / density
    u = [m * inverse for m in along_axes(diffs)]
    square = u[0] * u[0] + u[1] * u[1] + u[2] * u[2]
    return density, u, square


def collide(f, b):
    sums, diffs = pairs_of(f)
    density, u, square = flow(f[0], sums, diffs)
    keep = 1.0 - b
    j = 0.1 * keep
    alpha, beta = 0.5 * (j + b), 0.5 * (j - b)
    scaled = (0.9 * keep) * density
    rest = scaled * (1.0 - 1.5 * square)
    flux = dots([scaled * part for part in u])
    out = [(j + b) * f[0] + (1.0 / 3.0) * rest]
    rest_axis, rest_diag = rest * (1.0 / 18.0), rest * (1.0 / 36.0)
    for i, along in enumerate(dots(u)):
        w = 1.0 / 18.0 if i < 3 else 1.0 / 36.0
        even = alpha * sums[i] + (rest_axis if i < 3 else rest_diag) + flux[i] * along * (4.5 * w)
        odd = beta * diffs[i] + flux[i] * (3.0 * w)
        out += [even + odd, even - odd]
    return out


def adjoint_values(u, square, b, h, wanted):
    s, d = pairs_of(h)
    w = [1.0 / 18.0] * 3 + [1.0 / 36.0] * 6
    t = [s[i] * w[i] for i in range(9)]
    h0 = h[0] * (1.0 / 3.0) + sum(t[1:], t[0])
    h1 = along_axes([d[i] * w[i] for i in range(9)])
    xx = t[0] + t[3] + t[4] + t[5] + t[6]
    yy = t[1] + t[3] + t[4] + t[7] + t[8]
    zz = t[2] + t[5] + t[6] + t[7] + t[8]
    xy, xz, yz = t[3] - t[4], t[5] - t[6], t[7] - t[8]
    v = (
        xx * u[0] + xy * u[1] + xz * u[2],
        xy * u[0] + yy * u[1] + yz * u[2],
        xz * u[0] + yz * u[1] + zz * u[2],
    )
    quad = u[0] * v[0] + u[1] * v[1] + u[2] * v[2]
    keep = 1.0 - b
    j, k = 0.1 * keep, 0.9 * keep
    alpha, beta = 0.5 * (j + b), 0.5 * (j - b)
    base = k * (h0 * (1.0 + 1.5 * square) - 4.5 * quad)
    push = dots([k * (3.0 * h1[i] + 9.0 * v[i] - 3.0 * u[i] * h0) for i in range(3)])
    out = {}
    if 0 in wanted:
        out[0] = (j + b) * h[0] + base
    for i in range(9):
        first, second = 2 * i + 1, 2 * i + 2
        if first in wanted or second in wanted:
            even = alpha * s[i] + base
            odd = beta * d[i] + push[i]
            if first in wanted:
                out[first] = even + odd
            if second in wanted:
                out[second] = even - odd
    return out, s, d, h0, h1, quad


def adjoint_collide(f, b, h, wanted, blend_part):
    fsums, fdiffs = pairs_of(f)
    density, u, square = flow(f[0], fsums, fdiffs)
    out, s, d, h0, h1, quad = adjoint_values(u, square, b, h, wanted)
    part = None
    if blend_part:
        equil = h0 * (1.0 - 1.5 * square) + 4.5 * quad
        equil = equil + 3.0 * (u[0] * h1[0] + u[1] * h1[1] + u[2] * h1[2])
        evens = sum((s[i] * fsums[i] for i in range(1, 9)), s[0] * fsums[0])
        odds = sum((d[i] * fdiffs[i] for i in range(1, 9)), d[0] * fdiffs[0])
        part = 0.9 * h[0] * f[0] + 0.45 * evens - 0.55 * odds - 0.9 * density * equil
    return out, part


def moment_sums(values):
    density = functools.reduce(lambda a, b: a + b, values.values())
    momentum = []
    for k in range(3):
        total = None
        for p, value in values.items():
            if VEL[p][k] == 1:
                total = value if total is None else total + value
        for p, value in values.items():
            if VEL[p][k] == -1:
                total = -value if total is None else total - value
        momentum.append(total)
    return [density] + momentum


def add(*totals):
    return [functools.reduce(lambda a, b: a + b, parts) for parts in zip(*totals)]


def put_message(ref, layers):
    for i, pair in enumerate(layers):
        ref[i] = pair[0]
    at = sublane(layers[0][1])
    for i in range(WIDE):
        tile = layers[i][1]
        if i // 2 < INSET:
            inset = pltpu.roll(layers[WIDE + i // 2][1], 5 if i % 2 else 3, 0)
            tile = jnp.where((at == 3) | (at == 4), inset, tile)
        ref[LAYERS + i] = tile
    for i in range(WIDE + INSET, LAYERS, 2):
        tile = layers[i][1]
        if i + 1 < LAYERS:
            tile = jnp.where((at < 2) | (at > 5), tile, pltpu.roll(layers[i + 1][1], 4, 0))
        ref[LAYERS + WIDE + (i - WIDE - INSET) // 2] = tile


def get_message(read, i):
    if i < WIDE:
        return (read(i), read(LAYERS + i))
    if i < WIDE + INSET:
        first, second = (read(LAYERS + 2 * (i - WIDE) + k) for k in range(2))
        first, second = pltpu.roll(first, 5, 0), pltpu.roll(second, 3, 0)
        return (read(i), jnp.where(sublane(first) < 4, first, second))
    tile = read(LAYERS + WIDE + (i - WIDE - INSET) // 2)
    return (read(i), pltpu.roll(tile, 4, 0) if (i - WIDE - INSET) % 2 else tile)


def turn_of(column):
    return min(column // 2, 1) if isinstance(column, int) else jnp.minimum(column // 2, 1)


def wide_layers(core):
    towards = [jnp.where(core == 0, a, b) for a, b in zip(LEFT, RIGHT)]
    return towards + ALONG + [BLEND]


def narrow_layers(core):
    return [jnp.where(core == 0, b, a) for a, b in zip(LEFT, RIGHT)] + [WEIGHT]


def start_kernel(
    f_hbm, porosity_hbm, weight_hbm, solid_hbm, surface_hbm, own_ref, half_ref,
    f_ref, porosity_ref, weight_ref, solid_ref, surface_ref, sems,
):
    small = [
        pltpu.make_async_copy(source, target, sems.at[i])
        for i, (source, target) in enumerate(
            (
                (solid_hbm, solid_ref),
                (surface_hbm, surface_ref),
                (porosity_hbm, porosity_ref),
                (weight_hbm, weight_ref),
            )
        )
    ]
    rows = [
        pltpu.make_async_copy(f_hbm.at[:, x], f_ref.at[:, x], sems.at[4 + x]) for x in range(4)
    ]
    for copy in rows + small:
        copy.start()
    core = lax.rem(lax.axis_index("span"), 2)
    at = lax.broadcasted_iota(jnp.int32, (8, 128), 0)
    low = (at < 4) == (core == 0)
    for copy in small:
        copy.wait()
    for x in range(4):
        porosity = porosity_ref[x]
        blend = jnp.where(
            solid_ref[x] == 1, 1.0, jnp.where(surface_ref[x] == 1, porosity, 0.0)
        )
        rows[x].wait()
        out = collide([f_ref[p, x] for p in range(19)], blend)
        for p in range(19):
            own_ref[p, x] = out[p]
        own_ref[BLEND, x] = blend
        own_ref[WEIGHT, x] = weight_ref[x]
        if x % 2:
            for i, layer in enumerate(wide_layers(core)):
                first, second = own_ref[layer, x - 1], own_ref[layer, x]
                half_ref[2 * i + x // 2] = jnp.where(low, first, pltpu.roll(second, 4, 0))
    for i, layer in enumerate(narrow_layers(core)):
        tile = own_ref[layer, 0]
        for x in range(1, 4):
            here = lax.rem(at + 8 - 2 * x + 2 * core, 8) < 2
            tile = jnp.where(here, pltpu.roll(own_ref[layer, x], 2 * x, 0), tile)
        if i == 5:
            half_ref[2 * SPAN_WIDE] = tile
            continue
        for k in range(4):
            slot = 2 * SPAN_FREE + 4 * i + k
            piece = jnp.where(core == 0, spin(tile, 3 - k), spin(tile, -k))
            free = lax.rem(at, 4) == 3 * (1 - core)
            half_ref[slot] = jnp.where(free, piece, half_ref[slot])


def inner_kernel(
    own_ref, both_ref, half_ref, side_ref, state_ref, next_ref, first_ref, second_ref, message_ref
):
    core = lax.rem(lax.axis_index("span"), 2)
    odd = lax.rem(lax.axis_index("stream"), 2)
    at = lax.broadcasted_iota(jnp.int32, (8, 128), 0)
    low = (at < 4) == (core == 0)
    for i, layer in enumerate(wide_layers(1 - core)):
        for x in range(4):
            tile = half_ref[2 * i + x // 2]
            tile = pltpu.roll(tile, 4, 0) if x % 2 else tile
            side_ref[layer, x] = jnp.where(low, both_ref[1 - core, layer, x], tile)
    for i, layer in enumerate(narrow_layers(1 - core)):
        rows = half_ref[2 * SPAN_WIDE]
        for k in range(4 if i < 5 else 0):
            piece = half_ref[2 * SPAN_FREE + 4 * i + k]
            piece = jnp.where(core == 1, spin(piece, k - 3), spin(piece, k))
            rows = jnp.where(lax.rem(at, 4) == k, piece, rows) if k else piece
        for x in range(4):
            side_ref[layer, x] = jnp.where(low, both_ref[1 - core, layer, x], spin(rows, -2 * x))

    def c0(p, x):
        return (own_ref[p, x], side_ref[p, x])

    def moved(p, pair):
        return shift_pair(pair, VEL[p][1], VEL[p][2], GHOST[p])

    for x in (1, 2):
        f = [moved(p, c0(p, x - CX[p])) for p in range(19)]
        blend = c0(BLEND, x)
        for t in range(2):
            tiles = [f[p][t] for p in range(19)]
            out = collide(tiles, blend[t])
            for p in range(19):
                state_ref[p, x - 1, t] = tiles[p]
                next_ref[p, x - 1, t] = out[p]

    def c1(p, x):
        return (next_ref[p, x - 1, 0], next_ref[p, x - 1, 1])

    for side, near, far, inward, outward in ((0, 3, 2, UP, DOWN), (1, 0, 1, DOWN, UP)):
        step = far - near
        enter = [moved(p, c0(p, near)) for p in inward]
        known = {p: moved(p, c0(p, near if p in FLAT else far)) for p in inward + FLAT}
        blend = c0(BLEND, near)
        j = [0.1 * (1.0 - part) for part in blend]
        layers = [None] * LAYERS
        layers[STATE : STATE + 5] = enter
        halves = [moment_sums({p: known[p][t] for p in known}) for t in range(2)]
        layers[MOMENTS : MOMENTS + 4] = list(zip(*halves))
        layers[NEAR_BLEND] = blend
        came = {p: moved(p, c1(p, far + step)) for p in inward}
        came.update({p: moved(p, c1(p, far)) for p in FLAT})
        for p in outward:
            came[p] = moved(p, tuple(blend[t] * known[OPP[p]][t] for t in range(2)))
        halves = [moment_sums({p: came[p][t] for p in came}) for t in range(2)]
        layers[SUM_FAR : SUM_FAR + 4] = list(zip(*halves))
        came = {p: moved(p, c1(p, far)) for p in inward}
        for p in FLAT:
            came[p] = moved(
                p,
                tuple(j[t] * known[p][t] + blend[t] * known[OPP[p]][t] for t in range(2)),
            )
        halves = [moment_sums({p: came[p][t] for p in came}) for t in range(2)]
        layers[SUM_NEAR : SUM_NEAR + 4] = list(zip(*halves))
        came = {p: moved(p, tuple(j[t] * known[p][t] for t in range(2))) for p in inward}
        halves = [moment_sums({p: came[p][t] for p in came}) for t in range(2)]
        halves = [[half[0], half[2], half[3]] for half in halves]
        layers[SUM_OWN : SUM_OWN + 3] = list(zip(*halves))
        layers[WEIGHT_FAR] = c0(WEIGHT, far)
        layers[WEIGHT_NEAR] = c0(WEIGHT, near)
        put_message(message_ref.at[side], layers)
    towards = lax.rem(1 - odd + turn_of(lax.axis_index("span")), 2)
    for i in range(TILES):
        first_ref[i] = message_ref[towards, i]
        second_ref[i] = message_ref[1 - towards, i]


def last_kernel(
    f_ref, solid_ref, surface_ref, own_ref, side_ref, state_ref, next_ref, one_ref, two_ref,
    adjoint_hbm, sensitivity_hbm, adjoint_ref, sensitivity_ref,
    s1_ref, c1_ref, sum_ref, flow_ref, a1_ref, field_ref, came_ref, sems,
):
    place = lax.axis_index("stream")
    at_start = place == 0
    at_end = place == lax.axis_size("stream") - 1
    origin = lax.rem(1 - lax.rem(place, 2) + turn_of(lax.axis_index("span")), 2)

    for i in range(TILES):
        came_ref[1 - origin, i] = one_ref[i]
        came_ref[origin, i] = two_ref[origin, i]

    def low(i):
        return came_ref[0, i]

    def high(i):
        return came_ref[1, i]

    ends = (
        (low, at_start, 0, -1, UP, DOWN),
        (high, at_end, 3, 1, DOWN, UP),
    )

    def moved(p, pair, fill=None):
        return shift_pair(pair, VEL[p][1], VEL[p][2], GHOST[p] if fill is None else fill)

    def c0(p, x):
        return (own_ref[p, x], side_ref[p, x])

    for read, end, x, out, inward, outward in ends:
        f = {p: moved(p, c0(p, x if p in FLAT else x - out)) for p in FLAT + outward}
        for i, p in enumerate(inward):
            f[p] = tuple(
                jnp.where(end, GHOST[p], part) for part in get_message(read, STATE + i)
            )
        blend = c0(BLEND, x)
        for t in range(2):
            tiles = [f[p][t] for p in range(19)]
            after = collide(tiles, blend[t])
            for p in range(19):
                s1_ref[p, x // 3, t] = tiles[p]
                c1_ref[p, x // 3, t] = after[p]

    def s1(p, x, t):
        return state_ref[p, x - 1, t] if x in (1, 2) else s1_ref[p, x // 3, t]

    def c1(p, x):
        ref, at = (next_ref, x - 1) if x in (1, 2) else (c1_ref, x // 3)
        return (ref[p, at, 0], ref[p, at, 1])

    def save_field(x, t, total, weight, end=None):
        inverse = 1.0 / total[0]
        u = [total[i] * inverse for i in range(1, 4)]
        kinetic = 0.5 * (u[0] * u[0] + u[1] * u[1] + u[2] * u[2])
        for i, value in enumerate(u + [kinetic]):
            value = weight * value
            field_ref[i, x + 2, t] = value if end is None else jnp.where(end, 0.0, value)

    for side, (read, end, x, out, inward, outward) in enumerate(ends):
        sent = [get_message(read, i) for i in range(LAYERS)]
        blend = sent[NEAR_BLEND]
        leaving = {p: moved(p, c0(p, x)) for p in outward}
        to_far, to_near, to_own = {}, {}, {}
        for t in range(2):
            total = add(
                moment_sums({p: leaving[p][t] for p in outward}),
                [sent[MOMENTS + i][t] for i in range(4)],
            )
            density = total[0]
            inverse = 1.0 / density
            u = [part * inverse for part in total[1:]]
            square = u[0] * u[0] + u[1] * u[1] + u[2] * u[2]
            for i, value in enumerate(u + [square]):
                flow_ref[side, i, t] = value
            keep = 1.0 - blend[t]
            scaled = (0.9 * keep) * density
            rest = scaled * (1.0 - 1.5 * square)
            along = dots(u)
            for p in range(19):
                value = float(WEIGHTS[p]) * rest
                if p:
                    cu = along[(p - 1) // 2]
                    flux = scaled * cu
                    value = value + flux * cu * float(4.5 * WEIGHTS[p])
                    value = value + flux * float((3.0 if p % 2 else -3.0) * WEIGHTS[p])
                if p in outward:
                    to_far.setdefault(p, []).append(value + 0.1 * keep * leaving[p][t])
                elif p in inward:
                    to_own.setdefault(p, []).append(value + blend[t] * leaving[OPP[p]][t])
                else:
                    to_near.setdefault(p, []).append(value)
        to_far = {p: moved(p, tuple(pair), 0.0) for p, pair in to_far.items()}
        to_near = {p: moved(p, tuple(pair), 0.0) for p, pair in to_near.items()}
        to_own = {p: moved(p, tuple(pair), 0.0) for p, pair in to_own.items()}
        back = {p: moved(p, c1(p, x)) for p in outward}
        for t in range(2):
            total = add(
                moment_sums({p: to_far[p][t] for p in to_far}),
                [sent[SUM_FAR + i][t] for i in range(4)],
            )
            save_field(x + 2 * out, t, total, sent[WEIGHT_FAR][t], end)
            near = dict(to_near)
            near.update(back)
            total = add(
                moment_sums({p: near[p][t] for p in near}),
                [sent[SUM_NEAR + i][t] for i in range(4)],
            )
            save_field(x + out, t, total, sent[WEIGHT_NEAR][t], end)
            own = moment_sums({p: to_own[p][t] for p in to_own})
            ready = [sent[SUM_OWN + i][t] for i in range(3)]
            own = add(own, [ready[0], -out * ready[0], ready[1], ready[2]])
            ghost = moment_sums({p: GHOST[p] for p in inward})
            for i in range(4):
                sum_ref[side, i, t] = jnp.where(end, ghost[i], own[i])

    for x in range(4):
        pops, given = list(range(19)), None
        if x == 0:
            pops, given = FLAT + DOWN, 0
        if x == 3:
            pops, given = FLAT + UP, 1
        came = {p: moved(p, c1(p, x - CX[p])) for p in pops}
        weight = c0(WEIGHT, x)
        for t in range(2):
            total = moment_sums({p: came[p][t] for p in came})
            if given is not None:
                total = add(total, [sum_ref[given, i, t] for i in range(4)])
            save_field(x, t, total, weight[t])

    def cotangent(p, x):
        pair = []
        for t in range(2):
            value = -field_ref[3, x + CX[p] + 2, t]
            for k in range(3):
                if VEL[p][k] == 1:
                    value = value + field_ref[k, x + CX[p] + 2, t]
                if VEL[p][k] == -1:
                    value = value - field_ref[k, x + CX[p] + 2, t]
            pair.append(value)
        return shift_pair(tuple(pair), -VEL[p][1], -VEL[p][2], 0.0)

    for x in range(4):
        h = [cotangent(p, x) for p in range(19)]
        blend = c0(BLEND, x)
        for t in range(2):
            wanted = [p for p in range(19) if t == 0 or VEL[p][1] != 0]
            out, part = adjoint_collide(
                [s1(p, x, t) for p in range(19)],
                blend[t],
                [h[p][t] for p in range(19)],
                wanted,
                t == 0,
            )
            for p, value in out.items():
                a1_ref[p, x + 1, t] = value
            if part is not None:
                sensitivity_ref[x] = part
    for side, (read, end, x, out, inward, outward) in enumerate(ends):
        h = [cotangent(p, x + out) for p in range(19)]
        blend = get_message(read, NEAR_BLEND)
        for t in range(2):
            u = [flow_ref[side, i, t] for i in range(3)]
            wanted = [p for p in outward if t == 0 or VEL[p][1] != 0]
            got = adjoint_values(
                u, flow_ref[side, 3, t], blend[t], [h[p][t] for p in range(19)], wanted
            )[0]
            for p, value in got.items():
                a1_ref[p, x + out + 1, t] = jnp.where(end, 0.0, value)

    sent = []
    for x in range(4):
        h = []
        for p in range(19):
            at = x + CX[p] + 1
            tile = a1_ref[p, at, 0]
            if VEL[p][1]:
                tile = shift_y((tile, a1_ref[p, at, 1]), -VEL[p][1])[0]
            h.append(shift_z(tile, -VEL[p][2], 0.0))
        out, part = adjoint_collide(
            [f_ref[p, x] for p in range(19)], own_ref[BLEND, x], h, list(range(19)), True
        )
        for p in range(19):
            adjoint_ref[p, x] = out[p]
        sent.append(
            pltpu.make_async_copy(adjoint_ref.at[:, x], adjoint_hbm.at[:, x], sems.at[x])
        )
        sent[x].start()
        design = (solid_ref[x] == 0) & (surface_ref[x] == 1)
        sensitivity_ref[x] = jnp.where(design, sensitivity_ref[x] + part, 0.0)
    sent.append(pltpu.make_async_copy(sensitivity_ref, sensitivity_hbm, sems.at[4]))
    sent[4].start()
    for copy in sent:
        copy.wait()


def call(kernel, inputs, shapes, scratch=(), space=pltpu.VMEM, result=pltpu.VMEM):
    return pl.pallas_call(
        kernel,
        out_shape=[jax.ShapeDtypeStruct(shape, jnp.float32) for shape in shapes],
        in_specs=[pl.BlockSpec(memory_space=space)] * len(inputs),
        out_specs=[pl.BlockSpec(memory_space=result)] * len(shapes),
        scratch_shapes=scratch,
        compiler_params=pltpu.CompilerParams(vmem_limit_bytes=24 * 1024 * 1024),
    )(*inputs)


def shards(checkpoint, porosity, deposit_weight, solid_mask, surface_mask):
    stream, span = lax.axis_size("stream"), lax.axis_size("span")
    tile = (8, 128)
    block, half = (21, 4) + tile, (SPAN_TILES,) + tile
    inputs = tuple(
        pltpu.with_memory_space_constraint(value, pltpu.HBM)
        for value in (checkpoint, porosity, deposit_weight, solid_mask, surface_mask)
    )
    own, mine = call(
        start_kernel,
        inputs,
        [block, half],
        [pltpu.VMEM(value.shape, value.dtype) for value in inputs]
        + [pltpu.SemaphoreType.DMA((8,))],
        pltpu.HBM,
    )
    cores = [[i, i + 1] for i in range(0, span, 2)]
    chips = [(i, (i + 1) % span) for i in range(1, span, 2)]
    came = lax.ppermute(mine, "span", chips + [(b, a) for a, b in chips])
    both = lax.all_gather(own, "span", axis_index_groups=cores)
    rows = (19, 2, 2) + tile
    message = (TILES,) + tile
    side, state, following, first, second = call(
        inner_kernel,
        (own, both, came),
        [block, rows, rows, message, message],
        [pltpu.VMEM((2,) + message, jnp.float32)],
    )

    swaps, groups = [], []
    for j in range(span):
        turn = turn_of(j)
        swaps += [(i * span + j, (i + 1) * span + j) for i in range(1 - turn, stream - 1, 2)]
        groups += [[i * span + j, (i + 1) * span + j] for i in range(turn, stream - 1, 2)]
        if turn and j % 2:
            groups += [[i * span + j - 1, i * span + j] for i in (0, stream - 1)]
    axes = ("stream", "span")
    one = lax.ppermute(first, axes, swaps + [(b, a) for a, b in swaps])
    two = lax.all_gather(second, axes, axis_index_groups=groups)
    scratch = [
        (19, 4), (4,), (19, 2, 2), (19, 2, 2), (2, 4, 2), (2, 4, 2), (19, 6, 2), (4, 8, 2),
        (2, TILES),
    ]
    adjoint, sensitivity = call(
        last_kernel,
        (checkpoint, solid_mask, surface_mask, own, side, state, following, one, two),
        [(19, 4) + tile, (4,) + tile],
        [pltpu.VMEM(shape + tile, jnp.float32) for shape in scratch]
        + [pltpu.SemaphoreType.DMA((5,))],
        result=pl.ANY,
    )
    return (adjoint, sensitivity)


def solution(mesh):
    placed = (
        P(None, "stream", "span", None),
        P("stream", "span", None),
        P("stream", "span", None),
        P("stream", "span", None),
        P("stream", "span", None),
    )
    return jax.shard_map(
        shards,
        mesh=mesh,
        in_specs=placed,
        out_specs=(P(None, "stream", "span", None), P("stream", "span", None)),
        check_vma=False,
    )
```
